32 devices in a mesh: dp: 2 (over core), ctx: 4 (over z), head: 4 (over y, x).
Axes of the slice: x: 2, y: 2, z: 4, core: 2. Of those that a mesh axis runs over, the one named last changes fastest.
Arguments:
- x_raw: bfloat16 [2, 1024, 8192], P('dp', 'ctx', 'head'), may hold values from -6 to 6
- bc_raw: bfloat16 [2, 1024, 2, 1024], P('dp', 'ctx', None, 'head'), may hold values from -6 to 6
- z_gate: bfloat16 [2, 1024, 8192], P('dp', 'ctx', 'head'), may hold values from -20 to 20
- dt_raw: bfloat16 [2, 128, 1024], P('dp', 'head', 'ctx'), may hold values from -4 to 4
- resets: int32 [2, 1024], P('dp', 'ctx'), may hold values 0 or 1
- conv_x_weight: float32 [4, 8192], P(None, 'head'), may hold values from -3 to 3
- conv_x_bias: float32 [8192], P('head'), may hold values from -1.5 to 1.5
- conv_bc_weight: float32 [4, 2, 1024], P(None, None, 'head'), may hold values from -3 to 3
- conv_bc_bias: float32 [2, 1024], P(None, 'head'), may hold values from -1.5 to 1.5
- a_log: float32 [128], P('head'), may hold values from -9 to 1
- dt_bias: float32 [128], P('head'), may hold values from -13 to -3
- skip_weight: float32 [128], P('head'), may hold values from 0.5 to 2
- norm_gain: float32 [8192], P('head'), may hold values from 0.1 to 1.9
- grad_out: bfloat16 [2, 1024, 8192], P('dp', 'ctx', 'head'), may hold values from -6 to 6
Outputs:
- grad_x: bfloat16 [2, 1024, 8192], P('dp', 'ctx', 'head')
- grad_bc: bfloat16 [2, 1024, 2, 1024], P('dp', 'ctx', None, 'head')
- grad_z: bfloat16 [2, 1024, 8192], P('dp', 'ctx', 'head')
- grad_dt: float32 [2, 128, 1024], P('dp', 'head', 'ctx')
- grad_conv_x_weight: float32 [4, 8192], P(None, 'head')
- grad_conv_x_bias: float32 [8192], P('head')
- grad_conv_bc_weight: float32 [4, 2, 1024], P(None, None, 'head')
- grad_conv_bc_bias: float32 [2, 1024], P(None, 'head')
- grad_a_log: float32 [128], P('head')
- grad_dt_bias: float32 [128], P('head')
- grad_skip: float32 [128], P('head')
- grad_gain: float32 [8192], P('head')
The draws below stay inside these ranges and needn't reach their ends.
All inputs are finite; a program needn't handle non-finite values. No bound on the sum of `resets` on one device may be relied on, other than what follows from the above.
Results may differ from the reference program's by a relative error of at most 0.01595.
Values may be sent and summed in bfloat16 or wider, within the bound.
No kernel may reach another device: no remote copies, remote signals or barrier semaphores. Data moves between devices by JAX's collectives and lax.ppermute only.
A program may use at most 256 MiB of HBM per device.

```python
import functools
import jax
import jax.numpy as jnp
from jax import lax

HEADS = 128
HEAD_DIM = 64
NSTATE = 128
GROUPS = 8
CONV = 4
STRETCH = 128
INNER = 8192
BATCH = 2
LENGTH = 1024


def draw_a_log(key, part):
    values = jax.random.uniform(key, (HEADS,), jnp.float32, -2.0, 1.0)
    return values


def draw_z_gate(key, part):
    key_a = jax.random.fold_in(key, 11)
    key_b = jax.random.fold_in(key, 12)
    channel = jnp.exp(jax.random.uniform(key_b, (INNER,), jnp.float32, -1.15, 1.15))
    values = jax.random.normal(key_a, (BATCH, LENGTH, INNER), jnp.float32) * channel
    return jnp.clip(values, -20.0, 20.0).astype(jnp.bfloat16)


def place_ends(values, stream_key, least, top_value):
    extent = values.shape
    spot = [jax.random.randint(jax.random.fold_in(stream_key, axis), (), 0, extent[axis]) for axis in range(len(extent))]
    values = values.at[tuple(spot)].set(least)
    longest = extent.index(max(extent))
    spot[longest] = (spot[longest] + 1) % extent[longest]
    return values.at[tuple(spot)].set(top_value)


def level_of(key, dims, split, smallest, high):
    factor_of, own = 1.0, jax.random.fold_in(key, 6)
    for dim, parts in split:
        heights = jnp.exp(jax.random.uniform(jax.random.fold_in(own, dim), (parts,), jnp.float32, smallest / len(split), high / len(split)))
        factor_of = factor_of * jnp.repeat(heights, dims[dim] // parts).reshape([-1 if axis == dim else 1 for axis in range(len(dims))])
    return factor_of


def noise(stream_key, shape, deviation, bound, cuts=(), dtype=jnp.bfloat16):
    drawn = deviation * jax.random.normal(stream_key, shape, jnp.float32)
    if cuts:
        drawn = drawn * level_of(stream_key, shape, cuts, -0.22, 0.18)
    return jnp.clip(drawn, -bound, bound).astype(dtype)


def setup_inputs(seed: int = 0) -> dict:
    splits = jax.random.split(jax.random.key(seed), 15)
    return {
        "x_raw": noise(splits[0], (BATCH, LENGTH, INNER), 1.0, 6.0, ((0, 2), (1, 4), (2, 4))),
        "bc_raw": noise(splits[1], (BATCH, LENGTH, 2, GROUPS * NSTATE), 1.0, 6.0, ((0, 2), (1, 4), (3, 4))),
        "z_gate": draw_z_gate(jax.random.fold_in(splits[14], 71), 0),
        "dt_raw": noise(splits[3], (BATCH, HEADS, LENGTH), 1.0, 4.0, ((0, 2), (1, 4), (2, 4))),
        "resets": place_ends((jax.random.randint(splits[4], (BATCH, LENGTH), 0, LENGTH) < 4).astype(jnp.int32), jax.random.fold_in(splits[4], 1), 0, 1),
        "conv_x_weight": noise(splits[5], (CONV, INNER), CONV ** -0.5, 3.0, ((1, 4),), jnp.float32),
        "conv_x_bias": noise(splits[6], (INNER,), 0.3, 1.5, ((0, 4),), jnp.float32),
        "conv_bc_weight": noise(splits[7], (CONV, 2, GROUPS * NSTATE), CONV ** -0.5, 3.0, ((2, 4),), jnp.float32),
        "conv_bc_bias": noise(splits[8], (2, GROUPS * NSTATE), 0.3, 1.5, ((1, 4),), jnp.float32),
        "a_log": draw_a_log(jax.random.fold_in(splits[14], 71), 0),
        "dt_bias": jnp.clip(-13.0 + 10.0 * jax.random.uniform(splits[10], (HEADS,), jnp.float32) ** level_of(splits[10], (HEADS,), ((0, 4),), -0.2, 0.2), -13.0, -3.0),
        "skip_weight": jnp.clip(0.5 + 1.5 * jax.random.uniform(splits[11], (HEADS,), jnp.float32) ** level_of(splits[11], (HEADS,), ((0, 4),), -0.2, 0.2), 0.5, 2.0),
        "norm_gain": jnp.clip(1.0 + 0.18 * jax.random.normal(splits[12], (INNER,), jnp.float32), 0.1, 1.9),
        "grad_out": noise(splits[13], (BATCH, LENGTH, INNER), 1.0, 6.0, ((0, 2), (1, 4), (2, 4))),
    }


norm_eps = 1e-05

def kept(value):
    return lax.optimization_barrier(value)

def causal_conv(extended, counts, weight, conv_bias):
    pad_rows = CONV - 1
    row_count = extended.shape[0] - pad_rows
    shape_tail = (1,) * (extended.ndim - 1)
    summed = conv_bias + weight[0] * extended[pad_rows:]
    for lag_step in range(1, CONV):
        lower = pad_rows - lag_step
        live_mask = (counts[pad_rows:] == counts[lower:lower + row_count]).astype(jnp.float32)
        summed = summed + weight[lag_step] * extended[lower:lower + row_count] * live_mask.reshape((row_count,) + shape_tail)
    return kept(jax.nn.silu(summed).astype(jnp.bfloat16))

def rows_to_blocks(array_rows):
    return array_rows.reshape((array_rows.shape[0] // STRETCH, STRETCH) + array_rows.shape[1:])

def steps_to_blocks(steps_dt):
    shape_now = steps_dt.shape
    reshaped = steps_dt.reshape(shape_now[0], shape_now[1], shape_now[2] // STRETCH, STRETCH)
    return jnp.transpose(reshaped, (2, 0, 1, 3))

def from_before(block_c, prior_state, running, resets_seen):
    from_start = jnp.where(resets_seen == 0.0, jnp.exp(running), 0.0)
    state_half = kept(prior_state.astype(jnp.bfloat16))
    carried = jnp.einsum('tgn,ghpn->tghp', block_c.astype(jnp.float32), state_half.astype(jnp.float32))
    return carried * jnp.transpose(from_start, (2, 0, 1))[..., None]

def keep_factor(running, resets_seen):
    return jnp.where(resets_seen[-1] == 0.0, jnp.exp(running[..., -1]), 0.0)

def block_end(block_x, block_b, block_dt, running, resets_seen):
    to_end = jnp.where(resets_seen == resets_seen[-1], jnp.exp(running[..., -1:] - running), 0.0)
    scaled = kept((block_x.astype(jnp.float32) * jnp.transpose(block_dt * to_end, (2, 0, 1))[..., None]).astype(jnp.bfloat16))
    return jnp.einsum('sghp,sgn->ghpn', scaled.astype(jnp.float32), block_b.astype(jnp.float32))

def block_terms(prior_state, block_piece, decay_rate):
    block_x, block_b, block_c, block_dt, block_flags = block_piece
    running = jnp.cumsum(-decay_rate[:, :, None] * block_dt, axis=-1)
    resets_seen = jnp.cumsum(block_flags)
    position = jnp.arange(block_flags.shape[0])
    same_doc = (resets_seen[:, None] == resets_seen[None, :]) & (position[:, None] >= position[None, :])
    spread = running[..., :, None] - running[..., None, :]
    segment = jnp.where(same_doc, jnp.exp(jnp.where(same_doc, spread, 0.0)), 0.0)
    scores = jnp.einsum('tgn,sgn->gts', block_c.astype(jnp.float32), block_b.astype(jnp.float32))
    weights = kept((scores[:, None] * segment * block_dt[:, :, None, :]).astype(jnp.bfloat16))
    within = jnp.einsum('ghts,sghp->tghp', weights.astype(jnp.float32), block_x.astype(jnp.float32))
    carried = from_before(block_c, prior_state, running, resets_seen)
    fresh_state = block_end(block_x, block_b, block_dt, running, resets_seen)
    next_state = keep_factor(running, resets_seen)[..., None, None] * prior_state + fresh_state
    return (next_state, within + carried)

def scan_blocks(inputs, b_rows, c_rows, steps_dt, decay_rate, reset_flags, state_in):
    row_count = inputs.shape[0]
    pieces = (rows_to_blocks(inputs), rows_to_blocks(b_rows), rows_to_blocks(c_rows), steps_to_blocks(steps_dt), rows_to_blocks(reset_flags))
    stepper = jax.checkpoint(functools.partial(block_terms, decay_rate=decay_rate))
    final_state, outputs = lax.scan(stepper, state_in, pieces)
    return (outputs.reshape((row_count,) + inputs.shape[1:]), final_state)

def gate_output(y_ssd, inputs, z_in, skip_weight):
    row_count = inputs.shape[0]
    skip_term = skip_weight.reshape(inputs.shape[1], inputs.shape[2])[None, :, :, None] * inputs.astype(jnp.float32)
    mixed = kept((y_ssd + skip_term).astype(jnp.bfloat16))
    return mixed.astype(jnp.float32).reshape(row_count, -1) * jax.nn.silu(z_in)

def sequence_out(x_in, bc_in, z_in, dt_in, conv_x_weight, conv_x_bias, conv_bc_weight, conv_bc_bias, a_log, dt_bias, skip_weight, norm_gain, reset_flags):
    pad_rows = CONV - 1
    row_count = x_in.shape[0]
    per_group = HEADS // GROUPS
    counts = jnp.cumsum(reset_flags)
    padded_counts = jnp.concatenate([jnp.zeros((pad_rows,), jnp.float32), counts])
    x_ext = jnp.concatenate([jnp.zeros((pad_rows, x_in.shape[1]), jnp.float32), x_in])
    bc_ext = jnp.concatenate([jnp.zeros((pad_rows,) + bc_in.shape[1:], jnp.float32), bc_in])
    inputs = causal_conv(x_ext, padded_counts, conv_x_weight, conv_x_bias).reshape(row_count, GROUPS, per_group, HEAD_DIM)
    bc_conv = causal_conv(bc_ext, padded_counts, conv_bc_weight, conv_bc_bias)
    b_rows = bc_conv[:, 0].reshape(row_count, GROUPS, NSTATE)
    c_rows = bc_conv[:, 1].reshape(row_count, GROUPS, NSTATE)
    steps_dt = jax.nn.softplus(dt_in + dt_bias[:, None]).reshape(GROUPS, per_group, row_count)
    decay_rate = jnp.exp(a_log).reshape(GROUPS, per_group)
    state_zero = jnp.zeros((GROUPS, per_group, HEAD_DIM, NSTATE), jnp.float32)
    y_ssd, final_state = scan_blocks(inputs, b_rows, c_rows, steps_dt, decay_rate, reset_flags, state_zero)
    gated = gate_output(y_ssd, inputs, z_in, skip_weight)
    inv_rms = lax.rsqrt(lax.optimization_barrier(jnp.mean(gated * gated, axis=-1, keepdims=True)) + norm_eps)
    return gated * inv_rms * norm_gain

def reference(x_raw, bc_raw, z_gate, dt_raw, resets, conv_x_weight, conv_x_bias, conv_bc_weight, conv_bc_bias, a_log, dt_bias, skip_weight, norm_gain, grad_out):
    act_grads = ([], [], [], [])
    params = (conv_x_weight, conv_x_bias, conv_bc_weight, conv_bc_bias, a_log, dt_bias, skip_weight, norm_gain)
    param_sums = jax.tree.map(jnp.zeros_like, params)
    for seq_index in range(BATCH):
        forward = functools.partial(sequence_out, reset_flags=resets[seq_index].astype(jnp.float32))
        primals = (x_raw[seq_index].astype(jnp.float32), bc_raw[seq_index].astype(jnp.float32), z_gate[seq_index].astype(jnp.float32), dt_raw[seq_index].astype(jnp.float32)) + params
        normed, pullback = jax.vjp(forward, *primals)
        gradients = pullback(grad_out[seq_index].astype(jnp.float32))
        for slot_index in range(4):
            act_grads[slot_index].append(gradients[slot_index])
        param_sums = jax.tree.map(jnp.add, param_sums, tuple(gradients[4:]))
    grad_scale = float(BATCH * LENGTH) ** (-0.5)
    return (jnp.stack(act_grads[0]).astype(jnp.bfloat16), jnp.stack(act_grads[1]).astype(jnp.bfloat16), jnp.stack(act_grads[2]).astype(jnp.bfloat16), jnp.stack(act_grads[3]), param_sums[0] * grad_scale, param_sums[1] * grad_scale, param_sums[2] * grad_scale, param_sums[3] * grad_scale, param_sums[4] * grad_scale, param_sums[5] * grad_scale, param_sums[6] * grad_scale, param_sums[7] * grad_scale)
```

```python
import functools

import jax
import jax.numpy as jnp
from jax import lax
from jax.experimental import pallas as pl
from jax.experimental.pallas import tpu as pltpu
from jax.sharding import PartitionSpec as P

HEAD_DIM = 64
NSTATE = 128
CONV = 4
STRETCH = 128
INNER = 8192
HALO = CONV - 1
PAD = 8
CHUNK = 256
PAIR = 2 * HEAD_DIM
NORM_EPS = 1e-05
LOWEST = -1e30
VMEM_LIMIT = 40 * 1024 * 1024

f32 = jnp.float32
bf16 = jnp.bfloat16


def dot(a, b, contract=((1,), (0,))):
    return lax.dot_general(a, b, (contract, ((), ())), preferred_element_type=f32)


def dot_full(a, b):
    return lax.dot_general(
        a, b, (((1,), (0,)), ((), ())), precision=lax.Precision.HIGHEST, preferred_element_type=f32
    )


def iota(shape, dim):
    return lax.broadcasted_iota(jnp.int32, shape, dim)


def split3(value):
    high = value.astype(bf16)
    rest = value - high.astype(f32)
    middle = rest.astype(bf16)
    low = (rest - middle.astype(f32)).astype(bf16)
    return jnp.concatenate([high, middle, low], axis=0)


def spread_heads(rows, width):
    heads = rows.shape[0]
    shape = (heads, heads * width)
    pick = (iota(shape, 1) // width == iota(shape, 0)).astype(f32).astype(bf16)
    return dot(split3(rows), jnp.concatenate([pick] * 3, axis=0), ((0,), (0,)))


def head_sums(value, first, heads):
    shape = (heads, value.shape[1])
    pick = ((iota(shape, 1) + first) // HEAD_DIM == iota(shape, 0)).astype(f32).astype(bf16)
    high = value.astype(bf16)
    low = (value - high.astype(f32)).astype(bf16)
    last = ((1,), (1,))
    return dot(pick, high, last) + dot(pick, low, last)


def as_columns(row):
    return jnp.transpose(jnp.broadcast_to(row, (STRETCH, STRETCH)))


def sigmoid(value):
    return 0.5 * jnp.tanh(0.5 * value) + 0.5


def upper_ones():
    shape = (STRETCH, STRETCH)
    return (iota(shape, 0) <= iota(shape, 1)).astype(f32)


def resets_seen(flags_row):
    flags = jnp.broadcast_to(flags_row.astype(f32), (PAD, STRETCH)).astype(bf16)
    return dot(flags, upper_ones().astype(bf16))[0:1]


def decay_mask(seen):
    shape = (STRETCH, STRETCH)
    same = (as_columns(seen) == jnp.broadcast_to(seen, shape)) & (iota(shape, 0) >= iota(shape, 1))
    return jnp.where(same, 0.0, LOWEST)


def lanes(position, size):
    return pl.ds(pl.multiple_of(position * size, size), size)


def fill_extended(extended, halo_ref, rows_ref):
    extended[0:PAD, :] = halo_ref[...]
    extended[PAD:, :] = rows_ref[...].astype(f32)


def tap(extended, first, lag, part):
    return extended[PAD + first - lag : PAD + first - lag + STRETCH, part]


def conv_taps(extended, live_ref, first, part):
    width = extended[0:PAD, part].shape[1]
    taps = [tap(extended, first, 0, part)]
    for lag in range(1, CONV):
        mask = live_ref[PAD + first : PAD + first + STRETCH, lag - 1 : lag]
        taps.append(tap(extended, first, lag, part) * jnp.broadcast_to(mask, (STRETCH, width)))
    return taps


def conv_sum(taps, weight_ref, bias_ref, part):
    total = bias_ref[0:1, part] + weight_ref[0:1, part] * taps[0]
    for lag in range(1, CONV):
        total = total + weight_ref[lag : lag + 1, part] * taps[lag]
    return total


def conv_and_state(
    x_ref, xh_ref, bc_ref, bch_ref, wx_ref, bx_ref, wb_ref, bb_ref, dt_ref, alog_ref, flags_ref,
    live_ref, xc_ref, xp_ref, bcc_ref, run_ref, keep_ref, sdev_ref, sloc_ref,
    x_ext, bc_ext, dt_wide, end_wide, state,
):
    rows, channels = x_ref.shape
    fill_extended(x_ext, xh_ref, x_ref)
    fill_extended(bc_ext, bch_ref, bc_ref)
    blocks = rows // STRETCH
    rate = jnp.exp(alog_ref[...])
    product = None
    for block in range(blocks):
        first = block * STRETCH
        here = slice(first, first + STRETCH)
        every = slice(None)
        total = conv_sum(conv_taps(bc_ext, live_ref, first, every), wb_ref, bb_ref, every)
        bc_now = (total * sigmoid(total)).astype(bf16)
        bcc_ref[here, :] = bc_now
        b_turned = jnp.transpose(bc_now[:, 0:NSTATE].astype(f32)).astype(bf16)
        seen = resets_seen(flags_ref[:, here])
        dt = dt_ref[:, here]
        running = dot_full(-rate * dt, upper_ones())
        run_ref[:, here] = running
        final = running[:, STRETCH - 1 : STRETCH]
        seen_final = seen[:, STRETCH - 1 : STRETCH]
        to_end = jnp.where(seen == seen_final, jnp.exp(final - running), 0.0)
        keep = jnp.where(seen_final == 0.0, jnp.exp(final), 0.0)
        keep_row = spread_heads(jnp.broadcast_to(keep, (keep.shape[0], STRETCH)), HEAD_DIM)[0:1]
        keep_ref[block : block + 1, :] = keep_row
        product = keep_row if product is None else product * keep_row
        dt_wide[...] = spread_heads(dt, HEAD_DIM)
        end_wide[...] = spread_heads(to_end, HEAD_DIM)

        def chunk(step, carry):
            part = lanes(step, CHUNK)
            total = conv_sum(conv_taps(x_ext, live_ref, first, part), wx_ref, bx_ref, part)
            xc = (total * sigmoid(total)).astype(bf16)
            xc_ref[here, part] = xc
            stepped = (xc.astype(f32) * dt_wide[:, part]).astype(bf16)
            xp_ref[here, part] = stepped
            ended = (stepped.astype(f32) * end_wide[:, part]).astype(bf16)
            fresh = dot(b_turned, ended)
            if block > 0:
                fresh = keep_ref[block : block + 1, part] * state[:, part] + fresh
            if block < blocks - 1:
                state[:, part] = fresh
                sloc_ref[block, :, part] = fresh.astype(bf16)
            else:
                sdev_ref[:, part] = fresh.astype(bf16)
            return carry

        lax.fori_loop(0, channels // CHUNK, chunk, 0)
    keep_ref[blocks : blocks + 1, :] = product


def place_runs(run_ref, here, run_wide, run_tall):
    running = run_ref[:, here]
    run_wide[...] = spread_heads(running, STRETCH)
    for head in range(running.shape[0]):
        run_tall[head * PAD : (head + 1) * PAD, :] = jnp.broadcast_to(
            running[head : head + 1], (PAD, STRETCH)
        )


def block_weights(scores, mask, run_wide, run_tall, head):
    column = run_wide[:, lanes(head, STRETCH)]
    row = run_tall[pl.ds(pl.multiple_of(head * PAD, PAD), PAD), :][0:1]
    segment = jnp.exp(column - row + mask)
    return segment, (scores * segment).astype(bf16)


def both_heads(value):
    is_first = iota(value.shape, 1) < HEAD_DIM
    wide = value.astype(f32)
    zero = jnp.zeros_like(wide)
    return jnp.concatenate(
        [jnp.where(is_first, wide, zero).astype(bf16), jnp.where(is_first, zero, wide).astype(bf16)],
        axis=0,
    )


def within_blocks(xp_ref, bcc_ref, run_ref, flags_ref, y_ref, run_wide, run_tall):
    rows, channels = xp_ref.shape
    for block in range(rows // STRETCH):
        here = slice(block * STRETCH, (block + 1) * STRETCH)
        mask = decay_mask(resets_seen(flags_ref[:, here]))
        scores = dot(bcc_ref[here, NSTATE:], bcc_ref[here, 0:NSTATE], ((1,), (1,)))
        place_runs(run_ref, here, run_wide, run_tall)

        def pair(step, carry):
            _, w_first = block_weights(scores, mask, run_wide, run_tall, 2 * step)
            _, w_second = block_weights(scores, mask, run_wide, run_tall, 2 * step + 1)
            part = lanes(step, PAIR)
            y_ref[here, part] = dot(
                jnp.concatenate([w_first, w_second], axis=1), both_heads(xp_ref[here, part])
            )
            return carry

        lax.fori_loop(0, channels // PAIR, pair, 0)


def start_factor(run_ref, flags_ref, here):
    seen = resets_seen(flags_ref[:, here])
    return spread_heads(jnp.where(seen == 0.0, jnp.exp(run_ref[:, here]), 0.0), HEAD_DIM)


def block_state(block, prior_ref, sloc_ref, keep_ref, part):
    state = prior_ref[:, part]
    if block == 0:
        return state
    whole = keep_ref[0:1, part]
    for step in range(1, block):
        whole = whole * keep_ref[step : step + 1, part]
    return (whole * state.astype(f32) + sloc_ref[block - 1, :, part].astype(f32)).astype(bf16)


def gate_forward(
    y_ref, prior_ref, sloc_ref, keep_ref, bcc_ref, run_ref, flags_ref, xc_ref, skip_ref, z_ref,
    go_ref, gain_ref, yssd_ref, mixed_ref, sums_ref, start_wide,
):
    rows, channels = xc_ref.shape
    for block in range(rows // STRETCH):
        here = slice(block * STRETCH, (block + 1) * STRETCH)
        start_wide[...] = start_factor(run_ref, flags_ref, here)
        c_now = bcc_ref[here, NSTATE:]

        def chunk(step, carry):
            squares, products = carry
            part = lanes(step, CHUNK)
            carried = dot(c_now, block_state(block, prior_ref, sloc_ref, keep_ref, part))
            y_ssd = y_ref[here, part] + carried * start_wide[:, part]
            yssd_ref[here, part] = y_ssd
            mixed = (y_ssd + skip_ref[0:1, part] * xc_ref[here, part].astype(f32)).astype(bf16)
            mixed_ref[here, part] = mixed
            z = z_ref[here, part].astype(f32)
            gated = mixed.astype(f32) * (z * sigmoid(z))
            gained = go_ref[here, part].astype(f32) * gain_ref[0:1, part]
            return squares + gated * gated, products + gated * gained

        zero = jnp.zeros((STRETCH, CHUNK), f32)
        squares, products = lax.fori_loop(0, channels // CHUNK, chunk, (zero, zero))
        square_column = jnp.sum(squares, axis=1, keepdims=True)
        product_column = jnp.sum(products, axis=1, keepdims=True)
        shape = (STRETCH, STRETCH)
        mixed_up = jnp.where(
            iota(shape, 1) == 0,
            jnp.broadcast_to(square_column, shape),
            jnp.broadcast_to(product_column, shape),
        )
        sums_ref[:, here] = jnp.transpose(mixed_up)[0:PAD]


def norm_factors(totals_ref, here):
    squares = totals_ref[0:1, here]
    products = totals_ref[1:2, here]
    inv_rms = lax.rsqrt(squares * (1.0 / INNER) + NORM_EPS)
    pull = inv_rms * inv_rms * inv_rms * products * (1.0 / INNER)
    return (
        jnp.concatenate([as_columns(inv_rms)] * (CHUNK // STRETCH), axis=1),
        jnp.concatenate([as_columns(pull)] * (CHUNK // STRETCH), axis=1),
    )


def gate_backward(
    totals_ref, mixed_ref, z_ref, go_ref, gain_ref, keep_ref, bcc_ref, run_ref, flags_ref,
    dy_ref, adev_ref, aloc_ref, start_wide, adjoint,
):
    rows, channels = mixed_ref.shape
    blocks = rows // STRETCH
    for block in reversed(range(blocks)):
        here = slice(block * STRETCH, (block + 1) * STRETCH)
        start_wide[...] = start_factor(run_ref, flags_ref, here)
        inv_rms, pull = norm_factors(totals_ref, here)
        c_turned = jnp.transpose(bcc_ref[here, NSTATE:].astype(f32)).astype(bf16)

        def chunk(step, carry):
            part = lanes(step, CHUNK)
            z = z_ref[here, part].astype(f32)
            gate = z * sigmoid(z)
            gained = go_ref[here, part].astype(f32) * gain_ref[0:1, part]
            d_gated = gained * inv_rms - mixed_ref[here, part].astype(f32) * gate * pull
            dy = (d_gated * gate).astype(bf16)
            dy_ref[here, part] = dy
            fresh = dot(c_turned, (dy.astype(f32) * start_wide[:, part]).astype(bf16))
            if block < blocks - 1:
                fresh = fresh + keep_ref[block : block + 1, part] * adjoint[:, part]
            if block > 0:
                adjoint[:, part] = fresh
                aloc_ref[block - 1, :, part] = fresh.astype(bf16)
            else:
                adev_ref[:, part] = fresh.astype(bf16)
            return carry

        lax.fori_loop(0, channels // CHUNK, chunk, 0)


def within_backward(
    totals_ref, mixed_ref, z_ref, go_ref, gain_ref, dy_ref, yssd_ref, xc_ref, xp_ref, bcc_ref,
    run_ref, flags_ref, prior_ref, sloc_ref, keep_ref,
    gz_ref, dxp_ref, dbc_ref, drun_ref, chan_ref, run_wide, run_tall, start_wide,
):
    rows, channels = mixed_ref.shape
    heads = run_ref.shape[0]
    chan_ref[...] = jnp.zeros_like(chan_ref)
    for block in range(rows // STRETCH):
        here = slice(block * STRETCH, (block + 1) * STRETCH)
        mask = decay_mask(resets_seen(flags_ref[:, here]))
        b_now = bcc_ref[here, 0:NSTATE]
        c_now = bcc_ref[here, NSTATE:]
        scores = dot(c_now, b_now, ((1,), (1,)))
        place_runs(run_ref, here, run_wide, run_tall)
        start_wide[...] = start_factor(run_ref, flags_ref, here)
        inv_rms, pull = norm_factors(totals_ref, here)

        def chunk(step, carry):
            d_c, d_run = carry
            part = lanes(step, CHUNK)
            z = z_ref[here, part].astype(f32)
            gate_up = sigmoid(z)
            gate = z * gate_up
            go = go_ref[here, part].astype(f32)
            mixed = mixed_ref[here, part].astype(f32)
            gated = mixed * gate
            d_gated = go * gain_ref[0:1, part] * inv_rms - gated * pull
            slope = gate_up + gate * (1.0 - gate_up)
            gz_ref[here, part] = (d_gated * mixed * slope).astype(bf16)
            dy = dy_ref[here, part].astype(f32)
            chan_ref[0:1, part] += jnp.sum(go * gated * inv_rms, axis=0, keepdims=True)
            chan_ref[1:2, part] += jnp.sum(dy * xc_ref[here, part].astype(f32), axis=0, keepdims=True)
            d_run = d_run + head_sums(dy * yssd_ref[here, part], step * CHUNK, heads)
            started = (dy * start_wide[:, part]).astype(bf16)
            state = block_state(block, prior_ref, sloc_ref, keep_ref, part)
            return d_c + dot(started, state, ((1,), (1,))), d_run

        d_c, d_run = lax.fori_loop(
            0,
            channels // CHUNK,
            chunk,
            (jnp.zeros((STRETCH, NSTATE), f32), jnp.zeros((heads, STRETCH), f32)),
        )
        drun_ref[:, here] = d_run

        def pair(step, d_scores):
            part = lanes(step, PAIR)
            s_first, w_first = block_weights(scores, mask, run_wide, run_tall, 2 * step)
            s_second, w_second = block_weights(scores, mask, run_wide, run_tall, 2 * step + 1)
            dy = dy_ref[here, part]
            d_weights = dot(dy, both_heads(xp_ref[here, part]), ((1,), (1,)))
            dxp_ref[here, part] = dot(
                jnp.concatenate([w_first, w_second], axis=0), both_heads(dy), ((0,), (0,))
            )
            return (
                d_scores + d_weights[:, 0:STRETCH] * s_first + d_weights[:, STRETCH:] * s_second
            )

        d_scores = lax.fori_loop(
            0, channels // PAIR, pair, jnp.zeros((STRETCH, STRETCH), f32)
        ).astype(bf16)
        dbc_ref[here, 0:NSTATE] = dot(d_scores, c_now, ((0,), (0,)))
        dbc_ref[here, NSTATE:] = d_c + dot(d_scores, b_now)


def conv_backward(
    extended, d_ext, live_ref, weight_ref, bias_ref, d_ref, grad_ref, tail_ref, back_ref, dw_ref,
    rows, part,
):
    width = d_ref[0:PAD, part].shape[1]
    sums = None
    for first in range(0, rows, STRETCH):
        taps = conv_taps(extended, live_ref, first, part)
        total = conv_sum(taps, weight_ref, bias_ref, part)
        up = sigmoid(total)
        d_total = d_ref[first : first + STRETCH, part] * (up + total * up * (1.0 - up))
        d_ext[PAD + first : PAD + first + STRETCH, part] = d_total
        now = [jnp.sum(d_total * each, axis=0, keepdims=True) for each in taps]
        now.append(jnp.sum(d_total, axis=0, keepdims=True))
        sums = now if sums is None else [old + new for old, new in zip(sums, now)]
    for row, value in enumerate(sums):
        dw_ref[row : row + 1, part] = value
    for first, count in [(-PAD, PAD)] + [(at, STRETCH) for at in range(0, rows, STRETCH)]:
        begin = PAD + first
        grad = weight_ref[0:1, part] * d_ext[begin : begin + count, part]
        for lag in range(1, CONV):
            mask = live_ref[begin : begin + count, HALO + lag - 1 : HALO + lag]
            grad = grad + weight_ref[lag : lag + 1, part] * (
                d_ext[begin + lag : begin + lag + count, part]
                * jnp.broadcast_to(mask, (count, width))
            )
        if first < 0:
            back_ref[:, part] = grad
        else:
            grad_ref[first : first + count, part] = grad.astype(bf16)
            if first + count == rows:
                tail_ref[:, part] = grad[count - PAD :]


def finish_backward(
    later_ref, aloc_ref, prior_ref, sloc_ref, keep_ref, dxp_ref, dbc_ref, drun_ref, xp_ref, dy_ref,
    skip_ref, bcc_ref, run_ref, dt_ref, flags_ref, live_ref, x_ref, xh_ref, bc_ref, bch_ref,
    wx_ref, bx_ref, wb_ref, bb_ref, alog_ref, dtb_ref, dtr_ref,
    gx_ref, xtail_ref, xback_ref, dwx_ref, gbc_ref, bctail_ref, bcback_ref, dwb_ref, gdt_ref,
    heads_ref, x_ext, bc_ext, dx_ext, dbc_ext, d_x, d_bc, dt_wide, end_wide, ends,
):
    rows, channels = xp_ref.shape
    heads = run_ref.shape[0]
    blocks = rows // STRETCH
    fill_extended(x_ext, xh_ref, x_ref)
    fill_extended(bc_ext, bch_ref, bc_ref)
    for ext in (dx_ext, dbc_ext):
        ext[0:PAD, :] = jnp.zeros((PAD, ext.shape[1]), f32)
        ext[PAD + rows :, :] = jnp.zeros((PAD, ext.shape[1]), f32)
    rate = jnp.exp(alog_ref[...])
    d_alog = jnp.zeros((heads, 1), f32)
    d_dtb = jnp.zeros((heads, 1), f32)
    for block in range(blocks):
        here = slice(block * STRETCH, (block + 1) * STRETCH)
        seen = resets_seen(flags_ref[:, here])
        running = run_ref[:, here]
        dt = dt_ref[:, here]
        to_end = jnp.where(
            seen == seen[:, STRETCH - 1 : STRETCH],
            jnp.exp(running[:, STRETCH - 1 : STRETCH] - running),
            0.0,
        )
        dt_wide[...] = spread_heads(dt, HEAD_DIM)
        end_wide[...] = spread_heads(to_end, HEAD_DIM)
        b_now = bcc_ref[here, 0:NSTATE]

        def chunk(step, carry):
            d_b, per_step = carry
            part = lanes(step, CHUNK)
            later = later_ref[:, part]
            if block < blocks - 1:
                whole = keep_ref[block + 1 : block + 2, part]
                for place in range(block + 2, blocks):
                    whole = whole * keep_ref[place : place + 1, part]
                later = (aloc_ref[block, :, part].astype(f32) + whole * later.astype(f32)).astype(bf16)
            state = block_state(block, prior_ref, sloc_ref, keep_ref, part)
            d_keep = jnp.sum(later.astype(f32) * state.astype(f32), axis=0, keepdims=True)
            stepped = xp_ref[here, part].astype(f32)
            end = end_wide[:, part]
            d_end = dot(b_now, later) * end
            d_stepped = dxp_ref[here, part] + d_end
            ended = stepped * end
            ends[0:1, part] = (
                jnp.sum(stepped * d_end, axis=0, keepdims=True)
                + d_keep * keep_ref[block : block + 1, part]
            )
            d_x[here, part] = d_stepped * dt_wide[:, part] + skip_ref[0:1, part] * dy_ref[
                here, part
            ].astype(f32)
            return (
                d_b + dot(ended.astype(bf16), later, ((1,), (1,))),
                per_step + head_sums(stepped * d_stepped, step * CHUNK, heads),
            )

        d_b, per_step = lax.fori_loop(
            0,
            channels // CHUNK,
            chunk,
            (jnp.zeros((STRETCH, NSTATE), f32), jnp.zeros((heads, STRETCH), f32)),
        )
        d_bc[here, 0:NSTATE] = dbc_ref[here, 0:NSTATE] + d_b
        d_bc[here, NSTATE:] = dbc_ref[here, NSTATE:]
        at_end = head_sums(jnp.broadcast_to(ends[0:1, :], (STRETCH, channels)), 0, heads)
        is_last = iota((heads, STRETCH), 1) == STRETCH - 1
        d_run = drun_ref[:, here] - per_step + jnp.where(is_last, at_end, 0.0)
        shape = (STRETCH, STRETCH)
        d_log = dot_full(d_run, (iota(shape, 0) >= iota(shape, 1)).astype(f32))
        d_dt = per_step / dt - rate * d_log
        raw = dtr_ref[:, here].astype(f32) + dtb_ref[...]
        d_raw = d_dt / (1.0 + jnp.exp(-raw))
        gdt_ref[:, here] = d_raw
        d_alog = d_alog - jnp.sum(d_log * dt, axis=1, keepdims=True) * rate
        d_dtb = d_dtb + jnp.sum(d_raw, axis=1, keepdims=True)
    shape = heads_ref.shape
    heads_ref[...] = jnp.where(
        iota(shape, 1) == 0, jnp.broadcast_to(d_alog, shape), jnp.broadcast_to(d_dtb, shape)
    )

    def conv_chunk(step, carry):
        conv_backward(
            x_ext, dx_ext, live_ref, wx_ref, bx_ref, d_x, gx_ref, xtail_ref, xback_ref, dwx_ref,
            rows, lanes(step, STRETCH),
        )
        return carry

    lax.fori_loop(0, channels // STRETCH, conv_chunk, 0)
    for step in range(2):
        conv_backward(
            bc_ext, dbc_ext, live_ref, wb_ref, bb_ref, d_bc, gbc_ref, bctail_ref, bcback_ref,
            dwb_ref, rows, slice(step * NSTATE, (step + 1) * NSTATE),
        )


def call(kernel, operands, outs, scratch, flops, name):
    specs, arrays, count = [], [], 0
    for array, block, index in operands:
        block = array.shape if block is None else block
        index = (0,) * len(block) if index is None else index
        specs.append(pl.BlockSpec(block, functools.partial(lambda fixed, i: fixed, index)))
        arrays.append(array)
        size = 1
        for extent in block:
            size *= extent
        count += size * array.dtype.itemsize
    shapes = [jax.ShapeDtypeStruct(shape, dtype) for shape, dtype in outs]
    out_specs = [
        pl.BlockSpec(shape, functools.partial(lambda rank, i: (0,) * rank, len(shape)))
        for shape, _ in outs
    ]
    for shape in shapes:
        count += shape.size * shape.dtype.itemsize
    return pl.pallas_call(
        kernel,
        grid=(1,),
        in_specs=specs,
        out_specs=out_specs,
        out_shape=shapes,
        scratch_shapes=[pltpu.VMEM(shape, f32) for shape in scratch],
        compiler_params=pltpu.CompilerParams(vmem_limit_bytes=VMEM_LIMIT),
        cost_estimate=pl.CostEstimate(flops=flops, bytes_accessed=count, transcendentals=0),
        name=name,
    )(*arrays)


def chain(parts, decays, axis, backward):
    count = lax.axis_size(axis)
    arrived = [jnp.zeros(part.shape, bf16) for part in parts]
    for hop in range(count - 1):
        pairs = [(count - 1 - hop, count - 2 - hop)] if backward else [(hop, hop + 1)]
        for place, part in enumerate(parts):
            leaving = part
            if hop > 0:
                leaving = (decays[place] * arrived[place].astype(f32) + part.astype(f32)).astype(bf16)
            moved = lax.ppermute(leaving, axis, pairs)
            arrived[place] = moved if hop == 0 else arrived[place] + moved
    return arrived


def exchange_sum(value, axis):
    count = lax.axis_size(axis)
    stride = 1
    while stride < count:
        value = value + lax.ppermute(value, axis, [(i, i ^ stride) for i in range(count)])
        stride *= 2
    return value


def per_device(
    x_raw, bc_raw, z_gate, dt_raw, resets, conv_x_weight, conv_x_bias, conv_bc_weight,
    conv_bc_bias, a_log, dt_bias, skip_weight, norm_gain, grad_out,
):
    rows, inner = x_raw.shape[1:]
    groups = bc_raw.shape[3] // NSTATE
    heads = a_log.shape[0] // groups
    channels = inner // groups
    blocks = rows // STRETCH
    width = 2 * NSTATE

    def by_group(value):
        lead = value.shape[:-2]
        split = value.reshape(lead + (2, groups, NSTATE))
        return jnp.moveaxis(split, -3, -2).reshape(lead + (groups * width,))

    x_own, z_own, go_own, dt_own = x_raw[0], z_gate[0], grad_out[0], dt_raw[0]
    bc_own = by_group(bc_raw[0])
    flags = resets
    clear = 1.0 - resets[0].astype(f32)
    tail_keep = jnp.stack([clear[-1] * clear[-2], clear[-1], jnp.ones((), f32)])[:, None]
    tails = jnp.concatenate([x_own[-HALO:], bc_own[-HALO:]], axis=1) * tail_keep.astype(bf16)
    count = lax.axis_size("ctx")
    halo = lax.ppermute(tails, "ctx", [(i, i + 1) for i in range(count - 1)])
    halo = jnp.pad(halo.astype(f32), ((PAD - HALO, 0), (0, 0)))
    x_halo, bc_halo = halo[:, :inner], halo[:, inner:]
    one = jnp.ones((HALO,), f32)
    before = jnp.concatenate([one, clear])
    live = [clear]
    for lag in range(2, CONV):
        live.append(live[-1] * before[HALO + 1 - lag : HALO + 1 - lag + rows])
    back_live = [
        jnp.concatenate([jnp.zeros((PAD - lag,), f32), mask, jnp.zeros((lag,), f32)])
        for lag, mask in enumerate(live, 1)
    ]
    live = [jnp.concatenate([jnp.zeros((PAD,), f32), mask]) for mask in live]
    live = jnp.stack(live + back_live + [jnp.zeros((rows + PAD,), f32)] * 2, axis=1)
    dt = jax.nn.softplus(dt_own.astype(f32) + dt_bias[:, None])
    alog_column, dtb_column = a_log[:, None], dt_bias[:, None]
    bx, gain = conv_x_bias[None], norm_gain[None]
    wb, bb = by_group(conv_bc_weight), by_group(conv_bc_bias)[None]
    skip = jnp.repeat(skip_weight, HEAD_DIM)[None]

    def wide(array, group):
        return (array, (array.shape[0], channels), (0, group))

    def narrow(array, group):
        return (array, (array.shape[0], width), (0, group))

    def per_head(array, group):
        return (array, (heads, array.shape[1]), (group, 0))

    def whole(array):
        return (array, None, None)

    keep_rows = -(-(blocks + 1) // PAD) * PAD
    tall = (rows, channels)
    state_shape = (NSTATE, channels)
    local_shape = (blocks - 1, NSTATE, channels)
    work = rows * channels * STRETCH
    group_range = range(groups)
    held = []
    for g in group_range:
        held.append(
            call(
                conv_and_state,
                [
                    wide(x_own, g), wide(x_halo, g), narrow(bc_own, g), narrow(bc_halo, g),
                    wide(conv_x_weight, g), wide(bx, g), narrow(wb, g), narrow(bb, g),
                    per_head(dt, g), per_head(alog_column, g), whole(flags), whole(live),
                ],
                [
                    (tall, bf16), (tall, bf16), ((rows, width), bf16), ((heads, rows), f32),
                    ((keep_rows, channels), f32), (state_shape, bf16), (local_shape, bf16),
                ],
                [
                    (rows + PAD, channels), (rows + PAD, width), (STRETCH, channels),
                    (STRETCH, channels), state_shape,
                ],
                2 * work,
                "conv_and_state",
            )
        )
    xc, xp, bcc, run, keep, s_dev, s_loc = zip(*held)
    decay = [k[blocks : blocks + 1] for k in keep]
    prior = chain(s_dev, decay, "ctx", False)
    y_within = [
        call(
            within_blocks,
            [whole(xp[g]), whole(bcc[g]), whole(run[g]), whole(flags)],
            [(tall, f32)],
            [(STRETCH, heads * STRETCH), (heads * PAD, STRETCH)],
            6 * work,
            "within_blocks",
        )[0]
        for g in group_range
    ]
    held = [
        call(
            gate_forward,
            [
                whole(y_within[g]), whole(prior[g]), whole(s_loc[g]), whole(keep[g]), whole(bcc[g]),
                whole(run[g]), whole(flags), whole(xc[g]), wide(skip, g), wide(z_own, g),
                wide(go_own, g), wide(gain, g),
            ],
            [(tall, f32), (tall, bf16), ((PAD, rows), f32)],
            [(STRETCH, channels)],
            2 * work,
            "gate_forward",
        )
        for g in group_range
    ]
    y_ssd, mixed, sums = zip(*held)
    totals = exchange_sum(sum(sums[1:], sums[0]), "head")
    held = [
        call(
            gate_backward,
            [
                whole(totals), whole(mixed[g]), wide(z_own, g), wide(go_own, g), wide(gain, g),
                whole(keep[g]), whole(bcc[g]), whole(run[g]), whole(flags),
            ],
            [(tall, bf16), (state_shape, bf16), (local_shape, bf16)],
            [(STRETCH, channels), state_shape],
            2 * work,
            "gate_backward",
        )
        for g in group_range
    ]
    dy, a_dev, a_loc = zip(*held)
    later = chain(a_dev, decay, "ctx", True)
    held = [
        call(
            within_backward,
            [
                whole(totals), whole(mixed[g]), wide(z_own, g), wide(go_own, g), wide(gain, g),
                whole(dy[g]), whole(y_ssd[g]), whole(xc[g]), whole(xp[g]), whole(bcc[g]),
                whole(run[g]), whole(flags), whole(prior[g]), whole(s_loc[g]), whole(keep[g]),
            ],
            [
                (tall, bf16), (tall, f32), ((rows, width), f32), ((heads, rows), f32),
                ((PAD, channels), f32),
            ],
            [(STRETCH, heads * STRETCH), (heads * PAD, STRETCH), (STRETCH, channels)],
            10 * work,
            "within_backward",
        )
        for g in group_range
    ]
    gz, dxp, dbc, drun, chan = zip(*held)
    held = [
        call(
            finish_backward,
            [
                whole(later[g]), whole(a_loc[g]), whole(prior[g]), whole(s_loc[g]), whole(keep[g]),
                whole(dxp[g]), whole(dbc[g]), whole(drun[g]), whole(xp[g]), whole(dy[g]),
                wide(skip, g), whole(bcc[g]), whole(run[g]), per_head(dt, g), whole(flags),
                whole(live), wide(x_own, g), wide(x_halo, g), narrow(bc_own, g), narrow(bc_halo, g),
                wide(conv_x_weight, g), wide(bx, g), narrow(wb, g), narrow(bb, g),
                per_head(alog_column, g), per_head(dtb_column, g), per_head(dt_own, g),
            ],
            [
                (tall, bf16), ((PAD, channels), f32), ((PAD, channels), f32), ((PAD, channels), f32),
                ((rows, width), bf16), ((PAD, width), f32), ((PAD, width), f32), ((PAD, width), f32),
                ((heads, rows), f32), ((heads, STRETCH), f32),
            ],
            [
                (rows + PAD, channels), (rows + PAD, width), (rows + 2 * PAD, channels),
                (rows + 2 * PAD, width), tall, (rows, width), (STRETCH, channels),
                (STRETCH, channels), (PAD, channels),
            ],
            4 * work,
            "finish_backward",
        )
        for g in group_range
    ]
    gx, x_tail, x_back, dwx, gbc, bc_tail, bc_back, dwb, gdt, head_terms = zip(*held)

    def joined(pieces):
        return jnp.concatenate(pieces, axis=1)

    back = joined(x_back + bc_back)[PAD - HALO :]
    back = lax.ppermute(back, "ctx", [(i + 1, i) for i in range(count - 1)])
    ending = (joined(x_tail + bc_tail)[PAD - HALO :] + back * tail_keep).astype(bf16)
    grad_x = lax.dynamic_update_slice(joined(gx), ending[:, :inner], (rows - HALO, 0))
    grad_bc = lax.dynamic_update_slice(joined(gbc), ending[:, inner:], (rows - HALO, 0))

    def ungroup(value):
        lead = value.shape[:-1]
        split = value.reshape(lead + (groups, 2, NSTATE))
        return jnp.moveaxis(split, -3, -2).reshape(lead + (2, groups * NSTATE))

    chan_all, dwx_all, dwb_all = joined(chan), joined(dwx), joined(dwb)
    head_all = jnp.concatenate(head_terms, axis=0)[:, :2]
    pieces = [
        dwx_all[: CONV + 1].reshape(-1),
        dwb_all[: CONV + 1].reshape(-1),
        chan_all[0],
        jnp.sum(chan_all[1].reshape(-1, HEAD_DIM), axis=1),
        head_all[:, 0],
        head_all[:, 1],
    ]
    sizes = [piece.shape[0] for piece in pieces]
    flat = jnp.concatenate(pieces)
    flat = exchange_sum(exchange_sum(flat, "dp"), "ctx")
    flat = flat * float(lax.axis_size("dp") * count * rows) ** (-0.5)
    cut, at = [], 0
    for size in sizes:
        cut.append(flat[at : at + size])
        at += size
    x_terms = cut[0].reshape(CONV + 1, inner)
    bc_terms = ungroup(cut[1].reshape(CONV + 1, groups * width))
    return (
        grad_x[None],
        ungroup(grad_bc)[None],
        joined(gz)[None],
        jnp.concatenate(gdt, axis=0)[None],
        x_terms[:CONV],
        x_terms[CONV],
        bc_terms[:CONV],
        bc_terms[CONV],
        cut[4],
        cut[5],
        cut[3],
        cut[2],
    )


def solution(mesh):
    return jax.shard_map(
        per_device,
        mesh=mesh,
        in_specs=(
            P("dp", "ctx", "head"),
            P("dp", "ctx", None, "head"),
            P("dp", "ctx", "head"),
            P("dp", "head", "ctx"),
            P("dp", "ctx"),
            P(None, "head"),
            P("head"),
            P(None, None, "head"),
            P(None, "head"),
            P("head"),
            P("head"),
            P("head"),
            P("head"),
            P("dp", "ctx", "head"),
        ),
        out_specs=(
            P("dp", "ctx", "head"),
            P("dp", "ctx", None, "head"),
            P("dp", "ctx", "head"),
            P("dp", "head", "ctx"),
            P(None, "head"),
            P("head"),
            P(None, None, "head"),
            P(None, "head"),
            P("head"),
            P("head"),
            P("head"),
            P("head"),
        ),
        check_vma=False,
    )
```

```python
import functools

import jax
import jax.numpy as jnp
from jax import lax
from jax.experimental import pallas as pl
from jax.experimental.pallas import tpu as pltpu
from jax.sharding import PartitionSpec as P

HEAD_DIM = 64
NSTATE = 128
CONV = 4
STRETCH = 128
INNER = 8192
HALO = CONV - 1
PAD = 8
CHUNK = 256
PAIR = 2 * HEAD_DIM
NORM_EPS = 1e-05
LOWEST = -1e30
GAIN, SKIP, BACK = CONV + 1, CONV + 2, CONV + 3
PACKED = BACK + HALO
BLOCKED_LIMIT = 40 * 1024 * 1024
VMEM_LIMIT = 24 * 1024 * 1024
UNROLL = 2

f32 = jnp.float32
bf16 = jnp.bfloat16


def dot(a, b, contract=((1,), (0,))):
    return lax.dot_general(a, b, (contract, ((), ())), preferred_element_type=f32)


def dot_full(a, b):
    return lax.dot_general(
        a, b, (((1,), (0,)), ((), ())), precision=lax.Precision.HIGHEST, preferred_element_type=f32
    )


def iota(shape, dim):
    return lax.broadcasted_iota(jnp.int32, shape, dim)


def split3(value):
    high = value.astype(bf16)
    rest = value - high.astype(f32)
    middle = rest.astype(bf16)
    low = (rest - middle.astype(f32)).astype(bf16)
    return jnp.concatenate([high, middle, low], axis=0)


def spread_heads(rows, width):
    heads = rows.shape[0]
    shape = (heads, heads * width)
    pick = (iota(shape, 1) // width == iota(shape, 0)).astype(f32).astype(bf16)
    return dot(split3(rows), jnp.concatenate([pick] * 3, axis=0), ((0,), (0,)))


def head_sums(value, first, heads):
    shape = (heads, value.shape[1])
    pick = ((iota(shape, 1) + first) // HEAD_DIM == iota(shape, 0)).astype(f32).astype(bf16)
    high = value.astype(bf16)
    low = (value - high.astype(f32)).astype(bf16)
    last = ((1,), (1,))
    return dot(pick, high, last) + dot(pick, low, last)


def as_columns(row):
    return jnp.transpose(jnp.broadcast_to(row, (STRETCH, STRETCH)))


def sigmoid(value):
    return 0.5 * jnp.tanh(0.5 * value) + 0.5


def upper_ones():
    shape = (STRETCH, STRETCH)
    return (iota(shape, 0) <= iota(shape, 1)).astype(f32)


def resets_seen(flags_row):
    flags = jnp.broadcast_to(flags_row.astype(f32), (PAD, STRETCH)).astype(bf16)
    return dot(flags, upper_ones().astype(bf16))[0:1]


def decay_mask(seen):
    shape = (STRETCH, STRETCH)
    same = (as_columns(seen) == jnp.broadcast_to(seen, shape)) & (iota(shape, 0) >= iota(shape, 1))
    return jnp.where(same, 0.0, LOWEST)


def lanes(position, size):
    return pl.ds(pl.multiple_of(position * size, size), size)


def to_column(row, first, heads):
    shape = (heads, row.shape[1])
    pick = iota(shape, 1) == iota(shape, 0) + first
    return jnp.sum(jnp.where(pick, jnp.broadcast_to(row, shape), 0.0), axis=1, keepdims=True)


def over_channels(column):
    return spread_heads(jnp.broadcast_to(column, (column.shape[0], STRETCH)), HEAD_DIM)[0:1]


def softplus(value):
    small = jnp.exp(-jnp.abs(value))
    series = small * (1.0 - small * (1 / 2 - small * (1 / 3 - small * (1 / 4 - small * (1 / 5)))))
    return jnp.maximum(value, 0.0) + jnp.where(small < 0.03, series, jnp.log(1.0 + small))


def step_sizes(dtr_ref, dtb_ref, group):
    heads = dtr_ref.shape[0]
    return softplus(dtr_ref[...].astype(f32) + to_column(dtb_ref[...], group * heads, heads))


def to_end_factor(running, seen):
    final = running[:, STRETCH - 1 : STRETCH]
    return jnp.where(seen == seen[:, STRETCH - 1 : STRETCH], jnp.exp(final - running), 0.0)


def doubled(value):
    return jnp.concatenate([value, value], axis=1)


def fill_live(flags_ref, clear, live):
    rows = flags_ref.shape[1]
    clear[0:PAD, :] = jnp.ones((PAD, STRETCH), f32)
    for first in range(0, rows, STRETCH):
        flags = flags_ref[:, first : first + STRETCH].astype(f32)
        clear[PAD + first : PAD + first + STRETCH, :] = as_columns(1.0 - flags)
    for first in range(0, rows, STRETCH):
        begin = PAD + first
        product = clear[begin : begin + STRETCH, :]
        live[0, begin : begin + STRETCH, :] = product
        for lag in range(2, CONV):
            product = product * clear[begin - lag + 1 : begin - lag + 1 + STRETCH, :]
            live[lag - 1, begin : begin + STRETCH, :] = product


def fill_extended(extended, halo_ref, rows_ref):
    extended[PAD - HALO : PAD, :] = halo_ref[...]
    extended[PAD:, :] = rows_ref[...].astype(f32)


def conv_total(extended, live, weight_ref, bias_ref, first, part):
    begin = PAD + first
    total = bias_ref[0:1, part] + weight_ref[0:1, part] * extended[begin : begin + STRETCH, part]
    width = total.shape[1] // STRETCH
    for lag in range(1, CONV):
        mask = jnp.concatenate([live[lag - 1, begin : begin + STRETCH, :]] * width, axis=1)
        total = total + weight_ref[lag : lag + 1, part] * (
            extended[begin - lag : begin - lag + STRETCH, part] * mask
        )
    return total


def tail_factors(flags_ref):
    flags = flags_ref[:, flags_ref.shape[1] - STRETCH :].astype(f32)
    clear = as_columns(1.0 - flags)
    last = clear[STRETCH - 1 :]
    both = last * clear[STRETCH - 2 : STRETCH - 1]
    return jnp.concatenate([both, last, jnp.ones_like(last)], axis=0)[:, 0:1]


def tails(x_ref, bc_ref, flags_ref, out_ref):
    keep = tail_factors(flags_ref)
    inner = x_ref.shape[2]
    out_ref[:, 0:inner] = x_ref[0].astype(f32)[x_ref.shape[1] - HALO :] * keep
    groups = bc_ref.shape[3] // NSTATE
    for which in range(2):
        rows = bc_ref[0, :, which, :].astype(f32)[bc_ref.shape[1] - HALO :] * keep
        for group in range(groups):
            first = inner + (2 * group + which) * NSTATE
            out_ref[:, first : first + NSTATE] = rows[:, group * NSTATE : (group + 1) * NSTATE]


def conv_and_state(
    x_ref, xh_ref, bc_ref, bch_ref, wx_ref, bx_ref, wb_ref, bb_ref, dtr_ref, dtb_ref, alog_ref,
    flags_ref, xc_ref, xp_ref, ux_ref, bcc_ref, ubc_ref, dt_ref, run_ref, keep_ref, sdev_ref,
    sloc_ref, x_ext, bc_ext, clear, live, dt_wide, end_wide, state, *, group,
):
    rows, channels = x_ref.shape
    heads = dtr_ref.shape[0]
    fill_extended(x_ext, xh_ref, x_ref)
    fill_extended(bc_ext, bch_ref, bc_ref)
    fill_live(flags_ref, clear, live)
    blocks = rows // STRETCH
    rate = to_column(jnp.exp(alog_ref[...]), group * heads, heads)
    dt_ref[...] = step_sizes(dtr_ref, dtb_ref, group)
    product = None
    for block in range(blocks):
        first = block * STRETCH
        here = slice(first, first + STRETCH)
        every = slice(None)
        total = conv_total(bc_ext, live, wb_ref, bb_ref, first, every)
        ubc_ref[here, :] = total
        bc_now = (total * sigmoid(total)).astype(bf16)
        bcc_ref[here, :] = bc_now
        b_turned = jnp.transpose(bc_now[:, 0:NSTATE].astype(f32)).astype(bf16)
        seen = resets_seen(flags_ref[:, here])
        dt = dt_ref[:, here]
        running = dot_full(-rate * dt, upper_ones())
        run_ref[:, here] = running
        final = running[:, STRETCH - 1 : STRETCH]
        keep = jnp.where(seen[:, STRETCH - 1 : STRETCH] == 0.0, jnp.exp(final), 0.0)
        keep_row = over_channels(keep)
        keep_ref[block : block + 1, :] = keep_row
        product = keep_row if product is None else product * keep_row
        dt_wide[...] = spread_heads(dt, HEAD_DIM)
        end_wide[...] = spread_heads(to_end_factor(running, seen), HEAD_DIM)

        def chunk(step, carry):
            part = lanes(step, CHUNK)
            total = conv_total(x_ext, live, wx_ref, bx_ref, first, part)
            ux_ref[here, part] = total
            xc = (total * sigmoid(total)).astype(bf16)
            xc_ref[here, part] = xc
            stepped = (xc.astype(f32) * dt_wide[:, part]).astype(bf16)
            xp_ref[here, part] = stepped
            ended = (stepped.astype(f32) * end_wide[:, part]).astype(bf16)
            fresh = dot(b_turned, ended)
            if block > 0:
                fresh = keep_ref[block : block + 1, part] * state[:, part] + fresh
            if block < blocks - 1:
                state[:, part] = fresh
                sloc_ref[block, :, part] = fresh.astype(bf16)
            else:
                sdev_ref[:, part] = fresh.astype(bf16)
            return carry

        lax.fori_loop(0, channels // CHUNK, chunk, 0, unroll=UNROLL)
    keep_ref[blocks : blocks + 1, :] = product


def place_runs(run_ref, here, run_wide, run_tall):
    running = run_ref[:, here]
    run_wide[...] = spread_heads(running, STRETCH)
    for head in range(running.shape[0]):
        run_tall[head * PAD : (head + 1) * PAD, :] = jnp.broadcast_to(
            running[head : head + 1], (PAD, STRETCH)
        )


def block_weights(scores, mask, run_wide, run_tall, head):
    column = run_wide[:, lanes(head, STRETCH)]
    row = run_tall[pl.ds(pl.multiple_of(head * PAD, PAD), PAD), :][0:1]
    segment = jnp.exp(column - row + mask)
    return segment, (scores * segment).astype(bf16)


def both_heads(value):
    is_first = iota(value.shape, 1) < HEAD_DIM
    wide = value.astype(f32)
    zero = jnp.zeros_like(wide)
    return jnp.concatenate(
        [jnp.where(is_first, wide, zero).astype(bf16), jnp.where(is_first, zero, wide).astype(bf16)],
        axis=0,
    )


def slope_of(total):
    up = sigmoid(total)
    return up + total * up * (1.0 - up)


def within_blocks(
    xp_ref, bcc_ref, run_ref, flags_ref, ux_ref, ubc_ref, y_ref, sx_ref, sbc_ref, run_wide, run_tall
):
    rows, channels = xp_ref.shape
    for block in range(rows // STRETCH):
        here = slice(block * STRETCH, (block + 1) * STRETCH)
        mask = decay_mask(resets_seen(flags_ref[:, here]))
        scores = dot(bcc_ref[here, NSTATE:], bcc_ref[here, 0:NSTATE], ((1,), (1,)))
        place_runs(run_ref, here, run_wide, run_tall)
        sbc_ref[here, :] = slope_of(ubc_ref[here, :])

        def pair(step, carry):
            _, w_first = block_weights(scores, mask, run_wide, run_tall, 2 * step)
            _, w_second = block_weights(scores, mask, run_wide, run_tall, 2 * step + 1)
            part = lanes(step, PAIR)
            y_ref[here, part] = dot(
                jnp.concatenate([w_first, w_second], axis=1), both_heads(xp_ref[here, part])
            )
            sx_ref[here, part] = slope_of(ux_ref[here, part])
            return carry

        lax.fori_loop(0, channels // PAIR, pair, 0, unroll=UNROLL)


def start_factor(run_ref, flags_ref, here):
    seen = resets_seen(flags_ref[:, here])
    return spread_heads(jnp.where(seen == 0.0, jnp.exp(run_ref[:, here]), 0.0), HEAD_DIM)


def block_state(block, prior_ref, sloc_ref, keep_ref, part):
    state = prior_ref[0][:, part] + prior_ref[1][:, part]
    if block == 0:
        return state
    whole = keep_ref[0:1, part]
    for step in range(1, block):
        whole = whole * keep_ref[step : step + 1, part]
    return (whole * state.astype(f32) + sloc_ref[block - 1, :, part].astype(f32)).astype(bf16)


def gate_forward(
    y_ref, early_ref, last_ref, sloc_ref, keep_ref, bcc_ref, run_ref, flags_ref, xc_ref, skip_ref,
    z_ref, go_ref, gain_ref, yssd_ref, mixed_ref, sums_ref, start_wide, skip_wide, *, group,
):
    rows, channels = xc_ref.shape
    heads = run_ref.shape[0]
    prior_ref = (early_ref, last_ref)
    skip_wide[0:1, :] = over_channels(to_column(skip_ref[...], group * heads, heads))
    for block in range(rows // STRETCH):
        here = slice(block * STRETCH, (block + 1) * STRETCH)
        start_wide[...] = start_factor(run_ref, flags_ref, here)
        c_now = bcc_ref[here, NSTATE:]

        def chunk(step, carry):
            squares, products = carry
            part = lanes(step, CHUNK)
            carried = dot(c_now, block_state(block, prior_ref, sloc_ref, keep_ref, part))
            y_ssd = y_ref[here, part] + carried * start_wide[:, part]
            yssd_ref[here, part] = y_ssd
            mixed = (y_ssd + skip_wide[0:1, part] * xc_ref[here, part].astype(f32)).astype(bf16)
            mixed_ref[here, part] = mixed
            z = z_ref[here, part].astype(f32)
            gated = mixed.astype(f32) * (z * sigmoid(z))
            gained = go_ref[here, part].astype(f32) * gain_ref[0:1, part]
            return squares + gated * gated, products + gated * gained

        zero = jnp.zeros((STRETCH, CHUNK), f32)
        squares, products = lax.fori_loop(
            0, channels // CHUNK, chunk, (zero, zero), unroll=UNROLL
        )
        square_column = jnp.sum(squares, axis=1, keepdims=True)
        product_column = jnp.sum(products, axis=1, keepdims=True)
        shape = (STRETCH, STRETCH)
        mixed_up = jnp.where(
            iota(shape, 1) == 0,
            jnp.broadcast_to(square_column, shape),
            jnp.broadcast_to(product_column, shape),
        )
        sums_ref[:, here] = jnp.transpose(mixed_up)[0:PAD]


def norm_factors(totals_ref, here):
    squares = totals_ref[0:1, here]
    products = totals_ref[1:2, here]
    inv_rms = lax.rsqrt(squares * (1.0 / INNER) + NORM_EPS)
    pull = inv_rms * inv_rms * inv_rms * products * (1.0 / INNER)
    return doubled(as_columns(inv_rms)), doubled(as_columns(pull))


def gate_backward(
    totals_ref, mixed_ref, z_ref, go_ref, gain_ref, keep_ref, bcc_ref, run_ref, flags_ref,
    dy_ref, adev_ref, aloc_ref, start_wide, adjoint,
):
    rows, channels = mixed_ref.shape
    blocks = rows // STRETCH
    for block in reversed(range(blocks)):
        here = slice(block * STRETCH, (block + 1) * STRETCH)
        start_wide[...] = start_factor(run_ref, flags_ref, here)
        inv_rms, pull = norm_factors(totals_ref, here)
        c_turned = jnp.transpose(bcc_ref[here, NSTATE:].astype(f32)).astype(bf16)

        def chunk(step, carry):
            part = lanes(step, CHUNK)
            z = z_ref[here, part].astype(f32)
            gate = z * sigmoid(z)
            gained = go_ref[here, part].astype(f32) * gain_ref[0:1, part]
            d_gated = gained * inv_rms - mixed_ref[here, part].astype(f32) * gate * pull
            dy = (d_gated * gate).astype(bf16)
            dy_ref[here, part] = dy
            fresh = dot(c_turned, (dy.astype(f32) * start_wide[:, part]).astype(bf16))
            if block < blocks - 1:
                fresh = fresh + keep_ref[block : block + 1, part] * adjoint[:, part]
            if block > 0:
                adjoint[:, part] = fresh
                aloc_ref[block - 1, :, part] = fresh.astype(bf16)
            else:
                adev_ref[:, part] = fresh.astype(bf16)
            return carry

        lax.fori_loop(0, channels // CHUNK, chunk, 0, unroll=UNROLL)


def within_backward(
    totals_ref, mixed_ref, z_ref, go_ref, gain_ref, dy_ref, yssd_ref, xc_ref, xp_ref, bcc_ref,
    run_ref, flags_ref, early_ref, last_ref, sloc_ref, keep_ref,
    gz_ref, dxp_ref, dbc_ref, drun_ref, chan_ref, run_wide, run_tall, start_wide,
):
    rows, channels = mixed_ref.shape
    heads = run_ref.shape[0]
    prior_ref = (early_ref, last_ref)
    chan_ref[...] = jnp.zeros_like(chan_ref)
    for block in range(rows // STRETCH):
        here = slice(block * STRETCH, (block + 1) * STRETCH)
        mask = decay_mask(resets_seen(flags_ref[:, here]))
        b_now = bcc_ref[here, 0:NSTATE]
        c_now = bcc_ref[here, NSTATE:]
        scores = dot(c_now, b_now, ((1,), (1,)))
        place_runs(run_ref, here, run_wide, run_tall)
        start_wide[...] = start_factor(run_ref, flags_ref, here)
        inv_rms, pull = norm_factors(totals_ref, here)

        def chunk(step, carry):
            d_c, d_run = carry
            part = lanes(step, CHUNK)
            z = z_ref[here, part].astype(f32)
            gate_up = sigmoid(z)
            gate = z * gate_up
            go = go_ref[here, part].astype(f32)
            mixed = mixed_ref[here, part].astype(f32)
            gated = mixed * gate
            d_gated = go * gain_ref[0:1, part] * inv_rms - gated * pull
            slope = gate_up + gate * (1.0 - gate_up)
            gz_ref[here, part] = (d_gated * mixed * slope).astype(bf16)
            dy = dy_ref[here, part].astype(f32)
            chan_ref[0:1, part] += jnp.sum(go * gated * inv_rms, axis=0, keepdims=True)
            chan_ref[1:2, part] += jnp.sum(dy * xc_ref[here, part].astype(f32), axis=0, keepdims=True)
            d_run = d_run + head_sums(dy * yssd_ref[here, part], step * CHUNK, heads)
            started = (dy * start_wide[:, part]).astype(bf16)
            state = block_state(block, prior_ref, sloc_ref, keep_ref, part)
            return d_c + dot(started, state, ((1,), (1,))), d_run

        d_c, d_run = lax.fori_loop(
            0,
            channels // CHUNK,
            chunk,
            (jnp.zeros((STRETCH, NSTATE), f32), jnp.zeros((heads, STRETCH), f32)),
            unroll=UNROLL,
        )
        drun_ref[:, here] = d_run

        def pair(step, d_scores):
            part = lanes(step, PAIR)
            s_first, w_first = block_weights(scores, mask, run_wide, run_tall, 2 * step)
            s_second, w_second = block_weights(scores, mask, run_wide, run_tall, 2 * step + 1)
            dy = dy_ref[here, part]
            d_weights = dot(dy, both_heads(xp_ref[here, part]), ((1,), (1,)))
            dxp_ref[here, part] = dot(
                jnp.concatenate([w_first, w_second], axis=0), both_heads(dy), ((0,), (0,))
            )
            return (
                d_scores + d_weights[:, 0:STRETCH] * s_first + d_weights[:, STRETCH:] * s_second
            )

        d_scores = lax.fori_loop(
            0, channels // PAIR, pair, jnp.zeros((STRETCH, STRETCH), f32), unroll=UNROLL
        ).astype(bf16)
        dbc_ref[here, 0:NSTATE] = dot(d_scores, c_now, ((0,), (0,)))
        dbc_ref[here, NSTATE:] = d_c + dot(d_scores, b_now)


def conv_backward(d_ext, live, weight_ref, slope_ref, d_ref, x_ref, halo_ref, grad_ref, tail_ref,
                  pack_ref, rows, part):
    sums = None
    total = None
    for first in range(0, rows, STRETCH):
        here = slice(first, first + STRETCH)
        d_total = d_ref[here, part] * slope_ref[here, part]
        d_ext[PAD + first : PAD + first + STRETCH, part] = d_total
        now = jnp.sum(d_total, axis=0, keepdims=True)
        total = now if total is None else total + now
    pack_ref[CONV : CONV + 1, part] = total
    for first, count in [(-PAD, PAD)] + [(at, STRETCH) for at in range(0, rows, STRETCH)]:
        begin = PAD + first
        pieces = [d_ext[begin : begin + count, part]]
        for lag in range(1, CONV):
            moved = slice(begin + lag, begin + lag + count)
            pieces.append(d_ext[moved, part] * live[lag - 1, moved, :])
        grad = weight_ref[0:1, part] * pieces[0]
        for lag in range(1, CONV):
            grad = grad + weight_ref[lag : lag + 1, part] * pieces[lag]
        if first < 0:
            pack_ref[BACK : BACK + HALO, part] = grad[PAD - HALO :]
            seen = halo_ref[:, part]
            pieces = [piece[PAD - HALO :] for piece in pieces]
        else:
            grad_ref[first : first + count, part] = grad.astype(bf16)
            if first + count == rows:
                tail_ref[:, part] = grad[count - HALO :]
            seen = x_ref[first : first + count, part].astype(f32)
        now = [jnp.sum(seen * piece, axis=0, keepdims=True) for piece in pieces]
        sums = now if sums is None else [old + new for old, new in zip(sums, now)]
    for row, value in enumerate(sums):
        pack_ref[row : row + 1, part] = value


def finish_backward(
    later_early, later_last, aloc_ref, early_ref, last_ref, sloc_ref, keep_ref, dxp_ref, dbc_ref,
    drun_ref, xp_ref, dy_ref, skip_ref, bcc_ref, run_ref, dt_ref, flags_ref, sx_ref, sbc_ref,
    x_ref, xh_ref, bc_ref, bch_ref, wx_ref, wb_ref, alog_ref, dtb_ref, dtr_ref, chan_ref,
    gx_ref, xtail_ref, xpack_ref, gbc_ref, bctail_ref, bcpack_ref, gdt_ref,
    clear, live, dx_ext, dbc_ext, d_x, d_bc, dt_wide, end_wide, ends, skip_wide, *, group,
):
    rows, channels = xp_ref.shape
    heads = run_ref.shape[0]
    blocks = rows // STRETCH
    prior_ref = (early_ref, last_ref)
    fill_live(flags_ref, clear, live)
    live[:, PAD + rows :, :] = jnp.zeros((HALO, PAD, STRETCH), f32)
    live[:, 0:PAD, :] = jnp.zeros((HALO, PAD, STRETCH), f32)
    for ext in (dx_ext, dbc_ext):
        ext[0:PAD, :] = jnp.zeros((PAD, ext.shape[1]), f32)
        ext[PAD + rows :, :] = jnp.zeros((PAD, ext.shape[1]), f32)
    skip_wide[0:1, :] = over_channels(to_column(skip_ref[...], group * heads, heads))
    rate = to_column(jnp.exp(alog_ref[...]), group * heads, heads)
    dt_bias = to_column(dtb_ref[...], group * heads, heads)
    d_alog = jnp.zeros((heads, 1), f32)
    d_dtb = jnp.zeros((heads, 1), f32)
    for block in range(blocks):
        here = slice(block * STRETCH, (block + 1) * STRETCH)
        seen = resets_seen(flags_ref[:, here])
        running = run_ref[:, here]
        dt = dt_ref[:, here]
        dt_wide[...] = spread_heads(dt, HEAD_DIM)
        end_wide[...] = spread_heads(to_end_factor(running, seen), HEAD_DIM)
        b_now = bcc_ref[here, 0:NSTATE]

        def chunk(step, carry):
            d_b, per_step = carry
            part = lanes(step, CHUNK)
            later = later_early[:, part] + later_last[:, part]
            if block < blocks - 1:
                whole = keep_ref[block + 1 : block + 2, part]
                for place in range(block + 2, blocks):
                    whole = whole * keep_ref[place : place + 1, part]
                later = (aloc_ref[block, :, part].astype(f32) + whole * later.astype(f32)).astype(bf16)
            state = block_state(block, prior_ref, sloc_ref, keep_ref, part)
            d_keep = jnp.sum(later.astype(f32) * state.astype(f32), axis=0, keepdims=True)
            stepped = xp_ref[here, part].astype(f32)
            end = end_wide[:, part]
            d_end = dot(b_now, later) * end
            d_stepped = dxp_ref[here, part] + d_end
            ended = stepped * end
            ends[0:1, part] = (
                jnp.sum(stepped * d_end, axis=0, keepdims=True)
                + d_keep * keep_ref[block : block + 1, part]
            )
            d_x[here, part] = d_stepped * dt_wide[:, part] + skip_wide[0:1, part] * dy_ref[
                here, part
            ].astype(f32)
            return (
                d_b + dot(ended.astype(bf16), later, ((1,), (1,))),
                per_step + head_sums(stepped * d_stepped, step * CHUNK, heads),
            )

        d_b, per_step = lax.fori_loop(
            0,
            channels // CHUNK,
            chunk,
            (jnp.zeros((STRETCH, NSTATE), f32), jnp.zeros((heads, STRETCH), f32)),
            unroll=UNROLL,
        )
        d_bc[here, 0:NSTATE] = dbc_ref[here, 0:NSTATE] + d_b
        d_bc[here, NSTATE:] = dbc_ref[here, NSTATE:]
        at_end = head_sums(jnp.broadcast_to(ends[0:1, :], (STRETCH, channels)), 0, heads)
        is_last = iota((heads, STRETCH), 1) == STRETCH - 1
        d_run = drun_ref[:, here] - per_step + jnp.where(is_last, at_end, 0.0)
        shape = (STRETCH, STRETCH)
        d_log = dot_full(d_run, (iota(shape, 0) >= iota(shape, 1)).astype(f32))
        d_dt = per_step / dt - rate * d_log
        raw = dtr_ref[:, here].astype(f32) + dt_bias
        d_raw = d_dt / (1.0 + jnp.exp(-raw))
        gdt_ref[:, here] = d_raw
        d_alog = d_alog - jnp.sum(d_log * dt, axis=1, keepdims=True) * rate
        d_dtb = d_dtb + jnp.sum(d_raw, axis=1, keepdims=True)
    xpack_ref[GAIN : SKIP + 1, :] = chan_ref[0:2, :]
    bcpack_ref[GAIN : SKIP + 1, :] = jnp.zeros((2, bcpack_ref.shape[1]), f32)
    for place, column in enumerate((d_alog, d_dtb)):
        shape = (heads, STRETCH)
        pick = iota(shape, 1) == iota(shape, 0) + group * heads
        row = jnp.sum(jnp.where(pick, jnp.broadcast_to(column, shape), 0.0), axis=0, keepdims=True)
        bcpack_ref[GAIN : GAIN + 1, place * STRETCH : (place + 1) * STRETCH] = row

    def conv_chunk(step, carry):
        conv_backward(
            dx_ext, live, wx_ref, sx_ref, d_x, x_ref, xh_ref, gx_ref, xtail_ref, xpack_ref, rows,
            lanes(step, STRETCH),
        )
        return carry

    lax.fori_loop(0, channels // STRETCH, conv_chunk, 0, unroll=UNROLL)
    for step in range(2):
        conv_backward(
            dbc_ext, live, wb_ref, sbc_ref, d_bc, bc_ref, bch_ref, gbc_ref, bctail_ref, bcpack_ref,
            rows, slice(step * NSTATE, (step + 1) * NSTATE),
        )


def final_sums(mine_ref, pick_ref, flags_ref, *refs, arrivals, groups, scale):
    arrived, tails_x, tails_bc = refs[:arrivals], refs[arrivals], refs[arrivals + 1]
    out_wx, out_bx, out_wb, out_alog, out_dtb, out_skip, out_gain, ending_ref = refs[arrivals + 2 :]
    inner = tails_x.shape[1]
    total = mine_ref[0:BACK, :]
    back = jnp.zeros((HALO, total.shape[1]), f32)
    for place, ref in enumerate(arrived):
        value = ref[...].astype(f32)
        total = total + value[0:BACK]
        back = back + value[BACK:PACKED] * pick_ref[place : place + 1, 0:1]
    total = total * scale
    back = back * tail_factors(flags_ref)
    ending_ref[:, 0:inner] = (tails_x[...] + back[:, 0:inner]).astype(bf16)
    ending_ref[:, inner:] = (tails_bc[...] + back[:, inner:]).astype(bf16)
    out_wx[...] = total[0:CONV, 0:inner]
    out_bx[...] = total[CONV : CONV + 1, 0:inner]
    out_wb[...] = total[0 : CONV + 1, inner:]
    out_gain[...] = total[GAIN : GAIN + 1, 0:inner]
    heads = out_skip.shape[1]
    for out, shift in ((out_alog, 0), (out_dtb, STRETCH)):
        row = None
        for group in range(groups):
            first = inner + 2 * group * NSTATE + shift
            piece = total[GAIN : GAIN + 1, first : first + STRETCH]
            row = piece if row is None else row + piece
        out[...] = row[:, 0:heads]
    lane_sums = jnp.broadcast_to(total[SKIP : SKIP + 1, 0:inner], (PAD, inner))
    shape = (heads, inner)
    pick = (iota(shape, 1) // HEAD_DIM == iota(shape, 0)).astype(f32).astype(bf16)
    high = lane_sums.astype(bf16)
    low = (lane_sums - high.astype(f32)).astype(bf16)
    last = ((1,), (1,))
    out_skip[...] = (dot(high, pick, last) + dot(low, pick, last))[0:1]


def call(kernel, operands, outs, scratch, flops, name, blocked=False):
    cuts = [cut or {} for _, cut in operands]
    arrays = [array for array, _ in operands]
    shapes = [jax.ShapeDtypeStruct(shape, dtype) for shape, dtype in outs]

    def body(*refs):
        seen = []
        for ref, cut in zip(refs, cuts):
            if cut:
                ref = ref.at[tuple(cut.get(dim, slice(None)) for dim in range(len(ref.shape)))]
            seen.append(ref)
        kernel(*seen, *refs[len(cuts) :])

    def block_of(array, cut):
        shape, index = [], []
        for dim, extent in enumerate(array.shape):
            part = cut.get(dim, slice(0, extent))
            size = part.stop - part.start
            shape.append(size)
            index.append(part.start // size)
        return pl.BlockSpec(tuple(shape), functools.partial(lambda fixed, i: fixed, tuple(index)))

    in_vmem = pl.BlockSpec(memory_space=pltpu.VMEM)
    if blocked:
        grid, limit = {"grid": (1,)}, BLOCKED_LIMIT
        in_specs = [block_of(array, cut) for array, cut in zip(arrays, cuts)]
        out_specs = [block_of(shape, {}) for shape in shapes]
    else:
        grid, limit = {}, VMEM_LIMIT
        in_specs, out_specs = [in_vmem] * len(arrays), [in_vmem] * len(shapes)
    count = sum(each.size * each.dtype.itemsize for each in arrays + shapes)
    return pl.pallas_call(
        kernel if blocked else body,
        in_specs=in_specs,
        out_specs=out_specs,
        out_shape=shapes,
        scratch_shapes=[pltpu.VMEM(shape, f32) for shape in scratch],
        compiler_params=pltpu.CompilerParams(vmem_limit_bytes=limit),
        cost_estimate=pl.CostEstimate(flops=flops, bytes_accessed=count, transcendentals=0),
        name=name,
        **grid,
    )(*arrays)


def together(*values):
    return lax.optimization_barrier(values)


def chain(parts, decays, axis, backward, fillers):
    count = lax.axis_size(axis)
    zero = [jnp.zeros(part.shape, bf16) for part in parts]
    early, last = list(zero), list(zero)
    results = []
    for hop in range(count - 1):
        pairs = [(count - 1 - hop, count - 2 - hop)] if backward else [(hop, hop + 1)]
        leaving = list(parts)
        if hop > 0:
            for place, part in enumerate(parts):
                early[place] = early[place] + last[place] if hop > 1 else last[place]
                arrived = early[place].astype(f32)
                leaving[place] = (decays[place] * arrived + part.astype(f32)).astype(bf16)
        if hop < len(fillers):
            work, array = fillers[hop]
            array = together(array, *leaving)[0]
        last = [lax.ppermute(each, axis, pairs) for each in leaving]
        if hop < len(fillers):
            done = work(array)
            last[0], *done = together(last[0], *done)
            results.append(done)
    for work, array in fillers[len(results) :]:
        results.append(work(array))
    return list(zip(early, last)), results


def exchange_sum(value, axis):
    count = lax.axis_size(axis)
    stride = 1
    while stride < count:
        value = value + lax.ppermute(value, axis, [(i, i ^ stride) for i in range(count)])
        stride *= 2
    return value


def per_device(
    x_raw, bc_raw, z_gate, dt_raw, resets, conv_x_weight, conv_x_bias, conv_bc_weight,
    conv_bc_bias, a_log, dt_bias, skip_weight, norm_gain, grad_out,
):
    rows, inner = x_raw.shape[1:]
    groups = bc_raw.shape[3] // NSTATE
    heads = a_log.shape[0] // groups
    channels = inner // groups
    blocks = rows // STRETCH
    width = 2 * NSTATE

    def by_group(value):
        lead = value.shape[:-2]
        split = value.reshape(lead + (2, groups, NSTATE))
        return jnp.moveaxis(split, -3, -2).reshape(lead + (groups * width,))

    x_own, z_own, go_own, dt_own = x_raw[0], z_gate[0], grad_out[0], dt_raw[0]
    bc_own = by_group(bc_raw[0])
    flags = resets
    count = lax.axis_size("ctx")
    sent = call(
        tails,
        [
            (x_raw, {1: slice(rows - 16, rows)}),
            (bc_raw, {1: slice(rows - 16, rows)}),
            (flags, {1: slice(rows - STRETCH, rows)}),
        ],
        [((HALO, inner + groups * width), f32)],
        [],
        rows,
        "tails",
        True,
    )[0]
    halo = lax.ppermute(sent, "ctx", [(i, i + 1) for i in range(count - 1)])
    alog_row, dtb_row, skip_row = a_log[None], dt_bias[None], skip_weight[None]
    bx, gain = conv_x_bias[None], norm_gain[None]
    wb, bb = by_group(conv_bc_weight), by_group(conv_bc_bias)[None]

    def wide(array, group):
        return (array, {1: slice(group * channels, (group + 1) * channels)})

    def narrow(array, group, first=0):
        return (array, {1: slice(first + group * width, first + (group + 1) * width)})

    def per_head(array, group):
        return (array, {0: slice(group * heads, (group + 1) * heads)})

    def whole(array):
        return (array, None)

    keep_rows = -(-(blocks + 1) // PAD) * PAD
    tall, thin, row_shape = (rows, channels), (rows, width), (heads, rows)
    state_shape = (NSTATE, channels)
    local_shape = (blocks - 1, NSTATE, channels)
    clear_shape, live_shape = (rows + PAD, STRETCH), (HALO, rows + 2 * PAD, STRETCH)
    wide_scratch = (STRETCH, channels)
    run_scratch = [(STRETCH, heads * STRETCH), (heads * PAD, STRETCH)]
    work = rows * channels * STRETCH
    group_range = range(groups)
    held = []
    for g in group_range:
        held.append(
            call(
                functools.partial(conv_and_state, group=g),
                [
                    wide(x_own, g), wide(halo, g), narrow(bc_own, g), narrow(halo, g, inner),
                    wide(conv_x_weight, g), wide(bx, g), narrow(wb, g), narrow(bb, g),
                    per_head(dt_own, g), whole(dtb_row), whole(alog_row), whole(flags),
                ],
                [
                    (tall, bf16), (tall, bf16), (tall, f32), (thin, bf16), (thin, f32),
                    (row_shape, f32), (row_shape, f32), ((keep_rows, channels), f32),
                    (state_shape, bf16), (local_shape, bf16),
                ],
                [
                    (rows + PAD, channels), (rows + PAD, width), clear_shape, live_shape,
                    wide_scratch, wide_scratch, state_shape,
                ],
                2 * work,
                "conv_and_state",
            )
        )
    xc, xp, ux, bcc, ubc, dt, run, keep, s_dev, s_loc = zip(*held)
    decay = [k[blocks : blocks + 1] for k in keep]

    def forward_work(g):
        return lambda bcc_now: call(
            within_blocks,
            [
                whole(xp[g]), whole(bcc_now), whole(run[g]), whole(flags), whole(ux[g]), whole(ubc[g]),
            ],
            [(tall, f32), (tall, f32), (thin, f32)],
            run_scratch,
            6 * work,
            "within_blocks",
        )

    prior, held = chain(
        s_dev, decay, "ctx", False, [(forward_work(g), bcc[g]) for g in group_range]
    )
    y_within, slope_x, slope_bc = zip(*held)
    held = [
        call(
            functools.partial(gate_forward, group=g),
            [
                whole(y_within[g]), whole(prior[g][0]), whole(prior[g][1]), whole(s_loc[g]),
                whole(keep[g]), whole(bcc[g]), whole(run[g]), whole(flags), whole(xc[g]),
                whole(skip_row), wide(z_own, g), wide(go_own, g), wide(gain, g),
            ],
            [(tall, f32), (tall, bf16), ((PAD, rows), f32)],
            [wide_scratch, (PAD, channels)],
            2 * work,
            "gate_forward",
        )
        for g in group_range
    ]
    y_ssd, mixed, sums = zip(*held)
    totals = exchange_sum(sum(sums[1:], sums[0]), "head")
    held = [
        call(
            gate_backward,
            [
                whole(totals), whole(mixed[g]), wide(z_own, g), wide(go_own, g), wide(gain, g),
                whole(keep[g]), whole(bcc[g]), whole(run[g]), whole(flags),
            ],
            [(tall, bf16), (state_shape, bf16), (local_shape, bf16)],
            [wide_scratch, state_shape],
            2 * work,
            "gate_backward",
        )
        for g in group_range
    ]
    dy, a_dev, a_loc = zip(*held)

    def backward_work(g):
        return lambda bcc_now: call(
            within_backward,
            [
                whole(totals), whole(mixed[g]), wide(z_own, g), wide(go_own, g), wide(gain, g),
                whole(dy[g]), whole(y_ssd[g]), whole(xc[g]), whole(xp[g]), whole(bcc_now),
                whole(run[g]), whole(flags), whole(prior[g][0]), whole(prior[g][1]), whole(s_loc[g]),
                whole(keep[g]),
            ],
            [
                (tall, bf16), (tall, f32), (thin, f32), (row_shape, f32), ((PAD, channels), f32),
            ],
            run_scratch + [wide_scratch],
            10 * work,
            "within_backward",
            True,
        )

    later, held = chain(
        a_dev, decay, "ctx", True, [(backward_work(g), bcc[g]) for g in group_range]
    )
    gz, dxp, dbc, drun, chan = zip(*held)
    held = [
        call(
            functools.partial(finish_backward, group=g),
            [
                whole(later[g][0]), whole(later[g][1]), whole(a_loc[g]), whole(prior[g][0]),
                whole(prior[g][1]), whole(s_loc[g]), whole(keep[g]), whole(dxp[g]), whole(dbc[g]),
                whole(drun[g]), whole(xp[g]), whole(dy[g]), whole(skip_row), whole(bcc[g]),
                whole(run[g]), whole(dt[g]), whole(flags), whole(slope_x[g]), whole(slope_bc[g]),
                wide(x_own, g), wide(halo, g), narrow(bc_own, g), narrow(halo, g, inner),
                wide(conv_x_weight, g), narrow(wb, g), whole(alog_row), whole(dtb_row),
                per_head(dt_own, g), whole(chan[g]),
            ],
            [
                (tall, bf16), ((HALO, channels), f32), ((PACKED, channels), f32), (thin, bf16),
                ((HALO, width), f32), ((PACKED, width), f32), (row_shape, f32),
            ],
            [
                clear_shape, live_shape, (rows + 2 * PAD, channels), (rows + 2 * PAD, width), tall,
                thin, wide_scratch, wide_scratch, (PAD, channels), (PAD, channels),
            ],
            4 * work,
            "finish_backward",
            True,
        )
        for g in group_range
    ]
    gx, x_tail, x_pack, gbc, bc_tail, bc_pack, gdt = zip(*held)

    def joined(pieces):
        return jnp.concatenate(pieces, axis=1)

    def ungroup(value):
        lead = value.shape[:-1]
        split = value.reshape(lead + (groups, 2, NSTATE))
        return jnp.moveaxis(split, -3, -2).reshape(lead + (2, groups * NSTATE))

    packed = joined(x_pack + bc_pack)
    mine = packed
    for shift in range(1, lax.axis_size("dp")):
        size = lax.axis_size("dp")
        other = lax.ppermute(packed, "dp", [(i, (i + shift) % size) for i in range(size)])
        mine = jnp.where(jnp.arange(PACKED)[:, None] < BACK, mine + other, mine)
    leaving = mine.astype(bf16)
    here = lax.axis_index("ctx")
    arrived, picks = [], []
    for shift in range(1, count):
        arrived.append(lax.ppermute(leaving, "ctx", [(i, i ^ shift) for i in range(count)]))
        picks.append((here ^ shift) == here + 1)
    pick = jnp.broadcast_to(jnp.stack(picks).astype(f32)[:, None], (count - 1, STRETCH))
    out_wx, out_bx, out_wb, out_alog, out_dtb, out_skip, out_gain, ending = call(
        functools.partial(
            final_sums,
            arrivals=count - 1,
            groups=groups,
            scale=float(lax.axis_size("dp") * count * rows) ** (-0.5),
        ),
        [whole(mine), whole(pick), whole(flags)]
        + [whole(each) for each in arrived]
        + [whole(joined(x_tail)), whole(joined(bc_tail))],
        [
            ((CONV, inner), f32), ((1, inner), f32), ((CONV + 1, groups * width), f32),
            ((1, groups * heads), f32), ((1, groups * heads), f32), ((1, groups * heads), f32),
            ((1, inner), f32), ((HALO, inner + groups * width), bf16),
        ],
        [],
        rows * inner,
        "final_sums",
    )
    grad_x = lax.dynamic_update_slice(joined(gx), ending[:, :inner], (rows - HALO, 0))
    grad_bc = lax.dynamic_update_slice(
        ungroup(joined(gbc)), ungroup(ending[:, inner:]), (rows - HALO, 0, 0)
    )
    bc_terms = ungroup(out_wb)
    return (
        grad_x[None],
        grad_bc[None],
        joined(gz)[None],
        jnp.concatenate(gdt, axis=0)[None],
        out_wx,
        out_bx[0],
        bc_terms[:CONV],
        bc_terms[CONV],
        out_alog[0],
        out_dtb[0],
        out_skip[0],
        out_gain[0],
    )


def solution(mesh):
    return jax.shard_map(
        per_device,
        mesh=mesh,
        in_specs=(
            P("dp", "ctx", "head"),
            P("dp", "ctx", None, "head"),
            P("dp", "ctx", "head"),
            P("dp", "head", "ctx"),
            P("dp", "ctx"),
            P(None, "head"),
            P("head"),
            P(None, None, "head"),
            P(None, "head"),
            P("head"),
            P("head"),
            P("head"),
            P("head"),
            P("dp", "ctx", "head"),
        ),
        out_specs=(
            P("dp", "ctx", "head"),
            P("dp", "ctx", None, "head"),
            P("dp", "ctx", "head"),
            P("dp", "head", "ctx"),
            P(None, "head"),
            P("head"),
            P(None, None, "head"),
            P(None, "head"),
            P("head"),
            P("head"),
            P("head"),
            P("head"),
        ),
        check_vma=False,
    )
```

```python
import functools

import jax
import jax.numpy as jnp
from jax import lax
from jax.experimental import pallas as pl
from jax.experimental.pallas import tpu as pltpu
from jax.sharding import PartitionSpec as P

HEAD_DIM = 64
NSTATE = 128
CONV = 4
STRETCH = 128
INNER = 8192
HALO = CONV - 1
PAD = 8
CHUNK = 256
PAIR = 2 * HEAD_DIM
NORM_EPS = 1e-05
LOWEST = -1e30
GAIN, SKIP, BACK = CONV + 1, CONV + 2, CONV + 3
PACKED = BACK + HALO
A_LOG, DT_BIAS, SKIP_WEIGHT = range(3)
STAGES = 2
STREAM_LIMIT = 62 * 1024 * 1024
BLOCKED_LIMIT = 40 * 1024 * 1024
VMEM_LIMIT = 24 * 1024 * 1024
UNROLL = 2

f32 = jnp.float32
bf16 = jnp.bfloat16


def dot(a, b, contract=((1,), (0,))):
    return lax.dot_general(a, b, (contract, ((), ())), preferred_element_type=f32)


def dot_full(a, b):
    return lax.dot_general(
        a, b, (((1,), (0,)), ((), ())), precision=lax.Precision.HIGHEST, preferred_element_type=f32
    )


def iota(shape, dim):
    return lax.broadcasted_iota(jnp.int32, shape, dim)


def split3(value):
    high = value.astype(bf16)
    rest = value - high.astype(f32)
    middle = rest.astype(bf16)
    low = (rest - middle.astype(f32)).astype(bf16)
    return jnp.concatenate([high, middle, low], axis=0)


def spread_heads(rows, width):
    heads = rows.shape[0]
    shape = (heads, heads * width)
    pick = (iota(shape, 1) // width == iota(shape, 0)).astype(f32).astype(bf16)
    return dot(split3(rows), jnp.concatenate([pick] * 3, axis=0), ((0,), (0,)))


def head_sums(value, first, heads):
    shape = (heads, value.shape[1])
    pick = ((iota(shape, 1) + first) // HEAD_DIM == iota(shape, 0)).astype(f32).astype(bf16)
    high = value.astype(bf16)
    low = (value - high.astype(f32)).astype(bf16)
    last = ((1,), (1,))
    return dot(pick, high, last) + dot(pick, low, last)


def as_columns(row):
    return jnp.transpose(jnp.broadcast_to(row, (STRETCH, STRETCH)))


def sigmoid(value):
    return 0.5 * jnp.tanh(0.5 * value) + 0.5


def upper_ones():
    shape = (STRETCH, STRETCH)
    return (iota(shape, 0) <= iota(shape, 1)).astype(f32)


def resets_seen(flags_row):
    flags = jnp.broadcast_to(flags_row.astype(f32), (PAD, STRETCH)).astype(bf16)
    return dot(flags, upper_ones().astype(bf16))[0:1]


def decay_mask(seen):
    shape = (STRETCH, STRETCH)
    same = (as_columns(seen) == jnp.broadcast_to(seen, shape)) & (iota(shape, 0) >= iota(shape, 1))
    return jnp.where(same, 0.0, LOWEST)


def lanes(position, size):
    return pl.ds(pl.multiple_of(position * size, size), size)


def to_column(row, first, heads):
    shape = (heads, row.shape[1])
    pick = iota(shape, 1) == iota(shape, 0) + first
    return jnp.sum(jnp.where(pick, jnp.broadcast_to(row, shape), 0.0), axis=1, keepdims=True)


def over_channels(column):
    return spread_heads(jnp.broadcast_to(column, (column.shape[0], STRETCH)), HEAD_DIM)[0:1]


def softplus(value):
    small = jnp.exp(-jnp.abs(value))
    series = small * (1.0 - small * (1 / 2 - small * (1 / 3 - small * (1 / 4 - small * (1 / 5)))))
    return jnp.maximum(value, 0.0) + jnp.where(small < 0.03, series, jnp.log(1.0 + small))


def head_column(rows_ref, which, group, heads):
    return to_column(rows_ref[which : which + 1, :], group * heads, heads)


def step_sizes(dtr_ref, rows_ref, group):
    heads = dtr_ref.shape[0]
    return softplus(dtr_ref[...].astype(f32) + head_column(rows_ref, DT_BIAS, group, heads))


def to_end_factor(running, seen):
    final = running[:, STRETCH - 1 : STRETCH]
    return jnp.where(seen == seen[:, STRETCH - 1 : STRETCH], jnp.exp(final - running), 0.0)


def doubled(value):
    return jnp.concatenate([value, value], axis=1)


def fill_live(flags_ref, clear, live):
    rows = flags_ref.shape[1]
    clear[0:PAD, :] = jnp.ones((PAD, STRETCH), f32)
    for first in range(0, rows, STRETCH):
        flags = flags_ref[:, first : first + STRETCH].astype(f32)
        clear[PAD + first : PAD + first + STRETCH, :] = as_columns(1.0 - flags)
    for first in range(0, rows, STRETCH):
        begin = PAD + first
        product = clear[begin : begin + STRETCH, :]
        live[0, begin : begin + STRETCH, :] = product
        for lag in range(2, CONV):
            product = product * clear[begin - lag + 1 : begin - lag + 1 + STRETCH, :]
            live[lag - 1, begin : begin + STRETCH, :] = product


def fill_extended(extended, halo_ref, rows_ref):
    extended[PAD - HALO : PAD, :] = halo_ref[...]
    extended[PAD:, :] = rows_ref[...].astype(f32)


def conv_total(extended, live, weight_ref, bias_ref, first, part):
    begin = PAD + first
    total = bias_ref[0:1, part] + weight_ref[0:1, part] * extended[begin : begin + STRETCH, part]
    width = total.shape[1] // STRETCH
    for lag in range(1, CONV):
        mask = jnp.concatenate([live[lag - 1, begin : begin + STRETCH, :]] * width, axis=1)
        total = total + weight_ref[lag : lag + 1, part] * (
            extended[begin - lag : begin - lag + STRETCH, part] * mask
        )
    return total


def tail_factors(flags_ref):
    flags = flags_ref[:, flags_ref.shape[1] - STRETCH :].astype(f32)
    clear = as_columns(1.0 - flags)
    last = clear[STRETCH - 1 :]
    both = last * clear[STRETCH - 2 : STRETCH - 1]
    return jnp.concatenate([both, last, jnp.ones_like(last)], axis=0)[:, 0:1]


def tails(x_ref, bc_ref, flags_ref, out_ref, *, ready):
    ready(0)
    keep = tail_factors(flags_ref)
    inner = x_ref.shape[2]
    out_ref[:, 0:inner] = x_ref[0].astype(f32)[x_ref.shape[1] - HALO :] * keep
    groups = bc_ref.shape[3] // NSTATE
    for which in range(2):
        rows = bc_ref[0, :, which, :].astype(f32)[bc_ref.shape[1] - HALO :] * keep
        for group in range(groups):
            first = inner + (2 * group + which) * NSTATE
            out_ref[:, first : first + NSTATE] = rows[:, group * NSTATE : (group + 1) * NSTATE]


def conv_and_state(
    x_ref, xh_ref, bc_ref, bch_ref, wx_ref, bx_ref, wb_ref, bb_ref, dtr_ref, rows_ref,
    flags_ref, xc_ref, xp_ref, ux_ref, bcc_ref, ubc_ref, dt_ref, run_ref, keep_ref, sdev_ref,
    sloc_ref, x_ext, bc_ext, clear, live, dt_wide, end_wide, state, *, group,
):
    rows, channels = x_ref.shape
    heads = dtr_ref.shape[0]
    fill_extended(x_ext, xh_ref, x_ref)
    fill_extended(bc_ext, bch_ref, bc_ref)
    fill_live(flags_ref, clear, live)
    blocks = rows // STRETCH
    rate = jnp.exp(head_column(rows_ref, A_LOG, group, heads))
    dt_ref[...] = step_sizes(dtr_ref, rows_ref, group)
    product = None
    for block in range(blocks):
        first = block * STRETCH
        here = slice(first, first + STRETCH)
        every = slice(None)
        total = conv_total(bc_ext, live, wb_ref, bb_ref, first, every)
        ubc_ref[here, :] = total
        bc_now = (total * sigmoid(total)).astype(bf16)
        bcc_ref[here, :] = bc_now
        b_turned = jnp.transpose(bc_now[:, 0:NSTATE].astype(f32)).astype(bf16)
        seen = resets_seen(flags_ref[:, here])
        dt = dt_ref[:, here]
        running = dot_full(-rate * dt, upper_ones())
        run_ref[:, here] = running
        final = running[:, STRETCH - 1 : STRETCH]
        keep = jnp.where(seen[:, STRETCH - 1 : STRETCH] == 0.0, jnp.exp(final), 0.0)
        keep_row = over_channels(keep)
        keep_ref[block : block + 1, :] = keep_row
        product = keep_row if product is None else product * keep_row
        dt_wide[...] = spread_heads(dt, HEAD_DIM)
        end_wide[...] = spread_heads(to_end_factor(running, seen), HEAD_DIM)

        def chunk(step, carry):
            part = lanes(step, CHUNK)
            total = conv_total(x_ext, live, wx_ref, bx_ref, first, part)
            ux_ref[here, part] = total
            xc = (total * sigmoid(total)).astype(bf16)
            xc_ref[here, part] = xc
            stepped = (xc.astype(f32) * dt_wide[:, part]).astype(bf16)
            xp_ref[here, part] = stepped
            ended = (stepped.astype(f32) * end_wide[:, part]).astype(bf16)
            fresh = dot(b_turned, ended)
            if block > 0:
                fresh = keep_ref[block : block + 1, part] * state[:, part] + fresh
            if block < blocks - 1:
                state[:, part] = fresh
                sloc_ref[block, :, part] = fresh.astype(bf16)
            else:
                sdev_ref[:, part] = fresh.astype(bf16)
            return carry

        lax.fori_loop(0, channels // CHUNK, chunk, 0, unroll=UNROLL)
    keep_ref[blocks : blocks + 1, :] = product


def place_runs(run_ref, here, run_wide, run_tall):
    running = run_ref[:, here]
    run_wide[...] = spread_heads(running, STRETCH)
    for head in range(running.shape[0]):
        run_tall[head * PAD : (head + 1) * PAD, :] = jnp.broadcast_to(
            running[head : head + 1], (PAD, STRETCH)
        )


def block_weights(scores, mask, run_wide, run_tall, head):
    column = run_wide[:, lanes(head, STRETCH)]
    row = run_tall[pl.ds(pl.multiple_of(head * PAD, PAD), PAD), :][0:1]
    segment = jnp.exp(column - row + mask)
    return segment, (scores * segment).astype(bf16)


def both_heads(value):
    is_first = iota(value.shape, 1) < HEAD_DIM
    wide = value.astype(f32)
    zero = jnp.zeros_like(wide)
    return jnp.concatenate(
        [jnp.where(is_first, wide, zero).astype(bf16), jnp.where(is_first, zero, wide).astype(bf16)],
        axis=0,
    )


def slope_of(total):
    up = sigmoid(total)
    return up + total * up * (1.0 - up)


def within_blocks(
    xp_ref, bcc_ref, run_ref, flags_ref, ux_ref, ubc_ref, y_ref, sx_ref, sbc_ref, run_wide, run_tall
):
    rows, channels = xp_ref.shape
    for block in range(rows // STRETCH):
        here = slice(block * STRETCH, (block + 1) * STRETCH)
        mask = decay_mask(resets_seen(flags_ref[:, here]))
        scores = dot(bcc_ref[here, NSTATE:], bcc_ref[here, 0:NSTATE], ((1,), (1,)))
        place_runs(run_ref, here, run_wide, run_tall)
        sbc_ref[here, :] = slope_of(ubc_ref[here, :])

        def pair(step, carry):
            _, w_first = block_weights(scores, mask, run_wide, run_tall, 2 * step)
            _, w_second = block_weights(scores, mask, run_wide, run_tall, 2 * step + 1)
            part = lanes(step, PAIR)
            y_ref[here, part] = dot(
                jnp.concatenate([w_first, w_second], axis=1), both_heads(xp_ref[here, part])
            )
            sx_ref[here, part] = slope_of(ux_ref[here, part])
            return carry

        lax.fori_loop(0, channels // PAIR, pair, 0, unroll=UNROLL)


def start_factor(run_ref, flags_ref, here):
    seen = resets_seen(flags_ref[:, here])
    return jnp.where(seen == 0.0, jnp.exp(run_ref[:, here]), 0.0)


def block_state(block, prior_ref, sloc_ref, keep_ref, part):
    state = prior_ref[0][:, part] + prior_ref[1][:, part]
    if block == 0:
        return state
    whole = keep_ref[0:1, part]
    for step in range(1, block):
        whole = whole * keep_ref[step : step + 1, part]
    return (whole * state.astype(f32) + sloc_ref[block - 1, :, part].astype(f32)).astype(bf16)


def bundle_rows(rows):
    places = [rows]
    for size in (PAD, PAD, 2 * PAD, NSTATE // 4):
        places.append(places[-1] + size)
    return places


def gate_forward(
    y_ref, early_ref, last_ref, sloc_ref, keep_ref, bcc_ref, run_ref, flags_ref, xc_ref, rows_ref,
    z_ref, go_ref, gain_ref, *refs, group,
):
    *before, bundle_ref, sums_ref, start_wide, skip_wide = refs
    rows, channels = xc_ref.shape
    heads = run_ref.shape[0]
    prior_ref = (early_ref, last_ref)
    at_keep, at_gain, at_start, at_turned, _ = bundle_rows(rows)
    bundle_ref[at_keep:at_gain, :] = keep_ref[0:PAD, :]
    bundle_ref[at_gain:at_start, :] = jnp.broadcast_to(gain_ref[...], (PAD, channels))
    skip_wide[0:1, :] = over_channels(head_column(rows_ref, SKIP_WEIGHT, group, heads))
    quarter = NSTATE // 4
    for block in range(rows // STRETCH):
        here = slice(block * STRETCH, (block + 1) * STRETCH)
        start = start_factor(run_ref, flags_ref, here)
        bundle_ref[at_start : at_start + heads, here] = start
        start_wide[...] = spread_heads(start, HEAD_DIM)
        c_now = bcc_ref[here, NSTATE:]
        turned = jnp.transpose(c_now.astype(f32))
        for turn in range(4):
            first = turn * rows + block * STRETCH
            bundle_ref[at_turned : at_turned + quarter, first : first + STRETCH] = turned[
                turn * quarter : (turn + 1) * quarter
            ]

        def chunk(step, carry):
            squares, products = carry
            part = lanes(step, CHUNK)
            carried = dot(c_now, block_state(block, prior_ref, sloc_ref, keep_ref, part))
            y_now = y_ref[here, part] + carried * start_wide[:, part]
            y_now = y_now + skip_wide[0:1, part] * xc_ref[here, part].astype(f32)
            bundle_ref[here, part] = y_now
            z = z_ref[here, part].astype(f32)
            gated = y_now.astype(bf16).astype(f32) * (z * sigmoid(z))
            gained = go_ref[here, part].astype(f32) * gain_ref[0:1, part]
            return squares + gated * gated, products + gated * gained

        zero = jnp.zeros((STRETCH, CHUNK), f32)
        squares, products = lax.fori_loop(
            0, channels // CHUNK, chunk, (zero, zero), unroll=UNROLL
        )
        square_column = jnp.sum(squares, axis=1, keepdims=True)
        product_column = jnp.sum(products, axis=1, keepdims=True)
        shape = (STRETCH, STRETCH)
        both = jnp.where(
            iota(shape, 1) == 0,
            jnp.broadcast_to(square_column, shape),
            jnp.broadcast_to(product_column, shape),
        )
        total = jnp.transpose(both)[0:2]
        for ref in before:
            total = total + ref[:, here]
        sums_ref[:, here] = total


def norm_factors(totals_ref, here):
    squares = totals_ref[0:1, here]
    products = totals_ref[1:2, here]
    inv_rms = lax.rsqrt(squares * (1.0 / INNER) + NORM_EPS)
    pull = inv_rms * inv_rms * inv_rms * products * (1.0 / INNER)
    return doubled(as_columns(inv_rms)), doubled(as_columns(pull))


def gate_backward(
    own_ref, other_ref, bundle_ref, z_ref, go_ref, dy_ref, adev_ref, aloc_ref, totals_ref,
    start_wide, adjoint, *, heads,
):
    rows, channels = z_ref.shape
    blocks = rows // STRETCH
    at_keep, at_gain, at_start, at_turned, end = bundle_rows(rows)
    totals_ref[...] = own_ref[...] + other_ref[...]
    for block in reversed(range(blocks)):
        here = slice(block * STRETCH, (block + 1) * STRETCH)
        start_wide[...] = spread_heads(bundle_ref[at_start : at_start + heads, here], HEAD_DIM)
        inv_rms, pull = norm_factors(totals_ref, here)
        firsts = [turn * rows + block * STRETCH for turn in range(4)]
        c_turned = jnp.concatenate(
            [bundle_ref[at_turned:end, first : first + STRETCH] for first in firsts], axis=0
        ).astype(bf16)

        def chunk(step, carry):
            part = lanes(step, CHUNK)
            z = z_ref[here, part].astype(f32)
            gate = z * sigmoid(z)
            gained = go_ref[here, part].astype(f32) * bundle_ref[at_gain : at_gain + 1, part]
            mixed = bundle_ref[here, part].astype(bf16).astype(f32)
            d_gated = gained * inv_rms - mixed * gate * pull
            dy = (d_gated * gate).astype(bf16)
            dy_ref[here, part] = dy
            fresh = dot(c_turned, (dy.astype(f32) * start_wide[:, part]).astype(bf16))
            if block < blocks - 1:
                keep = bundle_ref[at_keep + block : at_keep + block + 1, part]
                fresh = fresh + keep * adjoint[:, part]
            if block > 0:
                adjoint[:, part] = fresh
                aloc_ref[block - 1, :, part] = fresh.astype(bf16)
            else:
                adev_ref[:, part] = fresh.astype(bf16)
            return carry

        lax.fori_loop(0, channels // CHUNK, chunk, 0, unroll=UNROLL)


def within_backward(
    totals_ref, bundle_ref, z_ref, go_ref, dy_ref, xc_ref, xp_ref, bcc_ref,
    run_ref, flags_ref, early_ref, last_ref, sloc_ref, keep_ref, rows_ref,
    gz_ref, dxp_ref, dbc_ref, drun_ref, chan_ref, run_wide, run_tall, start_wide, skip_wide, *, group,
):
    rows, channels = xc_ref.shape
    heads = run_ref.shape[0]
    prior_ref = (early_ref, last_ref)
    at_gain = bundle_rows(rows)[1]
    skip_wide[0:1, :] = over_channels(head_column(rows_ref, SKIP_WEIGHT, group, heads))
    chan_ref[...] = jnp.zeros_like(chan_ref)
    for block in range(rows // STRETCH):
        here = slice(block * STRETCH, (block + 1) * STRETCH)
        mask = decay_mask(resets_seen(flags_ref[:, here]))
        b_now = bcc_ref[here, 0:NSTATE]
        c_now = bcc_ref[here, NSTATE:]
        scores = dot(c_now, b_now, ((1,), (1,)))
        place_runs(run_ref, here, run_wide, run_tall)
        start_wide[...] = spread_heads(start_factor(run_ref, flags_ref, here), HEAD_DIM)
        inv_rms, pull = norm_factors(totals_ref, here)

        def chunk(step, carry):
            d_c, d_run = carry
            part = lanes(step, CHUNK)
            z = z_ref[here, part].astype(f32)
            gate_up = sigmoid(z)
            gate = z * gate_up
            go = go_ref[here, part].astype(f32)
            xc = xc_ref[here, part].astype(f32)
            y_now = bundle_ref[here, part]
            y_ssd = y_now - skip_wide[0:1, part] * xc
            mixed = y_now.astype(bf16).astype(f32)
            gated = mixed * gate
            d_gated = go * bundle_ref[at_gain : at_gain + 1, part] * inv_rms - gated * pull
            slope = gate_up + gate * (1.0 - gate_up)
            gz_ref[here, part] = (d_gated * mixed * slope).astype(bf16)
            dy = dy_ref[here, part].astype(f32)
            chan_ref[0:1, part] += jnp.sum(go * gated * inv_rms, axis=0, keepdims=True)
            chan_ref[1:2, part] += jnp.sum(dy * xc, axis=0, keepdims=True)
            d_run = d_run + head_sums(dy * y_ssd, step * CHUNK, heads)
            started = (dy * start_wide[:, part]).astype(bf16)
            state = block_state(block, prior_ref, sloc_ref, keep_ref, part)
            return d_c + dot(started, state, ((1,), (1,))), d_run

        d_c, d_run = lax.fori_loop(
            0,
            channels // CHUNK,
            chunk,
            (jnp.zeros((STRETCH, NSTATE), f32), jnp.zeros((heads, STRETCH), f32)),
            unroll=UNROLL,
        )
        drun_ref[:, here] = d_run

        def pair(step, d_scores):
            part = lanes(step, PAIR)
            s_first, w_first = block_weights(scores, mask, run_wide, run_tall, 2 * step)
            s_second, w_second = block_weights(scores, mask, run_wide, run_tall, 2 * step + 1)
            dy = dy_ref[here, part]
            d_weights = dot(dy, both_heads(xp_ref[here, part]), ((1,), (1,)))
            dxp_ref[here, part] = dot(
                jnp.concatenate([w_first, w_second], axis=0), both_heads(dy), ((0,), (0,))
            )
            return (
                d_scores + d_weights[:, 0:STRETCH] * s_first + d_weights[:, STRETCH:] * s_second
            )

        d_scores = lax.fori_loop(
            0, channels // PAIR, pair, jnp.zeros((STRETCH, STRETCH), f32), unroll=UNROLL
        ).astype(bf16)
        dbc_ref[here, 0:NSTATE] = dot(d_scores, c_now, ((0,), (0,)))
        dbc_ref[here, NSTATE:] = d_c + dot(d_scores, b_now)


def conv_backward(d_ext, live, weight_ref, slope_ref, d_ref, x_ref, halo_ref, grad_ref, tail_ref,
                  pack_ref, rows, part):
    sums = None
    total = None
    for first in range(0, rows, STRETCH):
        here = slice(first, first + STRETCH)
        d_total = d_ref[here, part] * slope_ref[here, part]
        d_ext[PAD + first : PAD + first + STRETCH, part] = d_total
        now = jnp.sum(d_total, axis=0, keepdims=True)
        total = now if total is None else total + now
    pack_ref[CONV : CONV + 1, part] = total
    for first, count in [(-PAD, PAD)] + [(at, STRETCH) for at in range(0, rows, STRETCH)]:
        begin = PAD + first
        pieces = [d_ext[begin : begin + count, part]]
        for lag in range(1, CONV):
            moved = slice(begin + lag, begin + lag + count)
            pieces.append(d_ext[moved, part] * live[lag - 1, moved, :])
        grad = weight_ref[0:1, part] * pieces[0]
        for lag in range(1, CONV):
            grad = grad + weight_ref[lag : lag + 1, part] * pieces[lag]
        if first < 0:
            pack_ref[BACK : BACK + HALO, part] = grad[PAD - HALO :]
            seen = halo_ref[:, part]
            pieces = [piece[PAD - HALO :] for piece in pieces]
        else:
            grad_ref[first : first + count, part] = grad.astype(bf16)
            if first + count == rows:
                tail_ref[:, part] = grad[count - HALO :]
            seen = x_ref[first : first + count, part].astype(f32)
        now = [jnp.sum(seen * piece, axis=0, keepdims=True) for piece in pieces]
        sums = now if sums is None else [old + new for old, new in zip(sums, now)]
    for row, value in enumerate(sums):
        pack_ref[row : row + 1, part] = value


def finish_backward(
    later_early, later_last, aloc_ref, early_ref, last_ref, sloc_ref, keep_ref, dxp_ref, dbc_ref,
    drun_ref, xp_ref, dy_ref, bcc_ref, run_ref, dt_ref, flags_ref, sx_ref, sbc_ref,
    x_ref, xh_ref, bc_ref, bch_ref, wx_ref, wb_ref, rows_ref, dtr_ref, chan_ref,
    gx_ref, xtail_ref, xpack_ref, gbc_ref, bctail_ref, bcpack_ref, gdt_ref,
    clear, live, dx_ext, dbc_ext, d_x, d_bc, dt_wide, end_wide, ends, skip_wide, *, group,
):
    rows, channels = xp_ref.shape
    heads = run_ref.shape[0]
    blocks = rows // STRETCH
    prior_ref = (early_ref, last_ref)
    fill_live(flags_ref, clear, live)
    live[:, PAD + rows :, :] = jnp.zeros((HALO, PAD, STRETCH), f32)
    live[:, 0:PAD, :] = jnp.zeros((HALO, PAD, STRETCH), f32)
    for ext in (dx_ext, dbc_ext):
        ext[0:PAD, :] = jnp.zeros((PAD, ext.shape[1]), f32)
        ext[PAD + rows :, :] = jnp.zeros((PAD, ext.shape[1]), f32)
    skip_wide[0:1, :] = over_channels(head_column(rows_ref, SKIP_WEIGHT, group, heads))
    rate = jnp.exp(head_column(rows_ref, A_LOG, group, heads))
    dt_bias = head_column(rows_ref, DT_BIAS, group, heads)
    d_alog = jnp.zeros((heads, 1), f32)
    d_dtb = jnp.zeros((heads, 1), f32)
    for block in range(blocks):
        here = slice(block * STRETCH, (block + 1) * STRETCH)
        seen = resets_seen(flags_ref[:, here])
        running = run_ref[:, here]
        dt = dt_ref[:, here]
        dt_wide[...] = spread_heads(dt, HEAD_DIM)
        end_wide[...] = spread_heads(to_end_factor(running, seen), HEAD_DIM)
        b_now = bcc_ref[here, 0:NSTATE]

        def chunk(step, carry):
            d_b, per_step = carry
            part = lanes(step, CHUNK)
            later = later_early[:, part] + later_last[:, part]
            if block < blocks - 1:
                whole = keep_ref[block + 1 : block + 2, part]
                for place in range(block + 2, blocks):
                    whole = whole * keep_ref[place : place + 1, part]
                later = (aloc_ref[block, :, part].astype(f32) + whole * later.astype(f32)).astype(bf16)
            state = block_state(block, prior_ref, sloc_ref, keep_ref, part)
            d_keep = jnp.sum(later.astype(f32) * state.astype(f32), axis=0, keepdims=True)
            stepped = xp_ref[here, part].astype(f32)
            end = end_wide[:, part]
            d_end = dot(b_now, later) * end
            d_stepped = dxp_ref[here, part] + d_end
            ended = stepped * end
            ends[0:1, part] = (
                jnp.sum(stepped * d_end, axis=0, keepdims=True)
                + d_keep * keep_ref[block : block + 1, part]
            )
            d_x[here, part] = d_stepped * dt_wide[:, part] + skip_wide[0:1, part] * dy_ref[
                here, part
            ].astype(f32)
            return (
                d_b + dot(ended.astype(bf16), later, ((1,), (1,))),
                per_step + head_sums(stepped * d_stepped, step * CHUNK, heads),
            )

        d_b, per_step = lax.fori_loop(
            0,
            channels // CHUNK,
            chunk,
            (jnp.zeros((STRETCH, NSTATE), f32), jnp.zeros((heads, STRETCH), f32)),
            unroll=UNROLL,
        )
        d_bc[here, 0:NSTATE] = dbc_ref[here, 0:NSTATE] + d_b
        d_bc[here, NSTATE:] = dbc_ref[here, NSTATE:]
        at_end = head_sums(jnp.broadcast_to(ends[0:1, :], (STRETCH, channels)), 0, heads)
        is_last = iota((heads, STRETCH), 1) == STRETCH - 1
        d_run = drun_ref[:, here] - per_step + jnp.where(is_last, at_end, 0.0)
        shape = (STRETCH, STRETCH)
        d_log = dot_full(d_run, (iota(shape, 0) >= iota(shape, 1)).astype(f32))
        d_dt = per_step / dt - rate * d_log
        raw = dtr_ref[:, here].astype(f32) + dt_bias
        d_raw = d_dt / (1.0 + jnp.exp(-raw))
        gdt_ref[:, here] = d_raw
        d_alog = d_alog - jnp.sum(d_log * dt, axis=1, keepdims=True) * rate
        d_dtb = d_dtb + jnp.sum(d_raw, axis=1, keepdims=True)
    xpack_ref[GAIN : SKIP + 1, :] = chan_ref[0:2, :]
    bcpack_ref[GAIN : SKIP + 1, :] = jnp.zeros((2, bcpack_ref.shape[1]), f32)
    for place, column in enumerate((d_alog, d_dtb)):
        shape = (heads, STRETCH)
        pick = iota(shape, 1) == iota(shape, 0) + group * heads
        row = jnp.sum(jnp.where(pick, jnp.broadcast_to(column, shape), 0.0), axis=0, keepdims=True)
        bcpack_ref[GAIN : GAIN + 1, place * STRETCH : (place + 1) * STRETCH] = row

    def conv_chunk(step, carry):
        conv_backward(
            dx_ext, live, wx_ref, sx_ref, d_x, x_ref, xh_ref, gx_ref, xtail_ref, xpack_ref, rows,
            lanes(step, STRETCH),
        )
        return carry

    lax.fori_loop(0, channels // STRETCH, conv_chunk, 0, unroll=UNROLL)
    for step in range(2):
        conv_backward(
            dbc_ext, live, wb_ref, sbc_ref, d_bc, bc_ref, bch_ref, gbc_ref, bctail_ref, bcpack_ref,
            rows, slice(step * NSTATE, (step + 1) * NSTATE),
        )


def final_sums(mine_ref, pick_ref, flags_ref, *refs, arrivals, groups, scale):
    arrived, tails_x, tails_bc = refs[:arrivals], refs[arrivals], refs[arrivals + 1]
    out_wx, out_bx, out_wb, out_bb, out_alog, out_dtb, out_skip, out_gain, ending_ref = refs[
        arrivals + 2 :
    ]
    inner = tails_x.shape[1]
    total = mine_ref[0:BACK, :]
    back = jnp.zeros((HALO, total.shape[1]), f32)
    for place, ref in enumerate(arrived):
        value = ref[...].astype(f32)
        total = total + value[0:BACK]
        back = back + value[BACK:PACKED] * pick_ref[place : place + 1, 0:1]
    total = total * scale
    back = back * tail_factors(flags_ref)
    ending_ref[:, 0:inner] = (tails_x[...] + back[:, 0:inner]).astype(bf16)
    ending_ref[:, inner:] = (tails_bc[...] + back[:, inner:]).astype(bf16)
    out_wx[...] = total[0:CONV, 0:inner]
    out_bx[...] = total[CONV : CONV + 1, 0:inner]
    for which in range(2):
        for group in range(groups):
            first = inner + (2 * group + which) * NSTATE
            to = slice(group * NSTATE, (group + 1) * NSTATE)
            out_wb[:, which, to] = total[0:CONV, first : first + NSTATE]
            out_bb[which : which + 1, to] = total[CONV : CONV + 1, first : first + NSTATE]
    out_gain[...] = total[GAIN : GAIN + 1, 0:inner]
    heads = out_skip.shape[1]
    for out, shift in ((out_alog, 0), (out_dtb, STRETCH)):
        row = None
        for group in range(groups):
            first = inner + 2 * group * NSTATE + shift
            piece = total[GAIN : GAIN + 1, first : first + STRETCH]
            row = piece if row is None else row + piece
        out[...] = row[:, 0:heads]
    lane_sums = jnp.broadcast_to(total[SKIP : SKIP + 1, 0:inner], (PAD, inner))
    shape = (heads, inner)
    pick = (iota(shape, 1) // HEAD_DIM == iota(shape, 0)).astype(f32).astype(bf16)
    high = lane_sums.astype(bf16)
    low = (lane_sums - high.astype(f32)).astype(bf16)
    last = ((1,), (1,))
    out_skip[...] = (dot(high, pick, last) + dot(low, pick, last))[0:1]


def call(kernel, operands, outs, scratch, flops, name, blocked=None, hbm_outs=()):
    operands = [(each + (None,))[:3] for each in operands]
    cuts = [cut or {} for _, cut, _ in operands]
    arrays = [array for array, _, _ in operands]
    stages = [stage for _, _, stage in operands]
    shapes = [jax.ShapeDtypeStruct(shape, dtype) for shape, dtype in outs]
    streamed = [place for place, stage in enumerate(stages) if stage is not None]
    buffers = []
    for place in streamed:
        cut = cuts[place]
        shape = tuple(
            cut[dim].stop - cut[dim].start if dim in cut else extent
            for dim, extent in enumerate(arrays[place].shape)
        )
        buffers.append(pltpu.VMEM(shape, arrays[place].dtype))
    copies_made = sum(len(stages[place]) for place in streamed)

    def body(*refs):
        count, made = len(cuts), len(buffers)
        rest = refs[count:]
        held = dict(zip(streamed, rest[len(rest) - made - 1 : len(rest) - 1])) if made else {}
        sems = rest[-1] if made else None
        seen, copies = [], []
        for place, (ref, cut) in enumerate(zip(refs, cuts)):
            if cut:
                ref = ref.at[tuple(cut.get(dim, slice(None)) for dim in range(len(ref.shape)))]
            if place in held:
                buffer = held[place]
                size = buffer.shape[-1] // len(stages[place])
                for turn, stage in enumerate(stages[place]):
                    part = (slice(None),) * (len(buffer.shape) - 1) + (
                        slice(turn * size, (turn + 1) * size),
                    )
                    copy = (stage, (ref.at[part], buffer.at[part], sems.at[len(copies)]))
                    copies.append(copy)
                ref = buffer
            seen.append(ref)
        for _, copy in sorted(copies, key=lambda each: each[0]):
            pltpu.make_async_copy(*copy).start()

        def ready(stage):
            for which, copy in copies:
                if which == stage:
                    pltpu.make_async_copy(*copy).wait()

        if made:
            kernel(*seen, *rest[: len(rest) - made - 1], ready=ready)
        else:
            kernel(*seen, *rest)

    def block_of(array, cut):
        shape, index = [], []
        for dim, extent in enumerate(array.shape):
            part = cut.get(dim, slice(0, extent))
            size = part.stop - part.start
            shape.append(size)
            index.append(part.start // size)
        return pl.BlockSpec(tuple(shape), functools.partial(lambda fixed, i: fixed, tuple(index)))

    in_vmem = pl.BlockSpec(memory_space=pltpu.VMEM)
    in_hbm = pl.BlockSpec(memory_space=pltpu.HBM)
    scratch_shapes = [
        pltpu.VMEM(each, f32) if isinstance(each, tuple) else each for each in scratch
    ]
    if blocked:
        grid, limit = {"grid": (1,)}, blocked
        in_specs = [block_of(array, cut) for array, cut in zip(arrays, cuts)]
        out_specs = [block_of(shape, {}) for shape in shapes]
    else:
        grid, limit = {}, STREAM_LIMIT if buffers else VMEM_LIMIT
        in_specs = [in_vmem if stage is None else in_hbm for stage in stages]
        out_specs = [in_hbm if place in hbm_outs else in_vmem for place in range(len(shapes))]
        if buffers:
            scratch_shapes += buffers + [pltpu.SemaphoreType.DMA((copies_made,))]
    count = sum(each.size * each.dtype.itemsize for each in arrays + shapes)
    return pl.pallas_call(
        kernel if blocked else body,
        in_specs=in_specs,
        out_specs=out_specs,
        out_shape=shapes,
        scratch_shapes=scratch_shapes,
        compiler_params=pltpu.CompilerParams(vmem_limit_bytes=limit),
        cost_estimate=pl.CostEstimate(flops=flops, bytes_accessed=count, transcendentals=0),
        name=name,
        **grid,
    )(*arrays)


def together(*values):
    return lax.optimization_barrier(values)


def chain(parts, decays, axis, backward, fillers):
    count = lax.axis_size(axis)
    zero = [jnp.zeros(part.shape, bf16) for part in parts]
    early, last = list(zero), list(zero)
    results = []
    for hop in range(count - 1):
        pairs = [(count - 1 - hop, count - 2 - hop)] if backward else [(hop, hop + 1)]
        leaving = list(parts)
        if hop > 0:
            for place, part in enumerate(parts):
                early[place] = early[place] + last[place] if hop > 1 else last[place]
                arrived = early[place].astype(f32)
                leaving[place] = (decays[place] * arrived + part.astype(f32)).astype(bf16)
        if hop < len(fillers):
            work, array = fillers[hop]
            array = together(array, *leaving)[0]
        last = [lax.ppermute(each, axis, pairs) for each in leaving]
        if hop < len(fillers):
            done = work(array)
            last[0], *done = together(last[0], *done)
            results.append(done)
    for work, array in fillers[len(results) :]:
        results.append(work(array))
    return list(zip(early, last)), results


def exchange_terms(value, axis):
    count = lax.axis_size(axis)
    other = jnp.zeros_like(value)
    stride = 1
    while stride < count:
        value = value + other if stride > 1 else value
        other = lax.ppermute(value, axis, [(i, i ^ stride) for i in range(count)])
        stride *= 2
    return value, other


def per_device(
    x_raw, bc_raw, z_gate, dt_raw, resets, conv_x_weight, conv_x_bias, conv_bc_weight,
    conv_bc_bias, a_log, dt_bias, skip_weight, norm_gain, grad_out,
):
    rows, inner = x_raw.shape[1:]
    groups = bc_raw.shape[3] // NSTATE
    heads = a_log.shape[0] // groups
    channels = inner // groups
    blocks = rows // STRETCH
    width = 2 * NSTATE

    def by_group(value):
        lead = value.shape[:-2]
        split = value.reshape(lead + (2, groups, NSTATE))
        return jnp.moveaxis(split, -3, -2).reshape(lead + (groups * width,))

    x_own, z_own, go_own, dt_own = x_raw[0], z_gate[0], grad_out[0], dt_raw[0]
    bc_own = by_group(bc_raw[0])
    flags = resets
    count = lax.axis_size("ctx")
    sent = call(
        tails,
        [
            (x_raw, {1: slice(rows - 16, rows)}, [0]),
            (bc_raw, {1: slice(rows - 16, rows)}, [0]),
            (flags, {1: slice(rows - STRETCH, rows)}, [0]),
        ],
        [((HALO, inner + groups * width), f32)],
        [],
        rows,
        "tails",
    )[0]
    halo = lax.ppermute(sent, "ctx", [(i, i + 1) for i in range(count - 1)])
    head_rows = jnp.stack([a_log, dt_bias, skip_weight])
    head_rows = jnp.pad(head_rows, ((0, PAD - 3), (0, -head_rows.shape[1] % STRETCH)))
    bx, gain = conv_x_bias[None], norm_gain[None]
    wb, bb = by_group(conv_bc_weight), by_group(conv_bc_bias)[None]

    def wide(array, group):
        return (array, {1: slice(group * channels, (group + 1) * channels)})

    def narrow(array, group, first=0):
        return (array, {1: slice(first + group * width, first + (group + 1) * width)})

    def per_head(array, group):
        return (array, {0: slice(group * heads, (group + 1) * heads)})

    def whole(array):
        return (array, None)

    keep_rows = -(-(blocks + 1) // PAD) * PAD
    tall, thin, row_shape = (rows, channels), (rows, width), (heads, rows)
    state_shape = (NSTATE, channels)
    local_shape = (blocks - 1, NSTATE, channels)
    clear_shape, live_shape = (rows + PAD, STRETCH), (HALO, rows + 2 * PAD, STRETCH)
    wide_scratch = (STRETCH, channels)
    run_scratch = [(STRETCH, heads * STRETCH), (heads * PAD, STRETCH)]
    work = rows * channels * STRETCH
    group_range = range(groups)
    held = []
    for g in group_range:
        held.append(
            call(
                functools.partial(conv_and_state, group=g),
                [
                    wide(x_own, g), wide(halo, g), narrow(bc_own, g), narrow(halo, g, inner),
                    wide(conv_x_weight, g), wide(bx, g), narrow(wb, g), narrow(bb, g),
                    per_head(dt_own, g), whole(head_rows), whole(flags),
                ],
                [
                    (tall, bf16), (tall, bf16), (tall, f32), (thin, bf16), (thin, f32),
                    (row_shape, f32), (row_shape, f32), ((keep_rows, channels), f32),
                    (state_shape, bf16), (local_shape, bf16),
                ],
                [
                    (rows + PAD, channels), (rows + PAD, width), clear_shape, live_shape,
                    wide_scratch, wide_scratch, state_shape,
                ],
                2 * work,
                "conv_and_state",
            )
        )
    xc, xp, ux, bcc, ubc, dt, run, keep, s_dev, s_loc = zip(*held)
    decay = [k[blocks : blocks + 1] for k in keep]

    def forward_work(g):
        return lambda bcc_now: call(
            within_blocks,
            [
                whole(xp[g]), whole(bcc_now), whole(run[g]), whole(flags), whole(ux[g]), whole(ubc[g]),
            ],
            [(tall, f32), (tall, f32), (thin, f32)],
            run_scratch,
            6 * work,
            "within_blocks",
        )

    prior, held = chain(
        s_dev, decay, "ctx", False, [(forward_work(g), bcc[g]) for g in group_range]
    )
    y_within, slope_x, slope_bc = zip(*held)
    held, sums = [], ()
    for g in group_range:
        bundle, total = call(
            functools.partial(gate_forward, group=g),
            [
                whole(y_within[g]), whole(prior[g][0]), whole(prior[g][1]), whole(s_loc[g]),
                whole(keep[g]), whole(bcc[g]), whole(run[g]), whole(flags), whole(xc[g]),
                whole(head_rows), wide(z_own, g), wide(go_own, g), wide(gain, g),
            ]
            + [whole(each) for each in sums],
            [((bundle_rows(rows)[-1], channels), f32), ((2, rows), f32)],
            [wide_scratch, (PAD, channels)],
            2 * work,
            "gate_forward",
        )
        sums = (total,)
        held.append(bundle)
    bundle = held
    own, other = exchange_terms(sums[0], "head")
    held = [
        call(
            functools.partial(gate_backward, heads=heads),
            [whole(own), whole(other), whole(bundle[g]), wide(z_own, g), wide(go_own, g)],
            [(tall, bf16), (state_shape, bf16), (local_shape, bf16), ((2, rows), f32)],
            [wide_scratch, state_shape],
            2 * work,
            "gate_backward",
        )
        for g in group_range
    ]
    dy, a_dev, a_loc, totals = zip(*held)

    def backward_work(g):
        return lambda bcc_now: call(
            functools.partial(within_backward, group=g),
            [
                whole(totals[g]), whole(bundle[g]), wide(z_own, g), wide(go_own, g),
                whole(dy[g]), whole(xc[g]), whole(xp[g]), whole(bcc_now),
                whole(run[g]), whole(flags), whole(prior[g][0]), whole(prior[g][1]), whole(s_loc[g]),
                whole(keep[g]), whole(head_rows),
            ],
            [
                (tall, bf16), (tall, f32), (thin, f32), (row_shape, f32), ((PAD, channels), f32),
            ],
            run_scratch + [wide_scratch, (PAD, channels)],
            10 * work,
            "within_backward",
            BLOCKED_LIMIT,
        )

    later, held = chain(
        a_dev, decay, "ctx", True, [(backward_work(g), bcc[g]) for g in group_range]
    )
    gz, dxp, dbc, drun, chan = zip(*held)
    held = [
        call(
            functools.partial(finish_backward, group=g),
            [
                whole(later[g][0]), whole(later[g][1]), whole(a_loc[g]), whole(prior[g][0]),
                whole(prior[g][1]), whole(s_loc[g]), whole(keep[g]), whole(dxp[g]), whole(dbc[g]),
                whole(drun[g]), whole(xp[g]), whole(dy[g]), whole(bcc[g]), whole(run[g]),
                whole(dt[g]), whole(flags), whole(slope_x[g]), whole(slope_bc[g]), wide(x_own, g),
                wide(halo, g), narrow(bc_own, g), narrow(halo, g, inner), wide(conv_x_weight, g),
                narrow(wb, g), whole(head_rows), per_head(dt_own, g), whole(chan[g]),
            ],
            [
                (tall, bf16), ((HALO, channels), f32), ((PACKED, channels), f32), (thin, bf16),
                ((HALO, width), f32), ((PACKED, width), f32), (row_shape, f32),
            ],
            [
                clear_shape, live_shape, (rows + 2 * PAD, channels), (rows + 2 * PAD, width), tall,
                thin, wide_scratch, wide_scratch, (PAD, channels), (PAD, channels),
            ],
            4 * work,
            "finish_backward",
            BLOCKED_LIMIT,
        )
        for g in group_range
    ]
    gx, x_tail, x_pack, gbc, bc_tail, bc_pack, gdt = zip(*held)

    def joined(pieces):
        return jnp.concatenate(pieces, axis=1)

    def ungroup(value):
        lead = value.shape[:-1]
        split = value.reshape(lead + (groups, 2, NSTATE))
        return jnp.moveaxis(split, -3, -2).reshape(lead + (2, groups * NSTATE))

    packed = joined(x_pack + bc_pack)
    mine = packed
    for shift in range(1, lax.axis_size("dp")):
        size = lax.axis_size("dp")
        other = lax.ppermute(packed, "dp", [(i, (i + shift) % size) for i in range(size)])
        mine = jnp.where(jnp.arange(PACKED)[:, None] < BACK, mine + other, mine)
    leaving = mine.astype(bf16)
    here = lax.axis_index("ctx")
    arrived, picks = [], []
    for shift in range(1, count):
        arrived.append(lax.ppermute(leaving, "ctx", [(i, i ^ shift) for i in range(count)]))
        picks.append((here ^ shift) == here + 1)
    pick = jnp.broadcast_to(jnp.stack(picks).astype(f32)[:, None], (count - 1, STRETCH))
    out_wx, out_bx, out_wb, out_bb, out_alog, out_dtb, out_skip, out_gain, ending = call(
        functools.partial(
            final_sums,
            arrivals=count - 1,
            groups=groups,
            scale=float(lax.axis_size("dp") * count * rows) ** (-0.5),
        ),
        [whole(mine), whole(pick), whole(flags)]
        + [whole(each) for each in arrived]
        + [whole(joined(x_tail)), whole(joined(bc_tail))],
        [
            ((CONV, inner), f32), ((1, inner), f32), ((CONV, 2, groups * NSTATE), f32),
            ((2, groups * NSTATE), f32),
            ((1, groups * heads), f32), ((1, groups * heads), f32), ((1, groups * heads), f32),
            ((1, inner), f32), ((HALO, inner + groups * width), bf16),
        ],
        [],
        rows * inner,
        "final_sums",
    )
    grad_x = lax.dynamic_update_slice(joined(gx), ending[:, :inner], (rows - HALO, 0))
    grad_bc = lax.dynamic_update_slice(
        ungroup(joined(gbc)), ungroup(ending[:, inner:]), (rows - HALO, 0, 0)
    )
    return (
        grad_x[None],
        grad_bc[None],
        joined(gz)[None],
        jnp.concatenate(gdt, axis=0)[None],
        out_wx,
        out_bx[0],
        out_wb,
        out_bb,
        out_alog[0],
        out_dtb[0],
        out_skip[0],
        out_gain[0],
    )


def solution(mesh):
    return jax.shard_map(
        per_device,
        mesh=mesh,
        in_specs=(
            P("dp", "ctx", "head"),
            P("dp", "ctx", None, "head"),
            P("dp", "ctx", "head"),
            P("dp", "head", "ctx"),
            P("dp", "ctx"),
            P(None, "head"),
            P("head"),
            P(None, None, "head"),
            P(None, "head"),
            P("head"),
            P("head"),
            P("head"),
            P("head"),
            P("dp", "ctx", "head"),
        ),
        out_specs=(
            P("dp", "ctx", "head"),
            P("dp", "ctx", None, "head"),
            P("dp", "ctx", "head"),
            P("dp", "head", "ctx"),
            P(None, "head"),
            P("head"),
            P(None, None, "head"),
            P(None, "head"),
            P("head"),
            P("head"),
            P("head"),
            P("head"),
        ),
        check_vma=False,
    )
```

```python
import functools

import jax
import jax.numpy as jnp
import numpy as np
from jax import lax
from jax.experimental import pallas as pl
from jax.experimental.pallas import tpu as pltpu
from jax.sharding import PartitionSpec as P

HEAD_DIM = 64
NSTATE = 128
CONV = 4
STRETCH = 128
INNER = 8192
HALO = CONV - 1
PAD = 8
CHUNK = 256
PAIR = 2 * HEAD_DIM
NORM_EPS = 1e-05
LOWEST = -1e30
GAIN, SKIP, BACK = CONV + 1, CONV + 2, CONV + 3
PACKED = BACK + HALO
A_LOG, DT_BIAS, SKIP_WEIGHT = range(3)
STAGES = 2
STREAM_LIMIT = 62 * 1024 * 1024
PIECES = 2
BLOCKED_LIMIT = 40 * 1024 * 1024
VMEM_LIMIT = 24 * 1024 * 1024

f32 = jnp.float32
bf16 = jnp.bfloat16


def dot(a, b, contract=((1,), (0,))):
    return lax.dot_general(a, b, (contract, ((), ())), preferred_element_type=f32)


def dot_full(a, b):
    return lax.dot_general(
        a, b, (((1,), (0,)), ((), ())), precision=lax.Precision.HIGHEST, preferred_element_type=f32
    )


def iota(shape, dim):
    return lax.broadcasted_iota(jnp.int32, shape, dim)


def split3(value):
    high = value.astype(bf16)
    rest = value - high.astype(f32)
    middle = rest.astype(bf16)
    low = (rest - middle.astype(f32)).astype(bf16)
    return jnp.concatenate([high, middle, low], axis=0)


def spread_heads(rows, width):
    heads = rows.shape[0]
    shape = (heads, heads * width)
    pick = (iota(shape, 1) // width == iota(shape, 0)).astype(f32).astype(bf16)
    return dot(split3(rows), jnp.concatenate([pick] * 3, axis=0), ((0,), (0,)))


def head_sums(value, first, heads):
    shape = (heads, value.shape[1])
    pick = ((iota(shape, 1) + first) // HEAD_DIM == iota(shape, 0)).astype(f32).astype(bf16)
    high = value.astype(bf16)
    low = (value - high.astype(f32)).astype(bf16)
    last = ((1,), (1,))
    return dot(pick, high, last) + dot(pick, low, last)


def as_columns(row):
    return jnp.transpose(jnp.broadcast_to(row, (STRETCH, STRETCH)))


def sigmoid(value):
    return 0.5 * jnp.tanh(0.5 * value) + 0.5


def upper_ones():
    shape = (STRETCH, STRETCH)
    return (iota(shape, 0) <= iota(shape, 1)).astype(f32)


def resets_seen(flags_row):
    flags = jnp.broadcast_to(flags_row.astype(f32), (PAD, STRETCH)).astype(bf16)
    return dot(flags, upper_ones().astype(bf16))[0:1]


def decay_mask(seen):
    shape = (STRETCH, STRETCH)
    same = (as_columns(seen) == jnp.broadcast_to(seen, shape)) & (iota(shape, 0) >= iota(shape, 1))
    return jnp.where(same, 0.0, LOWEST)


def lanes(position, size):
    return slice(position * size, (position + 1) * size)


def repeat(count, body, carry):
    for step in range(count):
        carry = body(step, carry)
    return carry


def piece_of(refs, part):
    width = refs[0].shape[1]
    ref = refs[part.start // width]
    return ref[:, part.start % width : part.start % width + part.stop - part.start]


def to_column(row, first, heads):
    shape = (heads, row.shape[1])
    pick = iota(shape, 1) == iota(shape, 0) + first
    return jnp.sum(jnp.where(pick, jnp.broadcast_to(row, shape), 0.0), axis=1, keepdims=True)


def over_channels(column):
    return spread_heads(jnp.broadcast_to(column, (column.shape[0], STRETCH)), HEAD_DIM)[0:1]


def softplus(value):
    small = jnp.exp(-jnp.abs(value))
    series = small * (1.0 - small * (1 / 2 - small * (1 / 3 - small * (1 / 4 - small * (1 / 5)))))
    return jnp.maximum(value, 0.0) + jnp.where(small < 0.03, series, jnp.log(1.0 + small))


def head_column(rows_ref, which, group, heads):
    return to_column(rows_ref[which : which + 1, :], group * heads, heads)


def step_sizes(dtr_ref, rows_ref, group):
    heads = dtr_ref.shape[0]
    return softplus(dtr_ref[...].astype(f32) + head_column(rows_ref, DT_BIAS, group, heads))


def to_end_factor(running, seen):
    final = running[:, STRETCH - 1 : STRETCH]
    return jnp.where(seen == seen[:, STRETCH - 1 : STRETCH], jnp.exp(final - running), 0.0)


def doubled(value):
    return jnp.concatenate([value, value], axis=1)


def fill_live(flags_ref, clear, live):
    rows = flags_ref.shape[1]
    clear[0:PAD, :] = jnp.ones((PAD, STRETCH), f32)
    for first in range(0, rows, STRETCH):
        flags = flags_ref[:, first : first + STRETCH].astype(f32)
        clear[PAD + first : PAD + first + STRETCH, :] = as_columns(1.0 - flags)
    for first in range(0, rows, STRETCH):
        begin = PAD + first
        product = clear[begin : begin + STRETCH, :]
        live[0, begin : begin + STRETCH, :] = product
        for lag in range(2, CONV):
            product = product * clear[begin - lag + 1 : begin - lag + 1 + STRETCH, :]
            live[lag - 1, begin : begin + STRETCH, :] = product


def fill_extended(extended, halo_ref, rows_ref):
    extended[PAD - HALO : PAD, :] = halo_ref[...]
    extended[PAD:, :] = rows_ref[...].astype(f32)


def conv_total(extended, live, weight_ref, bias_ref, first, part):
    begin = PAD + first
    total = bias_ref[0:1, part] + weight_ref[0:1, part] * extended[begin : begin + STRETCH, part]
    width = total.shape[1] // STRETCH
    for lag in range(1, CONV):
        mask = jnp.concatenate([live[lag - 1, begin : begin + STRETCH, :]] * width, axis=1)
        total = total + weight_ref[lag : lag + 1, part] * (
            extended[begin - lag : begin - lag + STRETCH, part] * mask
        )
    return total


def tail_factors(flags_ref):
    flags = flags_ref[:, flags_ref.shape[1] - STRETCH :].astype(f32)
    clear = as_columns(1.0 - flags)
    last = clear[STRETCH - 1 :]
    both = last * clear[STRETCH - 2 : STRETCH - 1]
    return jnp.concatenate([both, last, jnp.ones_like(last)], axis=0)[:, 0:1]


def tails(x_ref, bc_ref, flags_ref, out_ref, *, ready):
    ready(0)
    keep = tail_factors(flags_ref)
    inner = x_ref.shape[2]
    out_ref[:, 0:inner] = x_ref[0].astype(f32)[x_ref.shape[1] - HALO :] * keep
    groups = bc_ref.shape[3] // NSTATE
    for which in range(2):
        rows = bc_ref[0, :, which, :].astype(f32)[bc_ref.shape[1] - HALO :] * keep
        for group in range(groups):
            first = inner + (2 * group + which) * NSTATE
            out_ref[:, first : first + NSTATE] = rows[:, group * NSTATE : (group + 1) * NSTATE]


def conv_and_state(
    x_ref, xh_ref, bc_ref, bch_ref, wx_ref, bx_ref, wb_ref, bb_ref, dtr_ref, rows_ref,
    flags_ref, xc_ref, xp_ref, ux_ref, bcc_ref, ubc_ref, run_ref, keep_ref, sloc_ref, *refs, group,
):
    sdev_refs, decay_refs = refs[:PIECES], refs[PIECES : 2 * PIECES]
    x_ext, bc_ext, clear, live, dt_wide, end_wide, state = refs[2 * PIECES :]
    rows, channels = x_ref.shape
    heads = dtr_ref.shape[0]
    fill_extended(x_ext, xh_ref, x_ref)
    fill_extended(bc_ext, bch_ref, bc_ref)
    fill_live(flags_ref, clear, live)
    blocks = rows // STRETCH
    rate = jnp.exp(head_column(rows_ref, A_LOG, group, heads))
    dt_all = step_sizes(dtr_ref, rows_ref, group)
    product = None
    for block in range(blocks):
        first = block * STRETCH
        here = slice(first, first + STRETCH)
        every = slice(None)
        total = conv_total(bc_ext, live, wb_ref, bb_ref, first, every)
        ubc_ref[here, :] = total
        bc_now = (total * sigmoid(total)).astype(bf16)
        bcc_ref[here, :] = bc_now
        b_turned = jnp.transpose(bc_now[:, 0:NSTATE].astype(f32)).astype(bf16)
        seen = resets_seen(flags_ref[:, here])
        dt = dt_all[:, here]
        running = dot_full(-rate * dt, upper_ones())
        run_ref[:, here] = running
        final = running[:, STRETCH - 1 : STRETCH]
        keep = jnp.where(seen[:, STRETCH - 1 : STRETCH] == 0.0, jnp.exp(final), 0.0)
        keep_row = over_channels(keep)
        keep_ref[block : block + 1, :] = keep_row
        product = keep_row if product is None else product * keep_row
        dt_wide[...] = spread_heads(dt, HEAD_DIM)
        end_wide[...] = spread_heads(to_end_factor(running, seen), HEAD_DIM)

        def chunk(step, carry):
            part = lanes(step, CHUNK)
            total = conv_total(x_ext, live, wx_ref, bx_ref, first, part)
            ux_ref[here, part] = total
            xc = (total * sigmoid(total)).astype(bf16)
            xc_ref[here, part] = xc
            stepped = (xc.astype(f32) * dt_wide[:, part]).astype(bf16)
            xp_ref[here, part] = stepped
            ended = (stepped.astype(f32) * end_wide[:, part]).astype(bf16)
            fresh = dot(b_turned, ended)
            if block > 0:
                fresh = keep_ref[block : block + 1, part] * state[:, part] + fresh
            if block < blocks - 1:
                state[:, part] = fresh
                sloc_ref[block, :, part] = fresh.astype(bf16)
            else:
                put_piece(sdev_refs, part, fresh.astype(bf16))
            return carry

        repeat(channels // CHUNK, chunk, 0)
    for place, ref in enumerate(decay_refs):
        size = ref.shape[1]
        ref[...] = product[:, place * size : (place + 1) * size]


def place_runs(run_ref, here, run_wide, run_tall):
    running = run_ref[:, here]
    run_wide[...] = spread_heads(running, STRETCH)
    for head in range(running.shape[0]):
        run_tall[head * PAD : (head + 1) * PAD, :] = jnp.broadcast_to(
            running[head : head + 1], (PAD, STRETCH)
        )


def block_weights(scores, mask, run_wide, run_tall, head):
    column = run_wide[:, lanes(head, STRETCH)]
    row = run_tall[head * PAD : head * PAD + 1, :]
    segment = jnp.exp(column - row + mask)
    return segment, (scores * segment).astype(bf16)


def both_heads(value):
    is_first = iota(value.shape, 1) < HEAD_DIM
    wide = value.astype(f32)
    zero = jnp.zeros_like(wide)
    return jnp.concatenate(
        [jnp.where(is_first, wide, zero).astype(bf16), jnp.where(is_first, zero, wide).astype(bf16)],
        axis=0,
    )


def put_piece(refs, part, value):
    width = refs[0].shape[1]
    ref = refs[part.start // width]
    ref[:, part.start % width : part.start % width + part.stop - part.start] = value


def slope_of(total):
    up = sigmoid(total)
    return up + total * up * (1.0 - up)


def within_blocks(
    xp_ref, bcc_ref, run_ref, flags_ref, ux_ref, ubc_ref, y_ref, sx_ref, sbc_ref, run_wide, run_tall
):
    rows, channels = xp_ref.shape
    for block in range(rows // STRETCH):
        here = slice(block * STRETCH, (block + 1) * STRETCH)
        mask = decay_mask(resets_seen(flags_ref[:, here]))
        scores = dot(bcc_ref[here, NSTATE:], bcc_ref[here, 0:NSTATE], ((1,), (1,)))
        place_runs(run_ref, here, run_wide, run_tall)
        sbc_ref[here, :] = slope_of(ubc_ref[here, :])

        def pair(step, carry):
            _, w_first = block_weights(scores, mask, run_wide, run_tall, 2 * step)
            _, w_second = block_weights(scores, mask, run_wide, run_tall, 2 * step + 1)
            part = lanes(step, PAIR)
            y_ref[here, part] = dot(
                jnp.concatenate([w_first, w_second], axis=1), both_heads(xp_ref[here, part])
            )
            sx_ref[here, part] = slope_of(ux_ref[here, part])
            return carry

        repeat(channels // PAIR, pair, 0)


def start_factor(run_ref, flags_ref, here):
    seen = resets_seen(flags_ref[:, here])
    return jnp.where(seen == 0.0, jnp.exp(run_ref[:, here]), 0.0)


def block_state(block, prior_ref, sloc_ref, keep_ref, part):
    state = piece_of(prior_ref[:PIECES], part) + piece_of(prior_ref[PIECES:], part)
    if block == 0:
        return state
    whole = keep_ref[0:1, part]
    for step in range(1, block):
        whole = whole * keep_ref[step : step + 1, part]
    return (whole * state.astype(f32) + sloc_ref[block - 1, :, part].astype(f32)).astype(bf16)


def bundle_rows(rows):
    places = [rows]
    for size in (PAD, PAD, 2 * PAD, NSTATE // 4):
        places.append(places[-1] + size)
    return places


def gate_forward(
    y_ref, sloc_ref, keep_ref, bcc_ref, run_ref, flags_ref, xc_ref, rows_ref, z_ref, go_ref, gain_ref,
    *refs, group,
):
    prior_ref, refs = refs[: 2 * PIECES], refs[2 * PIECES :]
    *before, bundle_ref, sums_ref, start_wide, skip_wide = refs
    rows, channels = xc_ref.shape
    heads = run_ref.shape[0]
    at_keep, at_gain, at_start, at_turned, _ = bundle_rows(rows)
    bundle_ref[at_keep:at_gain, :] = keep_ref[0:PAD, :]
    bundle_ref[at_gain:at_start, :] = jnp.broadcast_to(gain_ref[...], (PAD, channels))
    skip_wide[0:1, :] = over_channels(head_column(rows_ref, SKIP_WEIGHT, group, heads))
    quarter = NSTATE // 4
    for block in range(rows // STRETCH):
        here = slice(block * STRETCH, (block + 1) * STRETCH)
        start = start_factor(run_ref, flags_ref, here)
        bundle_ref[at_start : at_start + heads, here] = start
        start_wide[...] = spread_heads(start, HEAD_DIM)
        c_now = bcc_ref[here, NSTATE:]
        turned = jnp.transpose(c_now.astype(f32))
        for turn in range(4):
            first = turn * rows + block * STRETCH
            bundle_ref[at_turned : at_turned + quarter, first : first + STRETCH] = turned[
                turn * quarter : (turn + 1) * quarter
            ]

        def chunk(step, carry):
            squares, products = carry
            part = lanes(step, CHUNK)
            carried = dot(c_now, block_state(block, prior_ref, sloc_ref, keep_ref, part))
            y_now = y_ref[here, part] + carried * start_wide[:, part]
            y_now = y_now + skip_wide[0:1, part] * xc_ref[here, part].astype(f32)
            bundle_ref[here, part] = y_now
            z = z_ref[here, part].astype(f32)
            gated = y_now.astype(bf16).astype(f32) * (z * sigmoid(z))
            gained = go_ref[here, part].astype(f32) * gain_ref[0:1, part]
            return squares + gated * gated, products + gated * gained

        zero = jnp.zeros((STRETCH, CHUNK), f32)
        squares, products = repeat(channels // CHUNK, chunk, (zero, zero))
        square_column = jnp.sum(squares, axis=1, keepdims=True)
        product_column = jnp.sum(products, axis=1, keepdims=True)
        shape = (STRETCH, STRETCH)
        both = jnp.where(
            iota(shape, 1) == 0,
            jnp.broadcast_to(square_column, shape),
            jnp.broadcast_to(product_column, shape),
        )
        total = jnp.transpose(both)[0:2]
        for ref in before:
            total = total + ref[:, here]
        sums_ref[:, here] = total


def norm_factors(totals_ref, here):
    squares = totals_ref[0:1, here]
    products = totals_ref[1:2, here]
    inv_rms = lax.rsqrt(squares * (1.0 / INNER) + NORM_EPS)
    pull = inv_rms * inv_rms * inv_rms * products * (1.0 / INNER)
    return doubled(as_columns(inv_rms)), doubled(as_columns(pull))


def gate_backward(
    own_ref, other_ref, bundle_ref, z_ref, go_ref, dy_ref, aloc_ref, totals_ref, y_ref, *refs, heads,
):
    adev_refs, (start_wide, adjoint) = refs[:PIECES], refs[PIECES:]
    rows, channels = z_ref.shape
    blocks = rows // STRETCH
    at_keep, at_gain, at_start, at_turned, end = bundle_rows(rows)
    totals_ref[...] = own_ref[...] + other_ref[...]
    for block in reversed(range(blocks)):
        here = slice(block * STRETCH, (block + 1) * STRETCH)
        start_wide[...] = spread_heads(bundle_ref[at_start : at_start + heads, here], HEAD_DIM)
        inv_rms, pull = norm_factors(totals_ref, here)
        firsts = [turn * rows + block * STRETCH for turn in range(4)]
        c_turned = jnp.concatenate(
            [bundle_ref[at_turned:end, first : first + STRETCH] for first in firsts], axis=0
        ).astype(bf16)

        def chunk(step, carry):
            part = lanes(step, CHUNK)
            z = z_ref[here, part].astype(f32)
            gate = z * sigmoid(z)
            gained = go_ref[here, part].astype(f32) * bundle_ref[at_gain : at_gain + 1, part]
            y_now = bundle_ref[here, part]
            y_ref[here, part] = y_now
            mixed = y_now.astype(bf16).astype(f32)
            d_gated = gained * inv_rms - mixed * gate * pull
            dy = (d_gated * gate).astype(bf16)
            dy_ref[here, part] = dy
            fresh = dot(c_turned, (dy.astype(f32) * start_wide[:, part]).astype(bf16))
            if block < blocks - 1:
                keep = bundle_ref[at_keep + block : at_keep + block + 1, part]
                fresh = fresh + keep * adjoint[:, part]
            if block > 0:
                adjoint[:, part] = fresh
                aloc_ref[block - 1, :, part] = fresh.astype(bf16)
            else:
                put_piece(adev_refs, part, fresh.astype(bf16))
            return carry

        repeat(channels // CHUNK, chunk, 0)


def within_backward(
    totals_ref, y_ref, z_ref, go_ref, gain_ref, dy_ref, xc_ref, xp_ref, bcc_ref,
    run_ref, flags_ref, sloc_ref, keep_ref, rows_ref, *refs, group,
):
    prior_ref, refs = refs[: 2 * PIECES], refs[2 * PIECES :]
    gz_ref, dxp_ref, dbc_ref, drun_ref, chan_ref, run_wide, run_tall, start_wide, skip_wide = refs
    rows, channels = xc_ref.shape
    heads = run_ref.shape[0]
    skip_wide[0:1, :] = over_channels(head_column(rows_ref, SKIP_WEIGHT, group, heads))
    chan_ref[...] = jnp.zeros_like(chan_ref)
    for block in range(rows // STRETCH):
        here = slice(block * STRETCH, (block + 1) * STRETCH)
        mask = decay_mask(resets_seen(flags_ref[:, here]))
        b_now = bcc_ref[here, 0:NSTATE]
        c_now = bcc_ref[here, NSTATE:]
        scores = dot(c_now, b_now, ((1,), (1,)))
        place_runs(run_ref, here, run_wide, run_tall)
        start_wide[...] = spread_heads(start_factor(run_ref, flags_ref, here), HEAD_DIM)
        inv_rms, pull = norm_factors(totals_ref, here)

        def chunk(step, carry):
            d_c, d_run = carry
            part = lanes(step, CHUNK)
            z = z_ref[here, part].astype(f32)
            gate_up = sigmoid(z)
            gate = z * gate_up
            go = go_ref[here, part].astype(f32)
            xc = xc_ref[here, part].astype(f32)
            y_now = y_ref[here, part]
            y_ssd = y_now - skip_wide[0:1, part] * xc
            mixed = y_now.astype(bf16).astype(f32)
            gated = mixed * gate
            d_gated = go * gain_ref[0:1, part] * inv_rms - gated * pull
            slope = gate_up + gate * (1.0 - gate_up)
            gz_ref[here, part] = (d_gated * mixed * slope).astype(bf16)
            dy = dy_ref[here, part].astype(f32)
            chan_ref[0:1, part] += jnp.sum(go * gated * inv_rms, axis=0, keepdims=True)
            chan_ref[1:2, part] += jnp.sum(dy * xc, axis=0, keepdims=True)
            d_run = d_run + head_sums(dy * y_ssd, step * CHUNK, heads)
            started = (dy * start_wide[:, part]).astype(bf16)
            state = block_state(block, prior_ref, sloc_ref, keep_ref, part)
            return d_c + dot(started, state, ((1,), (1,))), d_run

        d_c, d_run = repeat(
            channels // CHUNK,
            chunk,
            (jnp.zeros((STRETCH, NSTATE), f32), jnp.zeros((heads, STRETCH), f32)),
        )
        drun_ref[:, here] = d_run

        def pair(step, d_scores):
            part = lanes(step, PAIR)
            s_first, w_first = block_weights(scores, mask, run_wide, run_tall, 2 * step)
            s_second, w_second = block_weights(scores, mask, run_wide, run_tall, 2 * step + 1)
            dy = dy_ref[here, part]
            d_weights = dot(dy, both_heads(xp_ref[here, part]), ((1,), (1,)))
            dxp_ref[here, part] = dot(
                jnp.concatenate([w_first, w_second], axis=0), both_heads(dy), ((0,), (0,))
            )
            return (
                d_scores + d_weights[:, 0:STRETCH] * s_first + d_weights[:, STRETCH:] * s_second
            )

        d_scores = repeat(channels // PAIR, pair, jnp.zeros((STRETCH, STRETCH), f32)).astype(bf16)
        dbc_ref[here, 0:NSTATE] = dot(d_scores, c_now, ((0,), (0,)))
        dbc_ref[here, NSTATE:] = d_c + dot(d_scores, b_now)


def conv_backward(d_ext, live, weight_ref, slope_ref, d_ref, x_ref, halo_ref, grad_ref, tail_ref,
                  pack_ref, rows, part):
    sums = None
    total = None
    for first in range(0, rows, STRETCH):
        here = slice(first, first + STRETCH)
        d_total = d_ref[here, part] * slope_ref[here, part]
        d_ext[PAD + first : PAD + first + STRETCH, part] = d_total
        now = jnp.sum(d_total, axis=0, keepdims=True)
        total = now if total is None else total + now
    pack_ref[CONV : CONV + 1, part] = total
    for first, count in [(-PAD, PAD)] + [(at, STRETCH) for at in range(0, rows, STRETCH)]:
        begin = PAD + first
        pieces = [d_ext[begin : begin + count, part]]
        for lag in range(1, CONV):
            moved = slice(begin + lag, begin + lag + count)
            pieces.append(d_ext[moved, part] * live[lag - 1, moved, :])
        grad = weight_ref[0:1, part] * pieces[0]
        for lag in range(1, CONV):
            grad = grad + weight_ref[lag : lag + 1, part] * pieces[lag]
        if first < 0:
            pack_ref[BACK : BACK + HALO, part] = grad[PAD - HALO :]
            seen = halo_ref[:, part]
            pieces = [piece[PAD - HALO :] for piece in pieces]
        else:
            grad_ref[first : first + count, part] = grad.astype(bf16)
            if first + count == rows:
                tail_ref[:, part] = grad[count - HALO :]
            seen = x_ref[first : first + count, part].astype(f32)
        now = [jnp.sum(seen * piece, axis=0, keepdims=True) for piece in pieces]
        sums = now if sums is None else [old + new for old, new in zip(sums, now)]
    for row, value in enumerate(sums):
        pack_ref[row : row + 1, part] = value


def finish_backward(
    aloc_ref, sloc_ref, keep_ref, dxp_ref, dbc_ref, drun_ref, xp_ref, dy_ref, bcc_ref, run_ref,
    flags_ref, sx_ref, sbc_ref, x_ref, xh_ref, bc_ref, bch_ref, wx_ref, wb_ref, rows_ref, dtr_ref,
    chan_ref, *refs, group,
):
    later_refs, prior_ref, refs = refs[: 2 * PIECES], refs[2 * PIECES : 4 * PIECES], refs[4 * PIECES :]
    gx_ref, xtail_ref, xpack_ref, gbc_ref, bctail_ref, bcpack_ref, gdt_ref, *refs = refs
    clear, live, dx_ext, dbc_ext, d_x, d_bc, dt_wide, end_wide, ends, skip_wide = refs
    rows, channels = xp_ref.shape
    heads = run_ref.shape[0]
    blocks = rows // STRETCH
    fill_live(flags_ref, clear, live)
    live[:, PAD + rows :, :] = jnp.zeros((HALO, PAD, STRETCH), f32)
    live[:, 0:PAD, :] = jnp.zeros((HALO, PAD, STRETCH), f32)
    for ext in (dx_ext, dbc_ext):
        ext[0:PAD, :] = jnp.zeros((PAD, ext.shape[1]), f32)
        ext[PAD + rows :, :] = jnp.zeros((PAD, ext.shape[1]), f32)
    skip_wide[0:1, :] = over_channels(head_column(rows_ref, SKIP_WEIGHT, group, heads))
    rate = jnp.exp(head_column(rows_ref, A_LOG, group, heads))
    dt_bias = head_column(rows_ref, DT_BIAS, group, heads)
    dt_all = step_sizes(dtr_ref, rows_ref, group)
    d_alog = jnp.zeros((heads, 1), f32)
    d_dtb = jnp.zeros((heads, 1), f32)
    for block in range(blocks):
        here = slice(block * STRETCH, (block + 1) * STRETCH)
        seen = resets_seen(flags_ref[:, here])
        running = run_ref[:, here]
        dt = dt_all[:, here]
        dt_wide[...] = spread_heads(dt, HEAD_DIM)
        end_wide[...] = spread_heads(to_end_factor(running, seen), HEAD_DIM)
        b_now = bcc_ref[here, 0:NSTATE]

        def chunk(step, carry):
            d_b, per_step = carry
            part = lanes(step, CHUNK)
            later = piece_of(later_refs[:PIECES], part) + piece_of(later_refs[PIECES:], part)
            if block < blocks - 1:
                whole = keep_ref[block + 1 : block + 2, part]
                for place in range(block + 2, blocks):
                    whole = whole * keep_ref[place : place + 1, part]
                later = (aloc_ref[block, :, part].astype(f32) + whole * later.astype(f32)).astype(bf16)
            state = block_state(block, prior_ref, sloc_ref, keep_ref, part)
            d_keep = jnp.sum(later.astype(f32) * state.astype(f32), axis=0, keepdims=True)
            stepped = xp_ref[here, part].astype(f32)
            end = end_wide[:, part]
            d_end = dot(b_now, later) * end
            d_stepped = dxp_ref[here, part] + d_end
            ended = stepped * end
            ends[0:1, part] = (
                jnp.sum(stepped * d_end, axis=0, keepdims=True)
                + d_keep * keep_ref[block : block + 1, part]
            )
            d_x[here, part] = d_stepped * dt_wide[:, part] + skip_wide[0:1, part] * dy_ref[
                here, part
            ].astype(f32)
            return (
                d_b + dot(ended.astype(bf16), later, ((1,), (1,))),
                per_step + head_sums(stepped * d_stepped, step * CHUNK, heads),
            )

        d_b, per_step = repeat(
            channels // CHUNK,
            chunk,
            (jnp.zeros((STRETCH, NSTATE), f32), jnp.zeros((heads, STRETCH), f32)),
        )
        d_bc[here, 0:NSTATE] = dbc_ref[here, 0:NSTATE] + d_b
        d_bc[here, NSTATE:] = dbc_ref[here, NSTATE:]
        at_end = head_sums(jnp.broadcast_to(ends[0:1, :], (STRETCH, channels)), 0, heads)
        is_last = iota((heads, STRETCH), 1) == STRETCH - 1
        d_run = drun_ref[:, here] - per_step + jnp.where(is_last, at_end, 0.0)
        shape = (STRETCH, STRETCH)
        d_log = dot_full(d_run, (iota(shape, 0) >= iota(shape, 1)).astype(f32))
        d_dt = per_step / dt - rate * d_log
        raw = dtr_ref[:, here].astype(f32) + dt_bias
        d_raw = d_dt / (1.0 + jnp.exp(-raw))
        gdt_ref[:, here] = d_raw
        d_alog = d_alog - jnp.sum(d_log * dt, axis=1, keepdims=True) * rate
        d_dtb = d_dtb + jnp.sum(d_raw, axis=1, keepdims=True)
    xpack_ref[GAIN : SKIP + 1, :] = chan_ref[0:2, :]
    bcpack_ref[GAIN : SKIP + 1, :] = jnp.zeros((2, bcpack_ref.shape[1]), f32)
    for place, column in enumerate((d_alog, d_dtb)):
        shape = (heads, STRETCH)
        pick = iota(shape, 1) == iota(shape, 0) + group * heads
        row = jnp.sum(jnp.where(pick, jnp.broadcast_to(column, shape), 0.0), axis=0, keepdims=True)
        bcpack_ref[GAIN : GAIN + 1, place * STRETCH : (place + 1) * STRETCH] = row

    def conv_chunk(step, carry):
        conv_backward(
            dx_ext, live, wx_ref, sx_ref, d_x, x_ref, xh_ref, gx_ref, xtail_ref, xpack_ref, rows,
            lanes(step, STRETCH),
        )
        return carry

    repeat(channels // STRETCH, conv_chunk, 0)
    for step in range(2):
        conv_backward(
            dbc_ext, live, wb_ref, sbc_ref, d_bc, bc_ref, bch_ref, gbc_ref, bctail_ref, bcpack_ref,
            rows, slice(step * NSTATE, (step + 1) * NSTATE),
        )


def pack(*refs):
    *pieces, out_ref = refs
    at = 0
    for ref in pieces:
        size = ref.shape[1]
        out_ref[0 : BACK + 1, at : at + size] = ref[0 : BACK + 1, :]
        at += size
    whole = jnp.concatenate([ref[BACK + 1 : PACKED, :] for ref in pieces], axis=1)
    short = out_ref.shape[1] - at
    for row in range(PAD):
        first = row % (PAD // 2) * short
        out_ref[row : row + 1, at:] = whole[row // (PAD // 2) :][0:1, first : first + short]


def unpack_back(value, length):
    short = value.shape[1] - length
    rows = [value[BACK : BACK + 1, 0:length]]
    for half in range(2):
        pieces = [value[half * (PAD // 2) + turn :][0:1, length:] for turn in range(PAD // 2)]
        rows.append(jnp.concatenate(pieces, axis=1))
    return jnp.concatenate(rows, axis=0)


def final_sums(mine_ref, pick_ref, flags_ref, *refs, arrivals, groups, scale):
    arrived, refs = refs[:arrivals], refs[arrivals:]
    tails_x, tails_bc, refs = refs[:groups], refs[groups : 2 * groups], refs[2 * groups :]
    out_wx, out_bx, out_wb, out_bb, out_alog, out_dtb, out_skip, out_gain, ending_ref = refs
    inner = out_wx.shape[1]
    length = ending_ref.shape[1]
    total = mine_ref[0:BACK, 0:length]
    back = jnp.zeros((HALO, length), f32)
    for place, ref in enumerate(arrived):
        value = ref[...].astype(f32)
        total = total + value[0:BACK, 0:length]
        back = back + unpack_back(value, length) * pick_ref[place : place + 1, 0:1]
    total = total * scale
    back = back * tail_factors(flags_ref)
    at = 0
    for ref in tails_x + tails_bc:
        size = ref.shape[1]
        ending_ref[:, at : at + size] = (ref[...] + back[:, at : at + size]).astype(bf16)
        at += size
    out_wx[...] = total[0:CONV, 0:inner]
    out_bx[...] = total[CONV : CONV + 1, 0:inner]
    for which in range(2):
        for group in range(groups):
            first = inner + (2 * group + which) * NSTATE
            to = slice(group * NSTATE, (group + 1) * NSTATE)
            out_wb[:, which, to] = total[0:CONV, first : first + NSTATE]
            out_bb[which : which + 1, to] = total[CONV : CONV + 1, first : first + NSTATE]
    out_gain[...] = total[GAIN : GAIN + 1, 0:inner]
    heads = out_skip.shape[1]
    for out, shift in ((out_alog, 0), (out_dtb, STRETCH)):
        row = None
        for group in range(groups):
            first = inner + 2 * group * NSTATE + shift
            piece = total[GAIN : GAIN + 1, first : first + STRETCH]
            row = piece if row is None else row + piece
        out[...] = row[:, 0:heads]
    lane_sums = jnp.broadcast_to(total[SKIP : SKIP + 1, 0:inner], (PAD, inner))
    shape = (heads, inner)
    pick = (iota(shape, 1) // HEAD_DIM == iota(shape, 0)).astype(f32).astype(bf16)
    high = lane_sums.astype(bf16)
    low = (lane_sums - high.astype(f32)).astype(bf16)
    last = ((1,), (1,))
    out_skip[...] = (dot(high, pick, last) + dot(low, pick, last))[0:1]


def call(kernel, operands, outs, scratch, flops, name, blocked=None, hbm_outs=()):
    operands = [(each + (None,))[:3] for each in operands]
    cuts = [cut or {} for _, cut, _ in operands]
    arrays = [array for array, _, _ in operands]
    stages = [stage for _, _, stage in operands]
    shapes = [jax.ShapeDtypeStruct(shape, dtype) for shape, dtype in outs]
    streamed = [place for place, stage in enumerate(stages) if stage is not None]
    buffers = []
    for place in streamed:
        cut = cuts[place]
        shape = tuple(
            cut[dim].stop - cut[dim].start if dim in cut else extent
            for dim, extent in enumerate(arrays[place].shape)
        )
        buffers.append(pltpu.VMEM(shape, arrays[place].dtype))
    copies_made = sum(len(stages[place]) for place in streamed)

    def body(*refs):
        count, made = len(cuts), len(buffers)
        rest = refs[count:]
        held = dict(zip(streamed, rest[len(rest) - made - 1 : len(rest) - 1])) if made else {}
        sems = rest[-1] if made else None
        seen, copies = [], []
        for place, (ref, cut) in enumerate(zip(refs, cuts)):
            if cut:
                ref = ref.at[tuple(cut.get(dim, slice(None)) for dim in range(len(ref.shape)))]
            if place in held:
                buffer = held[place]
                size = buffer.shape[-1] // len(stages[place])
                for turn, stage in enumerate(stages[place]):
                    part = (slice(None),) * (len(buffer.shape) - 1) + (
                        slice(turn * size, (turn + 1) * size),
                    )
                    copy = (stage, (ref.at[part], buffer.at[part], sems.at[len(copies)]))
                    copies.append(copy)
                ref = buffer
            seen.append(ref)
        for _, copy in sorted(copies, key=lambda each: each[0]):
            pltpu.make_async_copy(*copy).start()

        def ready(stage):
            for which, copy in copies:
                if which == stage:
                    pltpu.make_async_copy(*copy).wait()

        if made:
            kernel(*seen, *rest[: len(rest) - made - 1], ready=ready)
        else:
            kernel(*seen, *rest)

    def block_of(array, cut):
        shape, index = [], []
        for dim, extent in enumerate(array.shape):
            part = cut.get(dim, slice(0, extent))
            size = part.stop - part.start
            shape.append(size)
            index.append(part.start // size)
        return pl.BlockSpec(tuple(shape), functools.partial(lambda fixed, i: fixed, tuple(index)))

    in_vmem = pl.BlockSpec(memory_space=pltpu.VMEM)
    in_hbm = pl.BlockSpec(memory_space=pltpu.HBM)
    scratch_shapes = [
        pltpu.VMEM(each, f32) if isinstance(each, tuple) else each for each in scratch
    ]
    if blocked:
        grid, limit = {"grid": (1,)}, blocked
        in_specs = [block_of(array, cut) for array, cut in zip(arrays, cuts)]
        out_specs = [block_of(shape, {}) for shape in shapes]
    else:
        grid, limit = {}, STREAM_LIMIT if buffers else VMEM_LIMIT
        in_specs = [in_vmem if stage is None else in_hbm for stage in stages]
        out_specs = [in_hbm if place in hbm_outs else in_vmem for place in range(len(shapes))]
        if buffers:
            scratch_shapes += buffers + [pltpu.SemaphoreType.DMA((copies_made,))]
    count = sum(each.size * each.dtype.itemsize for each in arrays + shapes)
    return pl.pallas_call(
        kernel if blocked else body,
        in_specs=in_specs,
        out_specs=out_specs,
        out_shape=shapes,
        scratch_shapes=scratch_shapes,
        compiler_params=pltpu.CompilerParams(vmem_limit_bytes=limit),
        cost_estimate=pl.CostEstimate(flops=flops, bytes_accessed=count, transcendentals=0),
        name=name,
        **grid,
    )(*arrays)


def together(*values):
    return lax.optimization_barrier(values)


def chain(parts, decays, axis, backward, fillers):
    count = lax.axis_size(axis)
    zero = [jnp.zeros(part.shape, bf16) for part in parts]
    early, last = list(zero), list(zero)
    results = []
    for hop in range(count - 1):
        pairs = [(count - 1 - hop, count - 2 - hop)] if backward else [(hop, hop + 1)]
        leaving = list(parts)
        if hop > 0:
            for place, part in enumerate(parts):
                if place:
                    last[place] = together(last[place], leaving[place - 1])[0]
                early[place] = early[place] + last[place] if hop > 1 else last[place]
                arrived = early[place].astype(f32)
                leaving[place] = (decays[place] * arrived + part.astype(f32)).astype(bf16)
        filler = fillers[hop - 1] if 0 < hop <= len(fillers) else None
        if filler:
            work, array = filler
            array = together(array, *leaving)[0]
        last = [lax.ppermute(each, axis, pairs) for each in leaving]
        if filler:
            done = work(array)
            last[0], *done = together(last[0], *done)
            results.append(done)
    for work, array in fillers[len(results) :]:
        results.append(work(array))
    return list(zip(early, last)), results


def exchange_terms(value, axis):
    count = lax.axis_size(axis)
    other = jnp.zeros_like(value)
    stride = 1
    while stride < count:
        value = value + other if stride > 1 else value
        other = lax.ppermute(value, axis, [(i, i ^ stride) for i in range(count)])
        stride *= 2
    return value, other


def per_device(
    x_raw, bc_raw, z_gate, dt_raw, resets, conv_x_weight, conv_x_bias, conv_bc_weight,
    conv_bc_bias, a_log, dt_bias, skip_weight, norm_gain, grad_out,
):
    rows, inner = x_raw.shape[1:]
    groups = bc_raw.shape[3] // NSTATE
    heads = a_log.shape[0] // groups
    channels = inner // groups
    blocks = rows // STRETCH
    width = 2 * NSTATE

    def by_group(value):
        lead = value.shape[:-2]
        split = value.reshape(lead + (2, groups, NSTATE))
        return jnp.moveaxis(split, -3, -2).reshape(lead + (groups * width,))

    x_own, z_own, go_own, dt_own = x_raw[0], z_gate[0], grad_out[0], dt_raw[0]
    bc_own = by_group(bc_raw[0])
    flags = resets
    count = lax.axis_size("ctx")
    sent = call(
        tails,
        [
            (x_raw, {1: slice(rows - 16, rows)}, [0]),
            (bc_raw, {1: slice(rows - 16, rows)}, [0]),
            (flags, {1: slice(rows - STRETCH, rows)}, [0]),
        ],
        [((HALO, inner + groups * width), f32)],
        [],
        rows,
        "tails",
    )[0]
    halo = lax.ppermute(sent, "ctx", [(i, i + 1) for i in range(count - 1)])
    head_rows = jnp.stack([a_log, dt_bias, skip_weight])
    head_rows = jnp.pad(head_rows, ((0, PAD - 3), (0, -head_rows.shape[1] % STRETCH)))
    bx, gain = conv_x_bias[None], norm_gain[None]
    wb, bb = by_group(conv_bc_weight), by_group(conv_bc_bias)[None]

    def wide(array, group):
        return (array, {1: slice(group * channels, (group + 1) * channels)})

    def narrow(array, group, first=0):
        return (array, {1: slice(first + group * width, first + (group + 1) * width)})

    def per_head(array, group):
        return (array, {0: slice(group * heads, (group + 1) * heads)})

    def whole(array):
        return (array, None)

    keep_rows = -(-blocks // PAD) * PAD
    tall, thin, row_shape = (rows, channels), (rows, width), (heads, rows)
    state_shape = (NSTATE, channels)
    piece_shape = (NSTATE, channels // PIECES)
    local_shape = (blocks - 1, NSTATE, channels)
    clear_shape, live_shape = (rows + PAD, STRETCH), (HALO, rows + 2 * PAD, STRETCH)
    wide_scratch = (STRETCH, channels)
    run_scratch = [(STRETCH, heads * STRETCH), (heads * PAD, STRETCH)]
    work = rows * channels * STRETCH
    group_range = range(groups)
    here = lax.axis_index("ctx")
    picks = [(here ^ shift) == here + 1 for shift in range(1, count)]
    pick = jnp.broadcast_to(jnp.stack(picks).astype(f32)[:, None], (count - 1, STRETCH))
    flags, pick = together(flags, pick)
    held = []
    flags_now = flags
    for g in group_range:
        if held:
            flags_now = together(flags, held[-1][-1])[0]
        held.append(
            call(
                functools.partial(conv_and_state, group=g),
                [
                    wide(x_own, g), wide(halo, g), narrow(bc_own, g), narrow(halo, g, inner),
                    wide(conv_x_weight, g), wide(bx, g), narrow(wb, g), narrow(bb, g),
                    per_head(dt_own, g), whole(head_rows), whole(flags_now),
                ],
                [
                    (tall, bf16), (tall, bf16), (tall, f32), (thin, bf16), (thin, f32),
                    (row_shape, f32), ((keep_rows, channels), f32), (local_shape, bf16),
                ]
                + [(piece_shape, bf16)] * PIECES
                + [((1, channels // PIECES), f32)] * PIECES,
                [
                    (rows + PAD, channels), (rows + PAD, width), clear_shape, live_shape,
                    wide_scratch, wide_scratch, state_shape,
                ],
                2 * work,
                "conv_and_state",
            )
        )
    xc, xp, ux, bcc, ubc, run, keep, s_loc, *pieces = zip(*held)
    s_dev, decay = pieces[:PIECES], pieces[PIECES:]

    def in_a_row(pieces):
        return [piece[g] for g in group_range for piece in pieces]

    def by_pieces(pairs):
        return [
            [pair[term] for term in range(2) for pair in pairs[g * PIECES : (g + 1) * PIECES]]
            for g in group_range
        ]


    def forward_work(g):
        return lambda bcc_now: call(
            within_blocks,
            [
                whole(xp[g]), whole(bcc_now), whole(run[g]), whole(flags), whole(ux[g]), whole(ubc[g]),
            ],
            [(tall, f32), (tall, f32), (thin, f32)],
            run_scratch,
            6 * work,
            "within_blocks",
        )

    prior, held = chain(
        in_a_row(s_dev), in_a_row(decay), "ctx", False, [(forward_work(g), bcc[g]) for g in group_range]
    )
    prior = by_pieces(prior)
    y_within, slope_x, slope_bc = zip(*held)
    held, sums = [], ()
    for g in group_range:
        bundle, total = call(
            functools.partial(gate_forward, group=g),
            [
                whole(y_within[g]), whole(s_loc[g]), whole(keep[g]), whole(bcc[g]), whole(run[g]),
                whole(flags), whole(xc[g]), whole(head_rows), wide(z_own, g), wide(go_own, g),
                wide(gain, g),
            ]
            + [whole(each) for each in prior[g]]
            + [whole(each) for each in sums],
            [((bundle_rows(rows)[-1], channels), f32), ((2, rows), f32)],
            [wide_scratch, (PAD, channels)],
            2 * work,
            "gate_forward",
        )
        sums = (total,)
        held.append(bundle)
    bundle = held
    own, other = exchange_terms(sums[0], "head")
    held = []
    for g in group_range:
        bundle_now = together(bundle[g], held[-1][-1])[0] if held else bundle[g]
        held.append(
            call(
                functools.partial(gate_backward, heads=heads),
                [whole(own), whole(other), whole(bundle_now), wide(z_own, g), wide(go_own, g)],
                [(tall, bf16), (local_shape, bf16), ((2, rows), f32), (tall, f32)]
                + [(piece_shape, bf16)] * PIECES,
                [wide_scratch, state_shape],
                2 * work,
                "gate_backward",
            )
        )
    dy, a_loc, totals, y_all, *a_dev = zip(*held)

    def backward_work(g):
        return lambda bcc_now: call(
            functools.partial(within_backward, group=g),
            [
                whole(totals[g]), whole(y_all[g]), wide(z_own, g), wide(go_own, g), wide(gain, g),
                whole(dy[g]), whole(xc[g]), whole(xp[g]), whole(bcc_now),
                whole(run[g]), whole(flags), whole(s_loc[g]), whole(keep[g]), whole(head_rows),
            ]
            + [whole(each) for each in prior[g]],
            [
                (tall, bf16), (tall, f32), (thin, f32), (row_shape, f32), ((PAD, channels), f32),
            ],
            run_scratch + [wide_scratch, (PAD, channels)],
            10 * work,
            "within_backward",
            BLOCKED_LIMIT,
        )

    later, held = chain(
        in_a_row(a_dev), in_a_row(decay), "ctx", True, [(backward_work(g), bcc[g]) for g in group_range]
    )
    later = by_pieces(later)
    gz, dxp, dbc, drun, chan = zip(*held)
    held = []
    for g in group_range:
        rows_now = together(head_rows, held[-1][-1])[0] if held else head_rows
        held.append(call(
            functools.partial(finish_backward, group=g),
            [
                whole(a_loc[g]), whole(s_loc[g]), whole(keep[g]), whole(dxp[g]), whole(dbc[g]),
                whole(drun[g]), whole(xp[g]), whole(dy[g]), whole(bcc[g]), whole(run[g]),
                whole(flags), whole(slope_x[g]), whole(slope_bc[g]), wide(x_own, g),
                wide(halo, g), narrow(bc_own, g), narrow(halo, g, inner), wide(conv_x_weight, g),
                narrow(wb, g), whole(rows_now), per_head(dt_own, g), whole(chan[g]),
            ]
            + [whole(each) for each in later[g] + prior[g]],
            [
                (tall, bf16), ((HALO, channels), f32), ((PACKED, channels), f32), (thin, bf16),
                ((HALO, width), f32), ((PACKED, width), f32), (row_shape, f32),
            ],
            [
                clear_shape, live_shape, (rows + 2 * PAD, channels), (rows + 2 * PAD, width), tall,
                thin, wide_scratch, wide_scratch, (PAD, channels), (PAD, channels),
            ],
            4 * work,
            "finish_backward",
            BLOCKED_LIMIT,
        ))
    gx, x_tail, x_pack, gbc, bc_tail, bc_pack, gdt = zip(*held)

    def joined(pieces):
        return jnp.concatenate(pieces, axis=1)

    def ungroup(value):
        lead = value.shape[:-1]
        split = value.reshape(lead + (groups, 2, NSTATE))
        return jnp.moveaxis(split, -3, -2).reshape(lead + (2, groups * NSTATE))

    length = inner + groups * width
    packed = call(
        pack,
        [whole(each) for each in x_pack + bc_pack],
        [((PAD, length + 2 * length // PAD), f32)],
        [],
        rows,
        "pack",
    )[0]
    mine = packed
    own_rows = np.ones((PAD, packed.shape[1]), np.float32)
    own_rows[BACK:] = 0.0
    own_rows[:, length:] = 0.0
    for shift in range(1, lax.axis_size("dp")):
        size = lax.axis_size("dp")
        other = lax.ppermute(packed, "dp", [(i, (i + shift) % size) for i in range(size)])
        mine = mine + other * own_rows
    leaving = mine.astype(bf16)
    arrived = [
        lax.ppermute(leaving, "ctx", [(i, i ^ shift) for i in range(count)])
        for shift in range(1, count)
    ]
    out_wx, out_bx, out_wb, out_bb, out_alog, out_dtb, out_skip, out_gain, ending = call(
        functools.partial(
            final_sums,
            arrivals=count - 1,
            groups=groups,
            scale=float(lax.axis_size("dp") * count * rows) ** (-0.5),
        ),
        [whole(mine), whole(pick), whole(flags)]
        + [whole(each) for each in arrived]
        + [whole(each) for each in x_tail + bc_tail],
        [
            ((CONV, inner), f32), ((1, inner), f32), ((CONV, 2, groups * NSTATE), f32),
            ((2, groups * NSTATE), f32),
            ((1, groups * heads), f32), ((1, groups * heads), f32), ((1, groups * heads), f32),
            ((1, inner), f32), ((HALO, inner + groups * width), bf16),
        ],
        [],
        rows * inner,
        "final_sums",
    )
    grad_x = lax.dynamic_update_slice(joined(gx), ending[:, :inner], (rows - HALO, 0))
    grad_bc = lax.dynamic_update_slice(
        ungroup(joined(gbc)), ungroup(ending[:, inner:]), (rows - HALO, 0, 0)
    )
    return (
        grad_x[None],
        grad_bc[None],
        joined(gz)[None],
        jnp.concatenate(gdt, axis=0)[None],
        out_wx,
        out_bx[0],
        out_wb,
        out_bb,
        out_alog[0],
        out_dtb[0],
        out_skip[0],
        out_gain[0],
    )


def solution(mesh):
    return jax.shard_map(
        per_device,
        mesh=mesh,
        in_specs=(
            P("dp", "ctx", "head"),
            P("dp", "ctx", None, "head"),
            P("dp", "ctx", "head"),
            P("dp", "head", "ctx"),
            P("dp", "ctx"),
            P(None, "head"),
            P("head"),
            P(None, None, "head"),
            P(None, "head"),
            P("head"),
            P("head"),
            P("head"),
            P("head"),
            P("dp", "ctx", "head"),
        ),
        out_specs=(
            P("dp", "ctx", "head"),
            P("dp", "ctx", None, "head"),
            P("dp", "ctx", "head"),
            P("dp", "head", "ctx"),
            P(None, "head"),
            P("head"),
            P(None, None, "head"),
            P(None, "head"),
            P("head"),
            P("head"),
            P("head"),
            P("head"),
        ),
        check_vma=False,
    )
```

```python
import functools

import jax
import jax.numpy as jnp
import numpy as np
from jax import lax
from jax.experimental import pallas as pl
from jax.experimental.pallas import tpu as pltpu
from jax.sharding import PartitionSpec as P

HEAD_DIM = 64
NSTATE = 128
CONV = 4
STRETCH = 128
INNER = 8192
HALO = CONV - 1
PAD = 8
CHUNK = 256
PAIR = 2 * HEAD_DIM
NORM_EPS = 1e-05
LOWEST = -1e30
GAIN, SKIP, BACK = CONV + 1, CONV + 2, CONV + 3
PACKED = BACK + HALO
A_LOG, DT_BIAS, SKIP_WEIGHT = range(3)
STAGES = 2
STREAM_LIMIT = 62 * 1024 * 1024
PIECES = 2
BLOCKED_LIMIT = 40 * 1024 * 1024
VMEM_LIMIT = 24 * 1024 * 1024

f32 = jnp.float32
bf16 = jnp.bfloat16


def dot(a, b, contract=((1,), (0,))):
    return lax.dot_general(a, b, (contract, ((), ())), preferred_element_type=f32)


def dot_full(a, b):
    return lax.dot_general(
        a, b, (((1,), (0,)), ((), ())), precision=lax.Precision.HIGHEST, preferred_element_type=f32
    )


def iota(shape, dim):
    return lax.broadcasted_iota(jnp.int32, shape, dim)


def split3(value):
    high = value.astype(bf16)
    rest = value - high.astype(f32)
    middle = rest.astype(bf16)
    low = (rest - middle.astype(f32)).astype(bf16)
    return jnp.concatenate([high, middle, low], axis=0)


def spread_heads(rows, width):
    heads = rows.shape[0]
    shape = (heads, heads * width)
    pick = (iota(shape, 1) // width == iota(shape, 0)).astype(f32).astype(bf16)
    return dot(split3(rows), jnp.concatenate([pick] * 3, axis=0), ((0,), (0,)))


def head_sums(value, first):
    shape = (value.shape[1], STRETCH)
    pick = ((iota(shape, 0) + first) // HEAD_DIM == iota(shape, 1)).astype(f32).astype(bf16)
    high = value.astype(bf16)
    low = (value - high.astype(f32)).astype(bf16)
    both = dot(jnp.concatenate([high, low], axis=0), pick)
    return both[: value.shape[0]] + both[value.shape[0] :]


def as_columns(row):
    return jnp.transpose(jnp.broadcast_to(row, (STRETCH, STRETCH)))


def sigmoid(value):
    return 0.5 * jnp.tanh(0.5 * value) + 0.5


def upper_ones():
    shape = (STRETCH, STRETCH)
    return (iota(shape, 0) <= iota(shape, 1)).astype(f32)


def resets_seen(flags_row):
    flags = jnp.broadcast_to(flags_row.astype(f32), (PAD, STRETCH)).astype(bf16)
    return dot(flags, upper_ones().astype(bf16))[0:1]


def decay_mask(seen):
    shape = (STRETCH, STRETCH)
    same = (as_columns(seen) == jnp.broadcast_to(seen, shape)) & (iota(shape, 0) >= iota(shape, 1))
    return jnp.where(same, 0.0, LOWEST)


def lanes(position, size):
    return slice(position * size, (position + 1) * size)


def repeat(count, body, carry):
    for step in range(count):
        carry = body(step, carry)
    return carry


def piece_of(refs, part):
    width = refs[0].shape[1]
    ref = refs[part.start // width]
    return ref[:, part.start % width : part.start % width + part.stop - part.start]


def to_column(row, first, heads):
    shape = (heads, row.shape[1])
    pick = iota(shape, 1) == iota(shape, 0) + first
    return jnp.sum(jnp.where(pick, jnp.broadcast_to(row, shape), 0.0), axis=1, keepdims=True)


def over_channels(column):
    return spread_heads(jnp.broadcast_to(column, (column.shape[0], STRETCH)), HEAD_DIM)[0:1]


def softplus(value):
    small = jnp.exp(-jnp.abs(value))
    series = small * (1.0 - small * (1 / 2 - small * (1 / 3 - small * (1 / 4 - small * (1 / 5)))))
    return jnp.maximum(value, 0.0) + jnp.where(small < 0.03, series, jnp.log(1.0 + small))


def head_column(rows_ref, which, group, heads):
    return to_column(rows_ref[which : which + 1, :], group * heads, heads)


def step_sizes(dtr_ref, rows_ref, group):
    heads = dtr_ref.shape[0]
    return softplus(dtr_ref[...].astype(f32) + head_column(rows_ref, DT_BIAS, group, heads))


def to_end_factor(running, seen):
    final = running[:, STRETCH - 1 : STRETCH]
    return jnp.where(seen == seen[:, STRETCH - 1 : STRETCH], jnp.exp(final - running), 0.0)


def doubled(value):
    return jnp.concatenate([value, value], axis=1)


def fill_live(flags_ref, clear, live):
    rows = flags_ref.shape[1]
    clear[0:PAD, :] = jnp.ones((PAD, STRETCH), f32)
    for first in range(0, rows, STRETCH):
        flags = flags_ref[:, first : first + STRETCH].astype(f32)
        clear[PAD + first : PAD + first + STRETCH, :] = as_columns(1.0 - flags)
    for first in range(0, rows, STRETCH):
        begin = PAD + first
        product = clear[begin : begin + STRETCH, :]
        live[0, begin : begin + STRETCH, :] = product
        for lag in range(2, CONV):
            product = product * clear[begin - lag + 1 : begin - lag + 1 + STRETCH, :]
            live[lag - 1, begin : begin + STRETCH, :] = product


def fill_extended(extended, halo_ref, rows_ref):
    for tile in range(extended.shape[0]):
        part = lanes(tile, STRETCH)
        extended[tile, PAD - HALO : PAD, :] = halo_ref[:, part]
        extended[tile, PAD:, :] = rows_ref[:, part].astype(f32)


def conv_total(extended, live, weight_ref, bias_ref, first, part):
    begin = PAD + first
    totals = []
    for tile in range(part.start // STRETCH, part.stop // STRETCH):
        cut = lanes(tile, STRETCH)
        total = bias_ref[0:1, cut] + weight_ref[0:1, cut] * extended[tile, begin : begin + STRETCH, :]
        for lag in range(1, CONV):
            total = total + weight_ref[lag : lag + 1, cut] * (
                extended[tile, begin - lag : begin - lag + STRETCH, :]
                * live[lag - 1, begin : begin + STRETCH, :]
            )
        totals.append(total)
    return totals[0] if len(totals) == 1 else jnp.concatenate(totals, axis=1)


def tail_factors(flags_ref):
    flags = flags_ref[:, flags_ref.shape[1] - STRETCH :].astype(f32)
    clear = as_columns(1.0 - flags)
    last = clear[STRETCH - 1 :]
    both = last * clear[STRETCH - 2 : STRETCH - 1]
    return jnp.concatenate([both, last, jnp.ones_like(last)], axis=0)[:, 0:1]


def tails(x_ref, bc_ref, flags_ref, out_ref, *, ready):
    ready(0)
    keep = tail_factors(flags_ref)
    inner = x_ref.shape[2]
    out_ref[:, 0:inner] = x_ref[0].astype(f32)[x_ref.shape[1] - HALO :] * keep
    groups = bc_ref.shape[3] // NSTATE
    for which in range(2):
        rows = bc_ref[0, :, which, :].astype(f32)[bc_ref.shape[1] - HALO :] * keep
        for group in range(groups):
            first = inner + (2 * group + which) * NSTATE
            out_ref[:, first : first + NSTATE] = rows[:, group * NSTATE : (group + 1) * NSTATE]


def conv_and_state(
    x_ref, xh_ref, bc_ref, bch_ref, wx_ref, bx_ref, wb_ref, bb_ref, dtr_ref, rows_ref,
    flags_ref, xc_ref, xp_ref, ux_ref, bcc_ref, ubc_ref, run_ref, keep_ref, sloc_ref, *refs, group,
):
    sdev_refs, decay_refs = refs[:PIECES], refs[PIECES : 2 * PIECES]
    x_ext, bc_ext, clear, live, dt_wide, end_wide, state = refs[2 * PIECES :]
    rows, channels = x_ref.shape
    heads = dtr_ref.shape[0]
    fill_extended(x_ext, xh_ref, x_ref)
    fill_extended(bc_ext, bch_ref, bc_ref)
    fill_live(flags_ref, clear, live)
    blocks = rows // STRETCH
    rate = jnp.exp(head_column(rows_ref, A_LOG, group, heads))
    dt_all = step_sizes(dtr_ref, rows_ref, group)
    product = None
    for block in range(blocks):
        first = block * STRETCH
        here = slice(first, first + STRETCH)
        every = slice(0, 2 * NSTATE)
        total = conv_total(bc_ext, live, wb_ref, bb_ref, first, every)
        ubc_ref[here, :] = total
        bc_now = (total * sigmoid(total)).astype(bf16)
        bcc_ref[here, :] = bc_now
        b_turned = jnp.transpose(bc_now[:, 0:NSTATE].astype(f32)).astype(bf16)
        seen = resets_seen(flags_ref[:, here])
        dt = dt_all[:, here]
        running = dot_full(-rate * dt, upper_ones())
        run_ref[:, here] = running
        final = running[:, STRETCH - 1 : STRETCH]
        keep = jnp.where(seen[:, STRETCH - 1 : STRETCH] == 0.0, jnp.exp(final), 0.0)
        keep_row = over_channels(keep)
        keep_ref[block : block + 1, :] = keep_row
        product = keep_row if product is None else product * keep_row
        dt_wide[...] = spread_heads(dt, HEAD_DIM)
        end_wide[...] = spread_heads(to_end_factor(running, seen), HEAD_DIM)

        def chunk(step, carry):
            part = lanes(step, CHUNK)
            total = conv_total(x_ext, live, wx_ref, bx_ref, first, part)
            ux_ref[here, part] = total
            xc = (total * sigmoid(total)).astype(bf16)
            xc_ref[here, part] = xc
            stepped = (xc.astype(f32) * dt_wide[:, part]).astype(bf16)
            xp_ref[here, part] = stepped
            ended = (stepped.astype(f32) * end_wide[:, part]).astype(bf16)
            fresh = dot(b_turned, ended)
            if block > 0:
                fresh = keep_ref[block : block + 1, part] * state[:, part] + fresh
            if block < blocks - 1:
                state[:, part] = fresh
                sloc_ref[block, :, part] = fresh.astype(bf16)
            else:
                put_piece(sdev_refs, part, fresh.astype(bf16))
            return carry

        repeat(channels // CHUNK, chunk, 0)
    for place, ref in enumerate(decay_refs):
        size = ref.shape[1]
        ref[...] = product[:, place * size : (place + 1) * size]


def place_runs(run_ref, here, run_wide, run_tall):
    running = run_ref[:, here]
    run_wide[...] = spread_heads(running, STRETCH)
    for head in range(running.shape[0]):
        run_tall[head * PAD : (head + 1) * PAD, :] = jnp.broadcast_to(
            running[head : head + 1], (PAD, STRETCH)
        )


def block_weights(scores, mask, run_wide, run_tall, head):
    column = run_wide[:, lanes(head, STRETCH)]
    row = run_tall[head * PAD : head * PAD + 1, :]
    segment = jnp.exp(column - row + mask)
    return segment, (scores * segment).astype(bf16)


def both_heads(value):
    is_first = iota(value.shape, 1) < HEAD_DIM
    wide = value.astype(f32)
    zero = jnp.zeros_like(wide)
    return jnp.concatenate(
        [jnp.where(is_first, wide, zero).astype(bf16), jnp.where(is_first, zero, wide).astype(bf16)],
        axis=0,
    )


def put_piece(refs, part, value):
    width = refs[0].shape[1]
    ref = refs[part.start // width]
    ref[:, part.start % width : part.start % width + part.stop - part.start] = value


def slope_of(total):
    up = sigmoid(total)
    return up + total * up * (1.0 - up)


def within_blocks(
    xp_ref, bcc_ref, run_ref, flags_ref, ux_ref, ubc_ref, y_ref, sx_ref, sbc_ref, run_wide, run_tall
):
    rows, channels = xp_ref.shape
    for block in range(rows // STRETCH):
        here = slice(block * STRETCH, (block + 1) * STRETCH)
        mask = decay_mask(resets_seen(flags_ref[:, here]))
        scores = dot(bcc_ref[here, NSTATE:], bcc_ref[here, 0:NSTATE], ((1,), (1,)))
        place_runs(run_ref, here, run_wide, run_tall)
        sbc_ref[here, :] = slope_of(ubc_ref[here, :])

        def pair(step, carry):
            _, w_first = block_weights(scores, mask, run_wide, run_tall, 2 * step)
            _, w_second = block_weights(scores, mask, run_wide, run_tall, 2 * step + 1)
            part = lanes(step, PAIR)
            y_ref[here, part] = dot(
                jnp.concatenate([w_first, w_second], axis=1), both_heads(xp_ref[here, part])
            )
            sx_ref[here, part] = slope_of(ux_ref[here, part])
            return carry

        repeat(channels // PAIR, pair, 0)


def start_factor(run_ref, flags_ref, here):
    seen = resets_seen(flags_ref[:, here])
    return jnp.where(seen == 0.0, jnp.exp(run_ref[:, here]), 0.0)


def block_state(block, prior_ref, sloc_ref, keep_ref, part):
    state = piece_of(prior_ref[:PIECES], part) + piece_of(prior_ref[PIECES:], part)
    if block == 0:
        return state
    whole = keep_ref[0:1, part]
    for step in range(1, block):
        whole = whole * keep_ref[step : step + 1, part]
    return (whole * state.astype(f32) + sloc_ref[block - 1, :, part].astype(f32)).astype(bf16)


def bundle_rows(rows):
    places = [rows]
    for size in (PAD, PAD, 2 * PAD, NSTATE // 4):
        places.append(places[-1] + size)
    return places


def gate_forward(
    y_ref, sloc_ref, keep_ref, bcc_ref, run_ref, flags_ref, xc_ref, rows_ref, z_ref, go_ref, gain_ref,
    *refs, group,
):
    prior_ref, refs = refs[: 2 * PIECES], refs[2 * PIECES :]
    *before, bundle_ref, sums_ref, start_wide, skip_wide = refs
    rows, channels = xc_ref.shape
    heads = run_ref.shape[0]
    at_keep, at_gain, at_start, at_turned, _ = bundle_rows(rows)
    bundle_ref[at_keep:at_gain, :] = keep_ref[0:PAD, :]
    bundle_ref[at_gain:at_start, :] = jnp.broadcast_to(gain_ref[...], (PAD, channels))
    skip_wide[0:1, :] = over_channels(head_column(rows_ref, SKIP_WEIGHT, group, heads))
    quarter = NSTATE // 4
    for block in range(rows // STRETCH):
        here = slice(block * STRETCH, (block + 1) * STRETCH)
        start = start_factor(run_ref, flags_ref, here)
        bundle_ref[at_start : at_start + heads, here] = start
        start_wide[...] = spread_heads(start, HEAD_DIM)
        c_now = bcc_ref[here, NSTATE:]
        turned = jnp.transpose(c_now.astype(f32))
        for turn in range(4):
            first = turn * rows + block * STRETCH
            bundle_ref[at_turned : at_turned + quarter, first : first + STRETCH] = turned[
                turn * quarter : (turn + 1) * quarter
            ]

        def chunk(step, carry):
            squares, products = carry
            part = lanes(step, CHUNK)
            carried = dot(c_now, block_state(block, prior_ref, sloc_ref, keep_ref, part))
            y_now = y_ref[here, part] + carried * start_wide[:, part]
            y_now = y_now + skip_wide[0:1, part] * xc_ref[here, part].astype(f32)
            bundle_ref[here, part] = y_now
            z = z_ref[here, part].astype(f32)
            gated = y_now.astype(bf16).astype(f32) * (z * sigmoid(z))
            gained = go_ref[here, part].astype(f32) * gain_ref[0:1, part]
            return squares + gated * gated, products + gated * gained

        zero = jnp.zeros((STRETCH, CHUNK), f32)
        squares, products = repeat(channels // CHUNK, chunk, (zero, zero))
        square_column = jnp.sum(squares, axis=1, keepdims=True)
        product_column = jnp.sum(products, axis=1, keepdims=True)
        shape = (STRETCH, STRETCH)
        both = jnp.where(
            iota(shape, 1) == 0,
            jnp.broadcast_to(square_column, shape),
            jnp.broadcast_to(product_column, shape),
        )
        total = jnp.transpose(both)[0:2]
        for ref in before:
            total = total + ref[:, here]
        sums_ref[:, here] = total


def norm_factors(totals_ref, here):
    squares = totals_ref[0:1, here]
    products = totals_ref[1:2, here]
    inv_rms = lax.rsqrt(squares * (1.0 / INNER) + NORM_EPS)
    pull = inv_rms * inv_rms * inv_rms * products * (1.0 / INNER)
    return doubled(as_columns(inv_rms)), doubled(as_columns(pull))


def gate_backward(
    own_ref, other_ref, bundle_ref, z_ref, go_ref, dy_ref, aloc_ref, totals_ref, y_ref, *refs, heads,
):
    adev_refs, (start_wide, adjoint) = refs[:PIECES], refs[PIECES:]
    rows, channels = z_ref.shape
    blocks = rows // STRETCH
    at_keep, at_gain, at_start, at_turned, end = bundle_rows(rows)
    totals_ref[...] = own_ref[...] + other_ref[...]
    for block in reversed(range(blocks)):
        here = slice(block * STRETCH, (block + 1) * STRETCH)
        start_wide[...] = spread_heads(bundle_ref[at_start : at_start + heads, here], HEAD_DIM)
        inv_rms, pull = norm_factors(totals_ref, here)
        firsts = [turn * rows + block * STRETCH for turn in range(4)]
        c_turned = jnp.concatenate(
            [bundle_ref[at_turned:end, first : first + STRETCH] for first in firsts], axis=0
        ).astype(bf16)

        def chunk(step, carry):
            part = lanes(step, CHUNK)
            z = z_ref[here, part].astype(f32)
            gate = z * sigmoid(z)
            gained = go_ref[here, part].astype(f32) * bundle_ref[at_gain : at_gain + 1, part]
            y_now = bundle_ref[here, part]
            y_ref[here, part] = y_now
            mixed = y_now.astype(bf16).astype(f32)
            d_gated = gained * inv_rms - mixed * gate * pull
            dy = (d_gated * gate).astype(bf16)
            dy_ref[here, part] = dy
            fresh = dot(c_turned, (dy.astype(f32) * start_wide[:, part]).astype(bf16))
            if block < blocks - 1:
                keep = bundle_ref[at_keep + block : at_keep + block + 1, part]
                fresh = fresh + keep * adjoint[:, part]
            if block > 0:
                adjoint[:, part] = fresh
                aloc_ref[block - 1, :, part] = fresh.astype(bf16)
            else:
                put_piece(adev_refs, part, fresh.astype(bf16))
            return carry

        repeat(channels // CHUNK, chunk, 0)


def within_backward(
    totals_ref, y_ref, z_ref, go_ref, gain_ref, dy_ref, xc_ref, xp_ref, bcc_ref, run_ref, flags_ref,
    sloc_ref, keep_ref, rows_ref, sx_ref, dtr_ref, *refs, group,
):
    prior_ref, refs = refs[: 2 * PIECES], refs[2 * PIECES :]
    gz_ref, dux_ref, dts_ref, ended_ref, dbc_ref, drun_ref, step_ref, chan_ref, *refs = refs
    run_wide, run_tall, start_wide, skip_wide, dt_wide, end_wide = refs
    rows, channels = xc_ref.shape
    heads = run_ref.shape[0]
    skip_wide[0:1, :] = over_channels(head_column(rows_ref, SKIP_WEIGHT, group, heads))
    chan_ref[...] = jnp.zeros_like(chan_ref)
    dt_all = step_sizes(dtr_ref, rows_ref, group)
    for block in range(rows // STRETCH):
        here = slice(block * STRETCH, (block + 1) * STRETCH)
        seen = resets_seen(flags_ref[:, here])
        mask = decay_mask(seen)
        dt_wide[...] = spread_heads(dt_all[:, here], HEAD_DIM)
        end_wide[...] = spread_heads(to_end_factor(run_ref[:, here], seen), HEAD_DIM)
        b_now = bcc_ref[here, 0:NSTATE]
        c_now = bcc_ref[here, NSTATE:]
        scores = dot(c_now, b_now, ((1,), (1,)))
        place_runs(run_ref, here, run_wide, run_tall)
        start_wide[...] = spread_heads(start_factor(run_ref, flags_ref, here), HEAD_DIM)
        inv_rms, pull = norm_factors(totals_ref, here)

        def chunk(step, carry):
            d_c, d_run = carry
            part = lanes(step, CHUNK)
            z = z_ref[here, part].astype(f32)
            gate_up = sigmoid(z)
            gate = z * gate_up
            go = go_ref[here, part].astype(f32)
            xc = xc_ref[here, part].astype(f32)
            y_now = y_ref[here, part]
            y_ssd = y_now - skip_wide[0:1, part] * xc
            mixed = y_now.astype(bf16).astype(f32)
            gated = mixed * gate
            d_gated = go * gain_ref[0:1, part] * inv_rms - gated * pull
            slope = gate_up + gate * (1.0 - gate_up)
            gz_ref[here, part] = (d_gated * mixed * slope).astype(bf16)
            dy = dy_ref[here, part].astype(f32)
            chan_ref[0:1, part] += jnp.sum(go * gated * inv_rms, axis=0, keepdims=True)
            chan_ref[1:2, part] += jnp.sum(dy * xc, axis=0, keepdims=True)
            d_run = d_run + head_sums(dy * y_ssd, step * CHUNK)
            started = (dy * start_wide[:, part]).astype(bf16)
            state = block_state(block, prior_ref, sloc_ref, keep_ref, part)
            return d_c + dot(started, state, ((1,), (1,))), d_run

        d_c, d_run = repeat(
            channels // CHUNK,
            chunk,
            (jnp.zeros((STRETCH, NSTATE), f32), jnp.zeros((STRETCH, STRETCH), f32)),
        )
        drun_ref[:, here] = jnp.transpose(d_run)[0:heads]

        def pair(step, carry):
            d_scores, per_step = carry
            part = lanes(step, PAIR)
            s_first, w_first = block_weights(scores, mask, run_wide, run_tall, 2 * step)
            s_second, w_second = block_weights(scores, mask, run_wide, run_tall, 2 * step + 1)
            dy = dy_ref[here, part]
            d_weights = dot(dy, both_heads(xp_ref[here, part]), ((1,), (1,)))
            d_stepped = dot(
                jnp.concatenate([w_first, w_second], axis=0), both_heads(dy), ((0,), (0,))
            )
            stepped = xp_ref[here, part].astype(f32)
            ended_ref[here, part] = (stepped * end_wide[:, part]).astype(bf16)
            slope = sx_ref[here, part]
            scaled = dt_wide[:, part] * slope
            dts_ref[here, part] = scaled
            dux_ref[here, part] = d_stepped * scaled + skip_wide[0:1, part] * dy.astype(f32) * slope
            return (
                d_scores + d_weights[:, 0:STRETCH] * s_first + d_weights[:, STRETCH:] * s_second,
                per_step + head_sums(stepped * d_stepped, step * PAIR),
            )

        d_scores, per_step = repeat(
            channels // PAIR,
            pair,
            (jnp.zeros((STRETCH, STRETCH), f32), jnp.zeros((STRETCH, STRETCH), f32)),
        )
        d_scores = d_scores.astype(bf16)
        step_ref[:, here] = jnp.transpose(per_step)[0:heads]
        dbc_ref[here, 0:NSTATE] = dot(d_scores, c_now, ((0,), (0,)))
        dbc_ref[here, NSTATE:] = d_c + dot(d_scores, b_now)


def put_total(d_ext, pack_ref, first, part, d_total):
    for tile in range(part.start // STRETCH, part.stop // STRETCH):
        at = tile * STRETCH - part.start
        d_ext[tile, PAD + first : PAD + first + STRETCH, :] = d_total[:, at : at + STRETCH]
    now = jnp.sum(d_total, axis=0, keepdims=True)
    pack_ref[CONV : CONV + 1, part] = pack_ref[CONV : CONV + 1, part] + now if first else now


def conv_backward(d_ext, live_up, weight_ref, x_ref, halo_ref, grad_ref, tail_ref, pack_ref, rows, tile):
    sums = None
    part = lanes(tile, STRETCH)
    for first, count in [(-PAD, PAD)] + [(at, STRETCH) for at in range(0, rows, STRETCH)]:
        begin = PAD + first
        pieces = [d_ext[tile, begin : begin + count, :]]
        for lag in range(1, CONV):
            moved = slice(begin + lag, begin + lag + count)
            pieces.append(d_ext[tile, moved, :] * live_up[lag - 1, begin : begin + count, :])
        grad = weight_ref[0:1, part] * pieces[0]
        for lag in range(1, CONV):
            grad = grad + weight_ref[lag : lag + 1, part] * pieces[lag]
        if first < 0:
            pack_ref[BACK : BACK + HALO, part] = grad[PAD - HALO :]
            seen = halo_ref[:, part]
            pieces = [piece[PAD - HALO :] for piece in pieces]
        else:
            grad_ref[first : first + count, part] = grad.astype(bf16)
            if first + count == rows:
                tail_ref[:, part] = grad[count - HALO :]
            seen = x_ref[first : first + count, part].astype(f32)
        now = [jnp.sum(seen * piece, axis=0, keepdims=True) for piece in pieces]
        sums = now if sums is None else [old + new for old, new in zip(sums, now)]
    for row, value in enumerate(sums):
        pack_ref[row : row + 1, part] = value


def finish_backward(
    aloc_ref, sloc_ref, keep_ref, dux_ref, dts_ref, ended_ref, dbc_ref, drun_ref, step_ref, xp_ref,
    bcc_ref, run_ref, flags_ref, sbc_ref, x_ref, xh_ref, bc_ref, bch_ref, wx_ref, wb_ref, rows_ref,
    dtr_ref, chan_ref, *refs, group,
):
    later_refs, prior_ref, refs = refs[: 2 * PIECES], refs[2 * PIECES : 4 * PIECES], refs[4 * PIECES :]
    gx_ref, xtail_ref, xpack_ref, gbc_ref, bctail_ref, bcpack_ref, gdt_ref, *refs = refs
    clear, live, live_up, dx_ext, dbc_ext, end_wide, ends = refs
    rows, channels = xp_ref.shape
    heads = run_ref.shape[0]
    blocks = rows // STRETCH
    fill_live(flags_ref, clear, live)
    live[:, PAD + rows :, :] = jnp.zeros((HALO, PAD, STRETCH), f32)
    live[:, 0:PAD, :] = jnp.zeros((HALO, PAD, STRETCH), f32)
    for lag in range(1, CONV):
        live_up[lag - 1] = live[lag - 1, lag : lag + rows + PAD, :]
    for ext in (dx_ext, dbc_ext):
        ext[:, 0:PAD, :] = jnp.zeros((ext.shape[0], PAD, STRETCH), f32)
        ext[:, PAD + rows :, :] = jnp.zeros((ext.shape[0], PAD, STRETCH), f32)
    rate = jnp.exp(head_column(rows_ref, A_LOG, group, heads))
    dt_bias = head_column(rows_ref, DT_BIAS, group, heads)
    dt_all = step_sizes(dtr_ref, rows_ref, group)
    d_alog = jnp.zeros((heads, 1), f32)
    d_dtb = jnp.zeros((heads, 1), f32)
    for block in range(blocks):
        here = slice(block * STRETCH, (block + 1) * STRETCH)
        running = run_ref[:, here]
        dt = dt_all[:, here]
        end_wide[...] = spread_heads(
            to_end_factor(running, resets_seen(flags_ref[:, here])), HEAD_DIM
        )
        b_now = bcc_ref[here, 0:NSTATE]

        def chunk(step, carry):
            d_b, per_step = carry
            part = lanes(step, CHUNK)
            later = piece_of(later_refs[:PIECES], part) + piece_of(later_refs[PIECES:], part)
            if block < blocks - 1:
                whole = keep_ref[block + 1 : block + 2, part]
                for place in range(block + 2, blocks):
                    whole = whole * keep_ref[place : place + 1, part]
                later = (aloc_ref[block, :, part].astype(f32) + whole * later.astype(f32)).astype(bf16)
            state = block_state(block, prior_ref, sloc_ref, keep_ref, part)
            d_keep = jnp.sum(later.astype(f32) * state.astype(f32), axis=0, keepdims=True)
            d_end = dot(b_now, later) * end_wide[:, part]
            product = xp_ref[here, part].astype(f32) * d_end
            at_ends = jnp.sum(product, axis=0, keepdims=True)
            at_ends = at_ends + d_keep * keep_ref[block : block + 1, part]
            ends[:, part] = jnp.broadcast_to(at_ends, (PAD, CHUNK))
            d_total = dux_ref[here, part] + d_end * dts_ref[here, part]
            put_total(dx_ext, xpack_ref, block * STRETCH, part, d_total)
            return (
                d_b + dot(ended_ref[here, part], later, ((1,), (1,))),
                per_step + head_sums(product, step * CHUNK),
            )

        zero = jnp.zeros((STRETCH, NSTATE), f32)
        d_b, per_step = repeat(channels // CHUNK, chunk, (zero, jnp.zeros((STRETCH, STRETCH), f32)))
        per_step = step_ref[:, here] + jnp.transpose(per_step)[0:heads]
        for place, d_part in enumerate((dbc_ref[here, 0:NSTATE] + d_b, dbc_ref[here, NSTATE:])):
            part = lanes(place, NSTATE)
            put_total(dbc_ext, bcpack_ref, block * STRETCH, part, d_part * sbc_ref[here, part])
        at_end = to_column(head_sums(ends[...], 0)[0:1], 0, heads)
        is_last = iota((heads, STRETCH), 1) == STRETCH - 1
        d_run = drun_ref[:, here] - per_step + jnp.where(is_last, at_end, 0.0)
        shape = (STRETCH, STRETCH)
        d_log = dot_full(d_run, (iota(shape, 0) >= iota(shape, 1)).astype(f32))
        d_dt = per_step / dt - rate * d_log
        raw = dtr_ref[:, here].astype(f32) + dt_bias
        d_raw = d_dt / (1.0 + jnp.exp(-raw))
        gdt_ref[:, here] = d_raw
        d_alog = d_alog - jnp.sum(d_log * dt, axis=1, keepdims=True) * rate
        d_dtb = d_dtb + jnp.sum(d_raw, axis=1, keepdims=True)
    xpack_ref[GAIN : SKIP + 1, :] = chan_ref[0:2, :]
    bcpack_ref[GAIN : SKIP + 1, :] = jnp.zeros((2, bcpack_ref.shape[1]), f32)
    for place, column in enumerate((d_alog, d_dtb)):
        shape = (heads, STRETCH)
        pick = iota(shape, 1) == iota(shape, 0) + group * heads
        row = jnp.sum(jnp.where(pick, jnp.broadcast_to(column, shape), 0.0), axis=0, keepdims=True)
        bcpack_ref[GAIN : GAIN + 1, place * STRETCH : (place + 1) * STRETCH] = row
    for step in range(channels // STRETCH):
        conv_backward(
            dx_ext, live_up, wx_ref, x_ref, xh_ref, gx_ref, xtail_ref, xpack_ref, rows, step
        )
    for step in range(2):
        conv_backward(
            dbc_ext, live_up, wb_ref, bc_ref, bch_ref, gbc_ref, bctail_ref, bcpack_ref, rows, step
        )


def pack(*refs):
    *pieces, out_ref = refs
    at = 0
    for ref in pieces:
        size = ref.shape[1]
        out_ref[0 : BACK + 1, at : at + size] = ref[0 : BACK + 1, :]
        at += size
    whole = jnp.concatenate([ref[BACK + 1 : PACKED, :] for ref in pieces], axis=1)
    short = out_ref.shape[1] - at
    for row in range(PAD):
        first = row % (PAD // 2) * short
        out_ref[row : row + 1, at:] = whole[row // (PAD // 2) :][0:1, first : first + short]


def unpack_back(value, length):
    short = value.shape[1] - length
    rows = [value[BACK : BACK + 1, 0:length]]
    for half in range(2):
        pieces = [value[half * (PAD // 2) + turn :][0:1, length:] for turn in range(PAD // 2)]
        rows.append(jnp.concatenate(pieces, axis=1))
    return jnp.concatenate(rows, axis=0)


def final_sums(mine_ref, pick_ref, flags_ref, *refs, arrivals, groups, scale):
    arrived, refs = refs[:arrivals], refs[arrivals:]
    tails_x, tails_bc, refs = refs[:groups], refs[groups : 2 * groups], refs[2 * groups :]
    out_wx, out_bx, out_wb, out_bb, out_alog, out_dtb, out_skip, out_gain, ending_ref = refs
    inner = out_wx.shape[1]
    length = ending_ref.shape[1]
    total = mine_ref[0:BACK, 0:length]
    back = jnp.zeros((HALO, length), f32)
    for place, ref in enumerate(arrived):
        value = ref[...].astype(f32)
        total = total + value[0:BACK, 0:length]
        back = back + unpack_back(value, length) * pick_ref[place : place + 1, 0:1]
    total = total * scale
    back = back * tail_factors(flags_ref)
    at = 0
    for ref in tails_x + tails_bc:
        size = ref.shape[1]
        ending_ref[:, at : at + size] = (ref[...] + back[:, at : at + size]).astype(bf16)
        at += size
    out_wx[...] = total[0:CONV, 0:inner]
    out_bx[...] = total[CONV : CONV + 1, 0:inner]
    for which in range(2):
        for group in range(groups):
            first = inner + (2 * group + which) * NSTATE
            to = slice(group * NSTATE, (group + 1) * NSTATE)
            out_wb[:, which, to] = total[0:CONV, first : first + NSTATE]
            out_bb[which : which + 1, to] = total[CONV : CONV + 1, first : first + NSTATE]
    out_gain[...] = total[GAIN : GAIN + 1, 0:inner]
    heads = out_skip.shape[1]
    for out, shift in ((out_alog, 0), (out_dtb, STRETCH)):
        row = None
        for group in range(groups):
            first = inner + 2 * group * NSTATE + shift
            piece = total[GAIN : GAIN + 1, first : first + STRETCH]
            row = piece if row is None else row + piece
        out[...] = row[:, 0:heads]
    lane_sums = jnp.broadcast_to(total[SKIP : SKIP + 1, 0:inner], (PAD, inner))
    shape = (heads, inner)
    pick = (iota(shape, 1) // HEAD_DIM == iota(shape, 0)).astype(f32).astype(bf16)
    high = lane_sums.astype(bf16)
    low = (lane_sums - high.astype(f32)).astype(bf16)
    last = ((1,), (1,))
    out_skip[...] = (dot(high, pick, last) + dot(low, pick, last))[0:1]


def call(kernel, operands, outs, scratch, flops, name, blocked=None, hbm_outs=()):
    operands = [(each + (None,))[:3] for each in operands]
    cuts = [cut or {} for _, cut, _ in operands]
    arrays = [array for array, _, _ in operands]
    stages = [stage for _, _, stage in operands]
    shapes = [jax.ShapeDtypeStruct(shape, dtype) for shape, dtype in outs]
    streamed = [place for place, stage in enumerate(stages) if stage is not None]
    buffers = []
    for place in streamed:
        cut = cuts[place]
        shape = tuple(
            cut[dim].stop - cut[dim].start if dim in cut else extent
            for dim, extent in enumerate(arrays[place].shape)
        )
        buffers.append(pltpu.VMEM(shape, arrays[place].dtype))
    copies_made = sum(len(stages[place]) for place in streamed)

    def body(*refs):
        count, made = len(cuts), len(buffers)
        rest = refs[count:]
        held = dict(zip(streamed, rest[len(rest) - made - 1 : len(rest) - 1])) if made else {}
        sems = rest[-1] if made else None
        seen, copies = [], []
        for place, (ref, cut) in enumerate(zip(refs, cuts)):
            if cut:
                ref = ref.at[tuple(cut.get(dim, slice(None)) for dim in range(len(ref.shape)))]
            if place in held:
                buffer = held[place]
                size = buffer.shape[-1] // len(stages[place])
                for turn, stage in enumerate(stages[place]):
                    part = (slice(None),) * (len(buffer.shape) - 1) + (
                        slice(turn * size, (turn + 1) * size),
                    )
                    copy = (stage, (ref.at[part], buffer.at[part], sems.at[len(copies)]))
                    copies.append(copy)
                ref = buffer
            seen.append(ref)
        for _, copy in sorted(copies, key=lambda each: each[0]):
            pltpu.make_async_copy(*copy).start()

        def ready(stage):
            for which, copy in copies:
                if which == stage:
                    pltpu.make_async_copy(*copy).wait()

        if made:
            kernel(*seen, *rest[: len(rest) - made - 1], ready=ready)
        else:
            kernel(*seen, *rest)

    def block_of(array, cut):
        shape, index = [], []
        for dim, extent in enumerate(array.shape):
            part = cut.get(dim, slice(0, extent))
            size = part.stop - part.start
            shape.append(size)
            index.append(part.start // size)
        return pl.BlockSpec(tuple(shape), functools.partial(lambda fixed, i: fixed, tuple(index)))

    in_vmem = pl.BlockSpec(memory_space=pltpu.VMEM)
    in_hbm = pl.BlockSpec(memory_space=pltpu.HBM)
    scratch_shapes = [
        pltpu.VMEM(each, f32) if isinstance(each, tuple) else each for each in scratch
    ]
    if blocked:
        grid, limit = {"grid": (1,)}, blocked
        in_specs = [block_of(array, cut) for array, cut in zip(arrays, cuts)]
        out_specs = [block_of(shape, {}) for shape in shapes]
    else:
        grid, limit = {}, STREAM_LIMIT if buffers else VMEM_LIMIT
        in_specs = [in_vmem if stage is None else in_hbm for stage in stages]
        out_specs = [in_hbm if place in hbm_outs else in_vmem for place in range(len(shapes))]
        if buffers:
            scratch_shapes += buffers + [pltpu.SemaphoreType.DMA((copies_made,))]
    count = sum(each.size * each.dtype.itemsize for each in arrays + shapes)
    return pl.pallas_call(
        kernel if blocked else body,
        in_specs=in_specs,
        out_specs=out_specs,
        out_shape=shapes,
        scratch_shapes=scratch_shapes,
        compiler_params=pltpu.CompilerParams(vmem_limit_bytes=limit),
        cost_estimate=pl.CostEstimate(flops=flops, bytes_accessed=count, transcendentals=0),
        name=name,
        **grid,
    )(*arrays)


def together(*values):
    return lax.optimization_barrier(values)


def chain(parts, decays, axis, backward, fillers):
    count = lax.axis_size(axis)
    zero = [jnp.zeros(part.shape, bf16) for part in parts]
    early, last = list(zero), list(zero)
    results = []
    for hop in range(count - 1):
        pairs = [(count - 1 - hop, count - 2 - hop)] if backward else [(hop, hop + 1)]
        leaving = list(parts)
        if hop > 0:
            for place, part in enumerate(parts):
                if place:
                    last[place] = together(last[place], leaving[place - 1])[0]
                early[place] = early[place] + last[place] if hop > 1 else last[place]
                arrived = early[place].astype(f32)
                leaving[place] = (decays[place] * arrived + part.astype(f32)).astype(bf16)
        filler = fillers[hop - 1] if 0 < hop <= len(fillers) else None
        if filler:
            work, array = filler
            array = together(array, *leaving)[0]
        last = [lax.ppermute(each, axis, pairs) for each in leaving]
        if filler:
            done = work(array)
            last[0], *done = together(last[0], *done)
            results.append(done)
    for work, array in fillers[len(results) :]:
        results.append(work(array))
    return list(zip(early, last)), results


def exchange_terms(value, axis):
    count = lax.axis_size(axis)
    other = jnp.zeros_like(value)
    stride = 1
    while stride < count:
        value = value + other if stride > 1 else value
        other = lax.ppermute(value, axis, [(i, i ^ stride) for i in range(count)])
        stride *= 2
    return value, other


def per_device(
    x_raw, bc_raw, z_gate, dt_raw, resets, conv_x_weight, conv_x_bias, conv_bc_weight,
    conv_bc_bias, a_log, dt_bias, skip_weight, norm_gain, grad_out,
):
    rows, inner = x_raw.shape[1:]
    groups = bc_raw.shape[3] // NSTATE
    heads = a_log.shape[0] // groups
    channels = inner // groups
    blocks = rows // STRETCH
    width = 2 * NSTATE

    def by_group(value):
        lead = value.shape[:-2]
        split = value.reshape(lead + (2, groups, NSTATE))
        return jnp.moveaxis(split, -3, -2).reshape(lead + (groups * width,))

    x_own, z_own, go_own, dt_own = x_raw[0], z_gate[0], grad_out[0], dt_raw[0]
    bc_own = by_group(bc_raw[0])
    flags = resets
    count = lax.axis_size("ctx")
    sent = call(
        tails,
        [
            (x_raw, {1: slice(rows - 16, rows)}, [0]),
            (bc_raw, {1: slice(rows - 16, rows)}, [0]),
            (flags, {1: slice(rows - STRETCH, rows)}, [0]),
        ],
        [((HALO, inner + groups * width), f32)],
        [],
        rows,
        "tails",
    )[0]
    halo = lax.ppermute(sent, "ctx", [(i, i + 1) for i in range(count - 1)])
    head_rows = jnp.stack([a_log, dt_bias, skip_weight])
    head_rows = jnp.pad(head_rows, ((0, PAD - 3), (0, -head_rows.shape[1] % STRETCH)))
    bx, gain = conv_x_bias[None], norm_gain[None]
    wb, bb = by_group(conv_bc_weight), by_group(conv_bc_bias)[None]

    def wide(array, group):
        return (array, {1: slice(group * channels, (group + 1) * channels)})

    def narrow(array, group, first=0):
        return (array, {1: slice(first + group * width, first + (group + 1) * width)})

    def per_head(array, group):
        return (array, {0: slice(group * heads, (group + 1) * heads)})

    def whole(array):
        return (array, None)

    keep_rows = -(-blocks // PAD) * PAD
    tall, thin, row_shape = (rows, channels), (rows, width), (heads, rows)
    state_shape = (NSTATE, channels)
    piece_shape = (NSTATE, channels // PIECES)
    local_shape = (blocks - 1, NSTATE, channels)
    clear_shape, live_shape = (rows + PAD, STRETCH), (HALO, rows + 2 * PAD, STRETCH)
    wide_scratch = (STRETCH, channels)
    run_scratch = [(STRETCH, heads * STRETCH), (heads * PAD, STRETCH)]
    work = rows * channels * STRETCH
    group_range = range(groups)
    here = lax.axis_index("ctx")
    picks = [(here ^ shift) == here + 1 for shift in range(1, count)]
    pick = jnp.broadcast_to(jnp.stack(picks).astype(f32)[:, None], (count - 1, STRETCH))
    flags, pick = together(flags, pick)
    held = []
    flags_now = flags
    for g in group_range:
        if held:
            flags_now = together(flags, held[-1][-1])[0]
        held.append(
            call(
                functools.partial(conv_and_state, group=g),
                [
                    wide(x_own, g), wide(halo, g), narrow(bc_own, g), narrow(halo, g, inner),
                    wide(conv_x_weight, g), wide(bx, g), narrow(wb, g), narrow(bb, g),
                    per_head(dt_own, g), whole(head_rows), whole(flags_now),
                ],
                [
                    (tall, bf16), (tall, bf16), (tall, f32), (thin, bf16), (thin, f32),
                    (row_shape, f32), ((keep_rows, channels), f32), (local_shape, bf16),
                ]
                + [(piece_shape, bf16)] * PIECES
                + [((1, channels // PIECES), f32)] * PIECES,
                [
                    (channels // STRETCH, rows + PAD, STRETCH), (width // STRETCH, rows + PAD, STRETCH),
                    clear_shape, live_shape,
                    wide_scratch, wide_scratch, state_shape,
                ],
                2 * work,
                "conv_and_state",
            )
        )
    xc, xp, ux, bcc, ubc, run, keep, s_loc, *pieces = zip(*held)
    s_dev, decay = pieces[:PIECES], pieces[PIECES:]

    def in_a_row(pieces):
        return [piece[g] for g in group_range for piece in pieces]

    def by_pieces(pairs):
        return [
            [pair[term] for term in range(2) for pair in pairs[g * PIECES : (g + 1) * PIECES]]
            for g in group_range
        ]


    def forward_work(g):
        return lambda bcc_now: call(
            within_blocks,
            [
                whole(xp[g]), whole(bcc_now), whole(run[g]), whole(flags), whole(ux[g]), whole(ubc[g]),
            ],
            [(tall, f32), (tall, f32), (thin, f32)],
            run_scratch,
            6 * work,
            "within_blocks",
        )

    prior, held = chain(
        in_a_row(s_dev), in_a_row(decay), "ctx", False, [(forward_work(g), bcc[g]) for g in group_range]
    )
    prior = by_pieces(prior)
    y_within, slope_x, slope_bc = zip(*held)
    held, sums = [], ()
    for g in group_range:
        bundle, total = call(
            functools.partial(gate_forward, group=g),
            [
                whole(y_within[g]), whole(s_loc[g]), whole(keep[g]), whole(bcc[g]), whole(run[g]),
                whole(flags), whole(xc[g]), whole(head_rows), wide(z_own, g), wide(go_own, g),
                wide(gain, g),
            ]
            + [whole(each) for each in prior[g]]
            + [whole(each) for each in sums],
            [((bundle_rows(rows)[-1], channels), f32), ((2, rows), f32)],
            [wide_scratch, (PAD, channels)],
            2 * work,
            "gate_forward",
        )
        sums = (total,)
        held.append(bundle)
    bundle = held
    own, other = exchange_terms(sums[0], "head")
    held = []
    for g in group_range:
        bundle_now = together(bundle[g], held[-1][-1])[0] if held else bundle[g]
        held.append(
            call(
                functools.partial(gate_backward, heads=heads),
                [whole(own), whole(other), whole(bundle_now), wide(z_own, g), wide(go_own, g)],
                [(tall, bf16), (local_shape, bf16), ((2, rows), f32), (tall, f32)]
                + [(piece_shape, bf16)] * PIECES,
                [wide_scratch, state_shape],
                2 * work,
                "gate_backward",
            )
        )
    dy, a_loc, totals, y_all, *a_dev = zip(*held)

    def backward_work(g):
        return lambda bcc_now: call(
            functools.partial(within_backward, group=g),
            [
                whole(totals[g]), whole(y_all[g]), wide(z_own, g), wide(go_own, g), wide(gain, g),
                whole(dy[g]), whole(xc[g]), whole(xp[g]), whole(bcc_now),
                whole(run[g]), whole(flags), whole(s_loc[g]), whole(keep[g]), whole(head_rows),
                whole(slope_x[g]), per_head(dt_own, g),
            ]
            + [whole(each) for each in prior[g]],
            [
                (tall, bf16), (tall, f32), (tall, f32), (tall, bf16), (thin, f32), (row_shape, f32),
                (row_shape, f32), ((PAD, channels), f32),
            ],
            run_scratch + [wide_scratch, (PAD, channels), wide_scratch, wide_scratch],
            10 * work,
            "within_backward",
            BLOCKED_LIMIT,
        )

    later, held = chain(
        in_a_row(a_dev), in_a_row(decay), "ctx", True, [(backward_work(g), bcc[g]) for g in group_range]
    )
    later = by_pieces(later)
    gz, dux, dts, ended, dbc, drun, per_step, chan = zip(*held)
    held = []
    for g in group_range:
        rows_now = together(head_rows, held[-1][-1])[0] if held else head_rows
        held.append(call(
            functools.partial(finish_backward, group=g),
            [
                whole(a_loc[g]), whole(s_loc[g]), whole(keep[g]), whole(dux[g]), whole(dts[g]),
                whole(ended[g]), whole(dbc[g]), whole(drun[g]), whole(per_step[g]), whole(xp[g]),
                whole(bcc[g]), whole(run[g]), whole(flags), whole(slope_bc[g]), wide(x_own, g),
                wide(halo, g), narrow(bc_own, g), narrow(halo, g, inner), wide(conv_x_weight, g),
                narrow(wb, g), whole(rows_now), per_head(dt_own, g), whole(chan[g]),
            ]
            + [whole(each) for each in later[g] + prior[g]],
            [
                (tall, bf16), ((HALO, channels), f32), ((PACKED, channels), f32), (thin, bf16),
                ((HALO, width), f32), ((PACKED, width), f32), (row_shape, f32),
            ],
            [
                clear_shape, live_shape, (HALO, rows + PAD, STRETCH),
                (channels // STRETCH, rows + 2 * PAD, STRETCH),
                (width // STRETCH, rows + 2 * PAD, STRETCH), wide_scratch, (PAD, channels),
            ],
            4 * work,
            "finish_backward",
            BLOCKED_LIMIT,
        ))
    gx, x_tail, x_pack, gbc, bc_tail, bc_pack, gdt = zip(*held)

    def joined(pieces):
        return jnp.concatenate(pieces, axis=1)

    def ungroup(value):
        lead = value.shape[:-1]
        split = value.reshape(lead + (groups, 2, NSTATE))
        return jnp.moveaxis(split, -3, -2).reshape(lead + (2, groups * NSTATE))

    length = inner + groups * width
    packed = call(
        pack,
        [whole(each) for each in x_pack + bc_pack],
        [((PAD, length + 2 * length // PAD), f32)],
        [],
        rows,
        "pack",
    )[0]
    mine = packed
    own_rows = np.ones((PAD, packed.shape[1]), np.float32)
    own_rows[BACK:] = 0.0
    own_rows[:, length:] = 0.0
    for shift in range(1, lax.axis_size("dp")):
        size = lax.axis_size("dp")
        other = lax.ppermute(packed, "dp", [(i, (i + shift) % size) for i in range(size)])
        mine = mine + other * own_rows
    leaving = mine.astype(bf16)
    arrived = [
        lax.ppermute(leaving, "ctx", [(i, i ^ shift) for i in range(count)])
        for shift in range(1, count)
    ]
    out_wx, out_bx, out_wb, out_bb, out_alog, out_dtb, out_skip, out_gain, ending = call(
        functools.partial(
            final_sums,
            arrivals=count - 1,
            groups=groups,
            scale=float(lax.axis_size("dp") * count * rows) ** (-0.5),
        ),
        [whole(mine), whole(pick), whole(flags)]
        + [whole(each) for each in arrived]
        + [whole(each) for each in x_tail + bc_tail],
        [
            ((CONV, inner), f32), ((1, inner), f32), ((CONV, 2, groups * NSTATE), f32),
            ((2, groups * NSTATE), f32),
            ((1, groups * heads), f32), ((1, groups * heads), f32), ((1, groups * heads), f32),
            ((1, inner), f32), ((HALO, inner + groups * width), bf16),
        ],
        [],
        rows * inner,
        "final_sums",
    )
    grad_x = lax.dynamic_update_slice(joined(gx), ending[:, :inner], (rows - HALO, 0))
    grad_bc = lax.dynamic_update_slice(
        ungroup(joined(gbc)), ungroup(ending[:, inner:]), (rows - HALO, 0, 0)
    )
    return (
        grad_x[None],
        grad_bc[None],
        joined(gz)[None],
        jnp.concatenate(gdt, axis=0)[None],
        out_wx,
        out_bx[0],
        out_wb,
        out_bb,
        out_alog[0],
        out_dtb[0],
        out_skip[0],
        out_gain[0],
    )


def solution(mesh):
    return jax.shard_map(
        per_device,
        mesh=mesh,
        in_specs=(
            P("dp", "ctx", "head"),
            P("dp", "ctx", None, "head"),
            P("dp", "ctx", "head"),
            P("dp", "head", "ctx"),
            P("dp", "ctx"),
            P(None, "head"),
            P("head"),
            P(None, None, "head"),
            P(None, "head"),
            P("head"),
            P("head"),
            P("head"),
            P("head"),
            P("dp", "ctx", "head"),
        ),
        out_specs=(
            P("dp", "ctx", "head"),
            P("dp", "ctx", None, "head"),
            P("dp", "ctx", "head"),
            P("dp", "head", "ctx"),
            P(None, "head"),
            P("head"),
            P(None, None, "head"),
            P(None, "head"),
            P("head"),
            P("head"),
            P("head"),
            P("head"),
        ),
        check_vma=False,
    )
```

```python
import functools

import jax
import jax.numpy as jnp
import numpy as np
from jax import lax
from jax.experimental import pallas as pl
from jax.experimental.pallas import tpu as pltpu
from jax.sharding import PartitionSpec as P

HEAD_DIM = 64
NSTATE = 128
CONV = 4
STRETCH = 128
INNER = 8192
HALO = CONV - 1
PAD = 8
CHUNK = 256
PAIR = 2 * HEAD_DIM
NORM_EPS = 1e-05
LOWEST = -1e30
GAIN, SKIP, BACK = CONV + 1, CONV + 2, CONV + 3
PACKED = BACK + HALO
A_LOG, DT_BIAS, SKIP_WEIGHT = range(3)
STAGES = 2
STREAM_LIMIT = 62 * 1024 * 1024
PIECES = 2
BLOCKED_LIMIT = 40 * 1024 * 1024
VMEM_LIMIT = 24 * 1024 * 1024

f32 = jnp.float32
bf16 = jnp.bfloat16


def dot(a, b, contract=((1,), (0,))):
    return lax.dot_general(a, b, (contract, ((), ())), preferred_element_type=f32)


def dot_full(a, b):
    return lax.dot_general(
        a, b, (((1,), (0,)), ((), ())), precision=lax.Precision.HIGHEST, preferred_element_type=f32
    )


def iota(shape, dim):
    return lax.broadcasted_iota(jnp.int32, shape, dim)


def split3(value):
    high = value.astype(bf16)
    rest = value - high.astype(f32)
    middle = rest.astype(bf16)
    low = (rest - middle.astype(f32)).astype(bf16)
    return jnp.concatenate([high, middle, low], axis=0)


def spread_heads(rows, width):
    heads = rows.shape[0]
    shape = (heads, heads * width)
    pick = (iota(shape, 1) // width == iota(shape, 0)).astype(f32).astype(bf16)
    return dot(split3(rows), jnp.concatenate([pick] * 3, axis=0), ((0,), (0,)))


def head_sums(value, first):
    shape = (value.shape[1], STRETCH)
    pick = ((iota(shape, 0) + first) // HEAD_DIM == iota(shape, 1)).astype(f32).astype(bf16)
    high = value.astype(bf16)
    low = (value - high.astype(f32)).astype(bf16)
    both = dot(jnp.concatenate([high, low], axis=0), pick)
    return both[: value.shape[0]] + both[value.shape[0] :]


def as_columns(row):
    return jnp.transpose(jnp.broadcast_to(row, (STRETCH, STRETCH)))


def sigmoid(value):
    return 0.5 * jnp.tanh(0.5 * value) + 0.5


def upper_ones():
    shape = (STRETCH, STRETCH)
    return (iota(shape, 0) <= iota(shape, 1)).astype(f32)


def resets_seen(flags_row):
    flags = jnp.broadcast_to(flags_row.astype(f32), (PAD, STRETCH)).astype(bf16)
    return dot(flags, upper_ones().astype(bf16))[0:1]


def decay_mask(seen):
    shape = (STRETCH, STRETCH)
    same = (as_columns(seen) == jnp.broadcast_to(seen, shape)) & (iota(shape, 0) >= iota(shape, 1))
    return jnp.where(same, 0.0, LOWEST)


def lanes(position, size):
    return slice(position * size, (position + 1) * size)


def repeat(count, body, carry):
    for step in range(count):
        carry = body(step, carry)
    return carry


def piece_of(refs, part):
    width = refs[0].shape[1]
    ref = refs[part.start // width]
    return ref[:, part.start % width : part.start % width + part.stop - part.start]


def to_column(row, first, heads):
    shape = (heads, row.shape[1])
    pick = iota(shape, 1) == iota(shape, 0) + first
    return jnp.sum(jnp.where(pick, jnp.broadcast_to(row, shape), 0.0), axis=1, keepdims=True)


def over_channels(column):
    return spread_heads(jnp.broadcast_to(column, (column.shape[0], PAD)), HEAD_DIM)[0:1]


def softplus(value):
    small = jnp.exp(-jnp.abs(value))
    series = small * (1.0 - small * (1 / 2 - small * (1 / 3 - small * (1 / 4 - small * (1 / 5)))))
    return jnp.maximum(value, 0.0) + jnp.where(small < 0.03, series, jnp.log(1.0 + small))


def head_column(rows_ref, which, group, heads):
    return to_column(rows_ref[which : which + 1, :], group * heads, heads)


def step_sizes(dtr_ref, rows_ref, group):
    heads = dtr_ref.shape[0]
    return softplus(dtr_ref[...].astype(f32) + head_column(rows_ref, DT_BIAS, group, heads))


def to_end_factor(running, seen):
    final = running[:, STRETCH - 1 : STRETCH]
    return jnp.where(seen == seen[:, STRETCH - 1 : STRETCH], jnp.exp(final - running), 0.0)


def doubled(value):
    return jnp.concatenate([value, value], axis=1)


def fill_live(flags_ref, clear, live):
    rows = flags_ref.shape[1]
    clear[0:PAD, :] = jnp.ones((PAD, STRETCH), f32)
    for first in range(0, rows, STRETCH):
        flags = flags_ref[:, first : first + STRETCH].astype(f32)
        clear[PAD + first : PAD + first + STRETCH, :] = as_columns(1.0 - flags)
    for first in range(0, rows, STRETCH):
        begin = PAD + first
        product = clear[begin : begin + STRETCH, :]
        live[0, begin : begin + STRETCH, :] = product
        for lag in range(2, CONV):
            product = product * clear[begin - lag + 1 : begin - lag + 1 + STRETCH, :]
            live[lag - 1, begin : begin + STRETCH, :] = product


def fill_extended(extended, halo_ref, rows_ref):
    for tile in range(extended.shape[0]):
        part = lanes(tile, STRETCH)
        extended[tile, PAD - HALO : PAD, :] = halo_ref[:, part]
        extended[tile, PAD:, :] = rows_ref[:, part].astype(f32)


def conv_total(extended, live, weight_ref, bias_ref, first, part):
    begin = PAD + first
    totals = []
    for tile in range(part.start // STRETCH, part.stop // STRETCH):
        cut = lanes(tile, STRETCH)
        total = bias_ref[0:1, cut] + weight_ref[0:1, cut] * extended[tile, begin : begin + STRETCH, :]
        for lag in range(1, CONV):
            total = total + weight_ref[lag : lag + 1, cut] * (
                extended[tile, begin - lag : begin - lag + STRETCH, :]
                * live[lag - 1, begin : begin + STRETCH, :]
            )
        totals.append(total)
    return totals[0] if len(totals) == 1 else jnp.concatenate(totals, axis=1)


def tail_factors(flags_ref):
    flags = flags_ref[:, flags_ref.shape[1] - STRETCH :].astype(f32)
    clear = as_columns(1.0 - flags)
    last = clear[STRETCH - 1 :]
    both = last * clear[STRETCH - 2 : STRETCH - 1]
    return jnp.concatenate([both, last, jnp.ones_like(last)], axis=0)[:, 0:1]


def tails(x_ref, bc_ref, flags_ref, out_ref, *, ready):
    ready(0)
    keep = tail_factors(flags_ref)
    inner = x_ref.shape[2]
    out_ref[:, 0:inner] = x_ref[0].astype(f32)[x_ref.shape[1] - HALO :] * keep
    groups = bc_ref.shape[3] // NSTATE
    for which in range(2):
        rows = bc_ref[0, :, which, :].astype(f32)[bc_ref.shape[1] - HALO :] * keep
        for group in range(groups):
            first = inner + (2 * group + which) * NSTATE
            out_ref[:, first : first + NSTATE] = rows[:, group * NSTATE : (group + 1) * NSTATE]


def conv_and_state(
    x_ref, xh_ref, bc_ref, bch_ref, wx_ref, bx_ref, wb_ref, bb_ref, dtr_ref, rows_ref,
    flags_ref, xc_ref, xp_ref, ux_ref, bcc_ref, ubc_ref, run_ref, keep_ref, sloc_ref, *refs, group,
):
    sdev_refs, decay_refs = refs[:PIECES], refs[PIECES : 2 * PIECES]
    x_ext, bc_ext, clear, live, dt_wide, end_wide, state = refs[2 * PIECES :]
    rows, channels = x_ref.shape
    heads = dtr_ref.shape[0]
    fill_extended(x_ext, xh_ref, x_ref)
    fill_extended(bc_ext, bch_ref, bc_ref)
    fill_live(flags_ref, clear, live)
    blocks = rows // STRETCH
    rate = jnp.exp(head_column(rows_ref, A_LOG, group, heads))
    dt_all = step_sizes(dtr_ref, rows_ref, group)
    product = None
    for block in range(blocks):
        first = block * STRETCH
        here = slice(first, first + STRETCH)
        every = slice(0, 2 * NSTATE)
        total = conv_total(bc_ext, live, wb_ref, bb_ref, first, every)
        ubc_ref[here, :] = total
        bc_now = (total * sigmoid(total)).astype(bf16)
        bcc_ref[here, :] = bc_now
        b_turned = jnp.transpose(bc_now[:, 0:NSTATE].astype(f32)).astype(bf16)
        seen = resets_seen(flags_ref[:, here])
        dt = dt_all[:, here]
        running = dot_full(-rate * dt, upper_ones())
        run_ref[:, here] = running
        final = running[:, STRETCH - 1 : STRETCH]
        keep = jnp.where(seen[:, STRETCH - 1 : STRETCH] == 0.0, jnp.exp(final), 0.0)
        keep_row = over_channels(keep)
        keep_ref[block : block + 1, :] = keep_row
        product = keep_row if product is None else product * keep_row
        dt_wide[...] = spread_heads(dt, HEAD_DIM)
        end_wide[...] = spread_heads(to_end_factor(running, seen), HEAD_DIM)

        def chunk(step, carry):
            part = lanes(step, CHUNK)
            total = conv_total(x_ext, live, wx_ref, bx_ref, first, part)
            ux_ref[here, part] = total
            xc = (total * sigmoid(total)).astype(bf16)
            xc_ref[here, part] = xc
            stepped = (xc.astype(f32) * dt_wide[:, part]).astype(bf16)
            xp_ref[here, part] = stepped
            ended = (stepped.astype(f32) * end_wide[:, part]).astype(bf16)
            fresh = dot(b_turned, ended)
            if block > 0:
                fresh = keep_ref[block : block + 1, part] * state[:, part] + fresh
            if block < blocks - 1:
                state[:, part] = fresh
                sloc_ref[block, :, part] = fresh.astype(bf16)
            else:
                put_piece(sdev_refs, part, fresh.astype(bf16))
            return carry

        repeat(channels // CHUNK, chunk, 0)
    for place, ref in enumerate(decay_refs):
        size = ref.shape[1]
        ref[...] = product[:, place * size : (place + 1) * size]


def place_runs(run_ref, here, run_wide, run_tall):
    running = run_ref[:, here]
    run_wide[...] = spread_heads(running, STRETCH)
    for head in range(running.shape[0]):
        run_tall[head * PAD : (head + 1) * PAD, :] = jnp.broadcast_to(
            running[head : head + 1], (PAD, STRETCH)
        )


def block_weights(scores, mask, run_wide, run_tall, head):
    column = run_wide[:, lanes(head, STRETCH)]
    row = run_tall[head * PAD : head * PAD + 1, :]
    segment = jnp.exp(column - row + mask)
    return segment, (scores * segment).astype(bf16)


def both_heads(value):
    is_first = iota(value.shape, 1) < HEAD_DIM
    wide = value.astype(f32)
    zero = jnp.zeros_like(wide)
    return jnp.concatenate(
        [jnp.where(is_first, wide, zero).astype(bf16), jnp.where(is_first, zero, wide).astype(bf16)],
        axis=0,
    )


def put_piece(refs, part, value):
    width = refs[0].shape[1]
    ref = refs[part.start // width]
    ref[:, part.start % width : part.start % width + part.stop - part.start] = value


def slope_of(total):
    up = sigmoid(total)
    return up + total * up * (1.0 - up)


def within_blocks(
    xp_ref, bcc_ref, run_ref, flags_ref, ux_ref, ubc_ref, y_ref, sx_ref, sbc_ref, run_wide, run_tall
):
    rows, channels = xp_ref.shape
    for block in range(rows // STRETCH):
        here = slice(block * STRETCH, (block + 1) * STRETCH)
        mask = decay_mask(resets_seen(flags_ref[:, here]))
        scores = dot(bcc_ref[here, NSTATE:], bcc_ref[here, 0:NSTATE], ((1,), (1,)))
        place_runs(run_ref, here, run_wide, run_tall)
        sbc_ref[here, :] = slope_of(ubc_ref[here, :])

        def pair(step, carry):
            _, w_first = block_weights(scores, mask, run_wide, run_tall, 2 * step)
            _, w_second = block_weights(scores, mask, run_wide, run_tall, 2 * step + 1)
            part = lanes(step, PAIR)
            y_ref[here, part] = dot(
                jnp.concatenate([w_first, w_second], axis=1), both_heads(xp_ref[here, part])
            )
            sx_ref[here, part] = slope_of(ux_ref[here, part])
            return carry

        repeat(channels // PAIR, pair, 0)


def start_factor(run_ref, flags_ref, here):
    seen = resets_seen(flags_ref[:, here])
    return jnp.where(seen == 0.0, jnp.exp(run_ref[:, here]), 0.0)


def block_state(block, prior_ref, sloc_ref, keep_ref, part):
    state = piece_of(prior_ref[:PIECES], part) + piece_of(prior_ref[PIECES:], part)
    if block == 0:
        return state
    whole = keep_ref[0:1, part]
    for step in range(1, block):
        whole = whole * keep_ref[step : step + 1, part]
    return (whole * state.astype(f32) + sloc_ref[block - 1, :, part].astype(f32)).astype(bf16)


def bundle_rows(rows):
    places = [rows]
    for size in (PAD, PAD, 2 * PAD, NSTATE // 4):
        places.append(places[-1] + size)
    return places


def gate_forward(
    y_ref, sloc_ref, keep_ref, bcc_ref, run_ref, flags_ref, xc_ref, rows_ref, z_ref, go_ref, gain_ref,
    *refs, group,
):
    prior_ref, refs = refs[: 2 * PIECES], refs[2 * PIECES :]
    *before, bundle_ref, sums_ref, start_wide, skip_wide = refs
    rows, channels = xc_ref.shape
    heads = run_ref.shape[0]
    at_keep, at_gain, at_start, at_turned, _ = bundle_rows(rows)
    bundle_ref[at_keep:at_gain, :] = keep_ref[0:PAD, :]
    bundle_ref[at_gain:at_start, :] = jnp.broadcast_to(gain_ref[...], (PAD, channels))
    skip_wide[0:1, :] = over_channels(head_column(rows_ref, SKIP_WEIGHT, group, heads))
    quarter = NSTATE // 4
    for block in range(rows // STRETCH):
        here = slice(block * STRETCH, (block + 1) * STRETCH)
        start = start_factor(run_ref, flags_ref, here)
        bundle_ref[at_start : at_start + heads, here] = start
        start_wide[...] = spread_heads(start, HEAD_DIM)
        c_now = bcc_ref[here, NSTATE:]
        turned = jnp.transpose(c_now.astype(f32))
        for turn in range(4):
            first = turn * rows + block * STRETCH
            bundle_ref[at_turned : at_turned + quarter, first : first + STRETCH] = turned[
                turn * quarter : (turn + 1) * quarter
            ]

        def chunk(step, carry):
            squares, products = carry
            part = lanes(step, CHUNK)
            carried = dot(c_now, block_state(block, prior_ref, sloc_ref, keep_ref, part))
            y_now = y_ref[here, part] + carried * start_wide[:, part]
            y_now = y_now + skip_wide[0:1, part] * xc_ref[here, part].astype(f32)
            bundle_ref[here, part] = y_now
            z = z_ref[here, part].astype(f32)
            gated = y_now.astype(bf16).astype(f32) * (z * sigmoid(z))
            gained = go_ref[here, part].astype(f32) * gain_ref[0:1, part]
            return squares + gated * gated, products + gated * gained

        zero = jnp.zeros((STRETCH, CHUNK), f32)
        squares, products = repeat(channels // CHUNK, chunk, (zero, zero))
        square_column = jnp.sum(squares, axis=1, keepdims=True)
        product_column = jnp.sum(products, axis=1, keepdims=True)
        shape = (STRETCH, STRETCH)
        both = jnp.where(
            iota(shape, 1) == 0,
            jnp.broadcast_to(square_column, shape),
            jnp.broadcast_to(product_column, shape),
        )
        total = jnp.transpose(both)[0:2]
        for ref in before:
            total = total + ref[:, here]
        sums_ref[:, here] = total


def norm_factors(totals_ref, here):
    squares = totals_ref[0:1, here]
    products = totals_ref[1:2, here]
    inv_rms = lax.rsqrt(squares * (1.0 / INNER) + NORM_EPS)
    pull = inv_rms * inv_rms * inv_rms * products * (1.0 / INNER)
    return doubled(as_columns(inv_rms)), doubled(as_columns(pull))


def gate_backward(
    own_ref, other_ref, bundle_ref, z_ref, go_ref, dy_ref, aloc_ref, totals_ref, y_ref, *refs, heads,
):
    adev_refs, (start_wide, adjoint) = refs[:PIECES], refs[PIECES:]
    rows, channels = z_ref.shape
    blocks = rows // STRETCH
    at_keep, at_gain, at_start, at_turned, end = bundle_rows(rows)
    totals_ref[...] = own_ref[...] + other_ref[...]
    for block in reversed(range(blocks)):
        here = slice(block * STRETCH, (block + 1) * STRETCH)
        start_wide[...] = spread_heads(bundle_ref[at_start : at_start + heads, here], HEAD_DIM)
        inv_rms, pull = norm_factors(totals_ref, here)
        firsts = [turn * rows + block * STRETCH for turn in range(4)]
        c_turned = jnp.concatenate(
            [bundle_ref[at_turned:end, first : first + STRETCH] for first in firsts], axis=0
        ).astype(bf16)

        def chunk(step, carry):
            part = lanes(step, CHUNK)
            z = z_ref[here, part].astype(f32)
            gate = z * sigmoid(z)
            gained = go_ref[here, part].astype(f32) * bundle_ref[at_gain : at_gain + 1, part]
            y_now = bundle_ref[here, part]
            y_ref[here, part] = y_now
            mixed = y_now.astype(bf16).astype(f32)
            d_gated = gained * inv_rms - mixed * gate * pull
            dy = (d_gated * gate).astype(bf16)
            dy_ref[here, part] = dy
            fresh = dot(c_turned, (dy.astype(f32) * start_wide[:, part]).astype(bf16))
            if block < blocks - 1:
                keep = bundle_ref[at_keep + block : at_keep + block + 1, part]
                fresh = fresh + keep * adjoint[:, part]
            if block > 0:
                adjoint[:, part] = fresh
                aloc_ref[block - 1, :, part] = fresh.astype(bf16)
            else:
                put_piece(adev_refs, part, fresh.astype(bf16))
            return carry

        repeat(channels // CHUNK, chunk, 0)


def within_backward(
    totals_ref, y_ref, z_ref, go_ref, gain_ref, dy_ref, xc_ref, xp_ref, bcc_ref, run_ref, flags_ref,
    sloc_ref, keep_ref, rows_ref, sx_ref, dtr_ref, *refs, group,
):
    prior_ref, refs = refs[: 2 * PIECES], refs[2 * PIECES :]
    gz_ref, dux_ref, dts_ref, ended_ref, dbc_ref, drun_ref, step_ref, chan_ref, *refs = refs
    run_wide, run_tall, start_wide, skip_wide, dt_wide, end_wide = refs
    rows, channels = xc_ref.shape
    heads = run_ref.shape[0]
    skip_wide[0:1, :] = over_channels(head_column(rows_ref, SKIP_WEIGHT, group, heads))
    chan_ref[...] = jnp.zeros_like(chan_ref)
    dt_all = step_sizes(dtr_ref, rows_ref, group)
    for block in range(rows // STRETCH):
        here = slice(block * STRETCH, (block + 1) * STRETCH)
        seen = resets_seen(flags_ref[:, here])
        mask = decay_mask(seen)
        dt_wide[...] = spread_heads(dt_all[:, here], HEAD_DIM)
        end_wide[...] = spread_heads(to_end_factor(run_ref[:, here], seen), HEAD_DIM)
        b_now = bcc_ref[here, 0:NSTATE]
        c_now = bcc_ref[here, NSTATE:]
        scores = dot(c_now, b_now, ((1,), (1,)))
        place_runs(run_ref, here, run_wide, run_tall)
        start_wide[...] = spread_heads(start_factor(run_ref, flags_ref, here), HEAD_DIM)
        inv_rms, pull = norm_factors(totals_ref, here)

        def chunk(step, carry):
            d_c, d_run = carry
            part = lanes(step, CHUNK)
            z = z_ref[here, part].astype(f32)
            gate_up = sigmoid(z)
            gate = z * gate_up
            go = go_ref[here, part].astype(f32)
            xc = xc_ref[here, part].astype(f32)
            y_now = y_ref[here, part]
            y_ssd = y_now - skip_wide[0:1, part] * xc
            mixed = y_now.astype(bf16).astype(f32)
            gated = mixed * gate
            d_gated = go * gain_ref[0:1, part] * inv_rms - gated * pull
            slope = gate_up + gate * (1.0 - gate_up)
            gz_ref[here, part] = (d_gated * mixed * slope).astype(bf16)
            dy = dy_ref[here, part].astype(f32)
            chan_ref[0:1, part] += jnp.sum(go * gated * inv_rms, axis=0, keepdims=True)
            chan_ref[1:2, part] += jnp.sum(dy * xc, axis=0, keepdims=True)
            d_run = d_run + head_sums(dy * y_ssd, step * CHUNK)
            started = (dy * start_wide[:, part]).astype(bf16)
            state = block_state(block, prior_ref, sloc_ref, keep_ref, part)
            return d_c + dot(started, state, ((1,), (1,))), d_run

        d_c, d_run = repeat(
            channels // CHUNK,
            chunk,
            (jnp.zeros((STRETCH, NSTATE), f32), jnp.zeros((STRETCH, STRETCH), f32)),
        )
        drun_ref[:, here] = jnp.transpose(d_run)[0:heads]

        def pair(step, carry):
            d_scores, per_step = carry
            part = lanes(step, PAIR)
            s_first, w_first = block_weights(scores, mask, run_wide, run_tall, 2 * step)
            s_second, w_second = block_weights(scores, mask, run_wide, run_tall, 2 * step + 1)
            dy = dy_ref[here, part]
            d_weights = dot(dy, both_heads(xp_ref[here, part]), ((1,), (1,)))
            d_stepped = dot(
                jnp.concatenate([w_first, w_second], axis=0), both_heads(dy), ((0,), (0,))
            )
            stepped = xp_ref[here, part].astype(f32)
            ended_ref[here, part] = (stepped * end_wide[:, part]).astype(bf16)
            slope = sx_ref[here, part]
            scaled = dt_wide[:, part] * slope
            dts_ref[here, part] = scaled
            dux_ref[here, part] = d_stepped * scaled + skip_wide[0:1, part] * dy.astype(f32) * slope
            return (
                d_scores + d_weights[:, 0:STRETCH] * s_first + d_weights[:, STRETCH:] * s_second,
                per_step + head_sums(stepped * d_stepped, step * PAIR),
            )

        d_scores, per_step = repeat(
            channels // PAIR,
            pair,
            (jnp.zeros((STRETCH, STRETCH), f32), jnp.zeros((STRETCH, STRETCH), f32)),
        )
        d_scores = d_scores.astype(bf16)
        step_ref[:, here] = jnp.transpose(per_step)[0:heads]
        dbc_ref[here, 0:NSTATE] = dot(d_scores, c_now, ((0,), (0,)))
        dbc_ref[here, NSTATE:] = d_c + dot(d_scores, b_now)


def put_total(d_ext, pack_ref, first, part, d_total):
    for tile in range(part.start // STRETCH, part.stop // STRETCH):
        at = tile * STRETCH - part.start
        d_ext[tile, PAD + first : PAD + first + STRETCH, :] = d_total[:, at : at + STRETCH]
    now = jnp.sum(d_total, axis=0, keepdims=True)
    pack_ref[CONV : CONV + 1, part] = pack_ref[CONV : CONV + 1, part] + now if first else now


def conv_backward(d_ext, live_up, weight_ref, x_ref, halo_ref, grad_ref, tail_ref, pack_ref, rows, tile):
    sums = None
    part = lanes(tile, STRETCH)
    for first, count in [(-PAD, PAD)] + [(at, STRETCH) for at in range(0, rows, STRETCH)]:
        begin = PAD + first
        pieces = [d_ext[tile, begin : begin + count, :]]
        for lag in range(1, CONV):
            moved = slice(begin + lag, begin + lag + count)
            pieces.append(d_ext[tile, moved, :] * live_up[lag - 1, begin : begin + count, :])
        grad = weight_ref[0:1, part] * pieces[0]
        for lag in range(1, CONV):
            grad = grad + weight_ref[lag : lag + 1, part] * pieces[lag]
        if first < 0:
            pack_ref[BACK : BACK + HALO, part] = grad[PAD - HALO :]
            seen = halo_ref[:, part]
            pieces = [piece[PAD - HALO :] for piece in pieces]
        else:
            grad_ref[first : first + count, part] = grad.astype(bf16)
            if first + count == rows:
                tail_ref[:, part] = grad[count - HALO :]
            seen = x_ref[first : first + count, part].astype(f32)
        now = [jnp.sum(seen * piece, axis=0, keepdims=True) for piece in pieces]
        sums = now if sums is None else [old + new for old, new in zip(sums, now)]
    for row, value in enumerate(sums):
        pack_ref[row : row + 1, part] = value


def finish_backward(
    aloc_ref, sloc_ref, keep_ref, dux_ref, dts_ref, ended_ref, dbc_ref, drun_ref, step_ref, xp_ref,
    bcc_ref, run_ref, flags_ref, sbc_ref, x_ref, xh_ref, bc_ref, bch_ref, wx_ref, wb_ref, rows_ref,
    dtr_ref, chan_ref, *refs, group,
):
    later_refs, prior_ref, refs = refs[: 2 * PIECES], refs[2 * PIECES : 4 * PIECES], refs[4 * PIECES :]
    gx_ref, xtail_ref, xpack_ref, gbc_ref, bctail_ref, bcpack_ref, gdt_ref, *refs = refs
    clear, live, live_up, dx_ext, dbc_ext, end_wide, ends = refs
    rows, channels = xp_ref.shape
    heads = run_ref.shape[0]
    blocks = rows // STRETCH
    fill_live(flags_ref, clear, live)
    live[:, PAD + rows :, :] = jnp.zeros((HALO, PAD, STRETCH), f32)
    live[:, 0:PAD, :] = jnp.zeros((HALO, PAD, STRETCH), f32)
    for lag in range(1, CONV):
        live_up[lag - 1] = live[lag - 1, lag : lag + rows + PAD, :]
    for ext in (dx_ext, dbc_ext):
        ext[:, 0:PAD, :] = jnp.zeros((ext.shape[0], PAD, STRETCH), f32)
        ext[:, PAD + rows :, :] = jnp.zeros((ext.shape[0], PAD, STRETCH), f32)
    rate = jnp.exp(head_column(rows_ref, A_LOG, group, heads))
    dt_bias = head_column(rows_ref, DT_BIAS, group, heads)
    dt_all = step_sizes(dtr_ref, rows_ref, group)
    d_alog = jnp.zeros((heads, 1), f32)
    d_dtb = jnp.zeros((heads, 1), f32)
    for block in range(blocks):
        here = slice(block * STRETCH, (block + 1) * STRETCH)
        running = run_ref[:, here]
        dt = dt_all[:, here]
        end_wide[...] = spread_heads(
            to_end_factor(running, resets_seen(flags_ref[:, here])), HEAD_DIM
        )
        b_now = bcc_ref[here, 0:NSTATE]

        def chunk(step, carry):
            d_b, per_step = carry
            part = lanes(step, CHUNK)
            later = piece_of(later_refs[:PIECES], part) + piece_of(later_refs[PIECES:], part)
            if block < blocks - 1:
                whole = keep_ref[block + 1 : block + 2, part]
                for place in range(block + 2, blocks):
                    whole = whole * keep_ref[place : place + 1, part]
                later = (aloc_ref[block, :, part].astype(f32) + whole * later.astype(f32)).astype(bf16)
            state = block_state(block, prior_ref, sloc_ref, keep_ref, part)
            d_keep = jnp.sum(later.astype(f32) * state.astype(f32), axis=0, keepdims=True)
            d_end = dot(b_now, later) * end_wide[:, part]
            product = xp_ref[here, part].astype(f32) * d_end
            at_ends = jnp.sum(product, axis=0, keepdims=True)
            at_ends = at_ends + d_keep * keep_ref[block : block + 1, part]
            ends[:, part] = jnp.broadcast_to(at_ends, (PAD, CHUNK))
            d_total = dux_ref[here, part] + d_end * dts_ref[here, part]
            put_total(dx_ext, xpack_ref, block * STRETCH, part, d_total)
            return (
                d_b + dot(ended_ref[here, part], later, ((1,), (1,))),
                per_step + head_sums(product, step * CHUNK),
            )

        zero = jnp.zeros((STRETCH, NSTATE), f32)
        d_b, per_step = repeat(channels // CHUNK, chunk, (zero, jnp.zeros((STRETCH, STRETCH), f32)))
        per_step = step_ref[:, here] + jnp.transpose(per_step)[0:heads]
        for place, d_part in enumerate((dbc_ref[here, 0:NSTATE] + d_b, dbc_ref[here, NSTATE:])):
            part = lanes(place, NSTATE)
            put_total(dbc_ext, bcpack_ref, block * STRETCH, part, d_part * sbc_ref[here, part])
        at_end = to_column(head_sums(ends[...], 0)[0:1], 0, heads)
        is_last = iota((heads, STRETCH), 1) == STRETCH - 1
        d_run = drun_ref[:, here] - per_step + jnp.where(is_last, at_end, 0.0)
        shape = (STRETCH, STRETCH)
        d_log = dot_full(d_run, (iota(shape, 0) >= iota(shape, 1)).astype(f32))
        d_dt = per_step / dt - rate * d_log
        raw = dtr_ref[:, here].astype(f32) + dt_bias
        d_raw = d_dt / (1.0 + jnp.exp(-raw))
        gdt_ref[:, here] = d_raw
        d_alog = d_alog - jnp.sum(d_log * dt, axis=1, keepdims=True) * rate
        d_dtb = d_dtb + jnp.sum(d_raw, axis=1, keepdims=True)
    xpack_ref[GAIN : SKIP + 1, :] = chan_ref[0:2, :]
    bcpack_ref[GAIN : SKIP + 1, :] = jnp.zeros((2, bcpack_ref.shape[1]), f32)
    for place, column in enumerate((d_alog, d_dtb)):
        shape = (heads, STRETCH)
        pick = iota(shape, 1) == iota(shape, 0) + group * heads
        row = jnp.sum(jnp.where(pick, jnp.broadcast_to(column, shape), 0.0), axis=0, keepdims=True)
        bcpack_ref[GAIN : GAIN + 1, place * STRETCH : (place + 1) * STRETCH] = row
    for step in range(channels // STRETCH):
        conv_backward(
            dx_ext, live_up, wx_ref, x_ref, xh_ref, gx_ref, xtail_ref, xpack_ref, rows, step
        )
    for step in range(2):
        conv_backward(
            dbc_ext, live_up, wb_ref, bc_ref, bch_ref, gbc_ref, bctail_ref, bcpack_ref, rows, step
        )


def pack(*refs):
    *pieces, out_ref = refs
    at = 0
    for ref in pieces:
        size = ref.shape[1]
        out_ref[0 : BACK + 1, at : at + size] = ref[0 : BACK + 1, :]
        at += size
    whole = jnp.concatenate([ref[BACK + 1 : PACKED, :] for ref in pieces], axis=1)
    short = out_ref.shape[1] - at
    for row in range(PAD):
        first = row % (PAD // 2) * short
        out_ref[row : row + 1, at:] = whole[row // (PAD // 2) :][0:1, first : first + short]


def unpack_back(value, length):
    short = value.shape[1] - length
    rows = [value[BACK : BACK + 1, 0:length]]
    for half in range(2):
        pieces = [value[half * (PAD // 2) + turn :][0:1, length:] for turn in range(PAD // 2)]
        rows.append(jnp.concatenate(pieces, axis=1))
    return jnp.concatenate(rows, axis=0)


def final_sums(mine_ref, pick_ref, flags_ref, *refs, arrivals, groups, scale):
    arrived, refs = refs[:arrivals], refs[arrivals:]
    tails_x, tails_bc, refs = refs[:groups], refs[groups : 2 * groups], refs[2 * groups :]
    out_wx, out_bx, out_wb, out_bb, out_alog, out_dtb, out_skip, out_gain, ending_ref = refs
    inner = out_wx.shape[1]
    length = ending_ref.shape[1]
    total = mine_ref[0:BACK, 0:length]
    back = jnp.zeros((HALO, length), f32)
    for place, ref in enumerate(arrived):
        value = ref[...].astype(f32)
        total = total + value[0:BACK, 0:length]
        back = back + unpack_back(value, length) * pick_ref[place : place + 1, 0:1]
    total = total * scale
    back = back * tail_factors(flags_ref)
    at = 0
    for ref in tails_x + tails_bc:
        size = ref.shape[1]
        ending_ref[:, at : at + size] = (ref[...] + back[:, at : at + size]).astype(bf16)
        at += size
    out_wx[...] = total[0:CONV, 0:inner]
    out_bx[...] = total[CONV : CONV + 1, 0:inner]
    for which in range(2):
        for group in range(groups):
            first = inner + (2 * group + which) * NSTATE
            to = slice(group * NSTATE, (group + 1) * NSTATE)
            out_wb[:, which, to] = total[0:CONV, first : first + NSTATE]
            out_bb[which : which + 1, to] = total[CONV : CONV + 1, first : first + NSTATE]
    out_gain[...] = total[GAIN : GAIN + 1, 0:inner]
    heads = out_skip.shape[1]
    for out, shift in ((out_alog, 0), (out_dtb, STRETCH)):
        row = None
        for group in range(groups):
            first = inner + 2 * group * NSTATE + shift
            piece = total[GAIN : GAIN + 1, first : first + STRETCH]
            row = piece if row is None else row + piece
        out[...] = row[:, 0:heads]
    lane_sums = jnp.broadcast_to(total[SKIP : SKIP + 1, 0:inner], (PAD, inner))
    shape = (heads, inner)
    pick = (iota(shape, 1) // HEAD_DIM == iota(shape, 0)).astype(f32).astype(bf16)
    high = lane_sums.astype(bf16)
    low = (lane_sums - high.astype(f32)).astype(bf16)
    last = ((1,), (1,))
    out_skip[...] = (dot(high, pick, last) + dot(low, pick, last))[0:1]


def call(kernel, operands, outs, scratch, flops, name, blocked=None, hbm_outs=()):
    operands = [(each + (None,))[:3] for each in operands]
    cuts = [cut or {} for _, cut, _ in operands]
    arrays = [array for array, _, _ in operands]
    stages = [stage for _, _, stage in operands]
    shapes = [jax.ShapeDtypeStruct(shape, dtype) for shape, dtype in outs]
    streamed = [place for place, stage in enumerate(stages) if stage is not None]
    buffers = []
    for place in streamed:
        cut = cuts[place]
        shape = tuple(
            cut[dim].stop - cut[dim].start if dim in cut else extent
            for dim, extent in enumerate(arrays[place].shape)
        )
        buffers.append(pltpu.VMEM(shape, arrays[place].dtype))
    copies_made = sum(len(stages[place]) for place in streamed)

    def body(*refs):
        count, made = len(cuts), len(buffers)
        rest = refs[count:]
        held = dict(zip(streamed, rest[len(rest) - made - 1 : len(rest) - 1])) if made else {}
        sems = rest[-1] if made else None
        seen, copies = [], []
        for place, (ref, cut) in enumerate(zip(refs, cuts)):
            if cut:
                ref = ref.at[tuple(cut.get(dim, slice(None)) for dim in range(len(ref.shape)))]
            if place in held:
                buffer = held[place]
                size = buffer.shape[-1] // len(stages[place])
                for turn, stage in enumerate(stages[place]):
                    part = (slice(None),) * (len(buffer.shape) - 1) + (
                        slice(turn * size, (turn + 1) * size),
                    )
                    copy = (stage, (ref.at[part], buffer.at[part], sems.at[len(copies)]))
                    copies.append(copy)
                ref = buffer
            seen.append(ref)
        for _, copy in sorted(copies, key=lambda each: each[0]):
            pltpu.make_async_copy(*copy).start()

        def ready(stage):
            for which, copy in copies:
                if which == stage:
                    pltpu.make_async_copy(*copy).wait()

        if made:
            kernel(*seen, *rest[: len(rest) - made - 1], ready=ready)
        else:
            kernel(*seen, *rest)

    def block_of(array, cut):
        shape, index = [], []
        for dim, extent in enumerate(array.shape):
            part = cut.get(dim, slice(0, extent))
            size = part.stop - part.start
            shape.append(size)
            index.append(part.start // size)
        return pl.BlockSpec(tuple(shape), functools.partial(lambda fixed, i: fixed, tuple(index)))

    in_vmem = pl.BlockSpec(memory_space=pltpu.VMEM)
    in_hbm = pl.BlockSpec(memory_space=pltpu.HBM)
    scratch_shapes = [
        pltpu.VMEM(each, f32) if isinstance(each, tuple) else each for each in scratch
    ]
    if blocked:
        grid, limit = {"grid": (1,)}, blocked
        in_specs = [block_of(array, cut) for array, cut in zip(arrays, cuts)]
        out_specs = [block_of(shape, {}) for shape in shapes]
    else:
        grid, limit = {}, STREAM_LIMIT if buffers else VMEM_LIMIT
        in_specs = [in_vmem if stage is None else in_hbm for stage in stages]
        out_specs = [in_hbm if place in hbm_outs else in_vmem for place in range(len(shapes))]
        if buffers:
            scratch_shapes += buffers + [pltpu.SemaphoreType.DMA((copies_made,))]
    count = sum(each.size * each.dtype.itemsize for each in arrays + shapes)
    return pl.pallas_call(
        kernel if blocked else body,
        in_specs=in_specs,
        out_specs=out_specs,
        out_shape=shapes,
        scratch_shapes=scratch_shapes,
        compiler_params=pltpu.CompilerParams(vmem_limit_bytes=limit),
        cost_estimate=pl.CostEstimate(flops=flops, bytes_accessed=count, transcendentals=0),
        name=name,
        **grid,
    )(*arrays)


def together(*values):
    return lax.optimization_barrier(values)


def chain(parts, decays, axis, backward, fillers):
    count = lax.axis_size(axis)
    zero = [jnp.zeros(part.shape, bf16) for part in parts]
    early, last = list(zero), list(zero)
    results = []
    for hop in range(count - 1):
        pairs = [(count - 1 - hop, count - 2 - hop)] if backward else [(hop, hop + 1)]
        leaving = list(parts)
        if hop > 0:
            for place, part in enumerate(parts):
                if place:
                    last[place] = together(last[place], leaving[place - 1])[0]
                early[place] = early[place] + last[place] if hop > 1 else last[place]
                arrived = early[place].astype(f32)
                leaving[place] = (decays[place] * arrived + part.astype(f32)).astype(bf16)
        filler = fillers[hop - 1] if 0 < hop <= len(fillers) else None
        if filler:
            work, array = filler
            array = together(array, *leaving)[0]
        last = [lax.ppermute(each, axis, pairs) for each in leaving]
        if filler:
            done = work(array)
            last[0], *done = together(last[0], *done)
            results.append(done)
    for work, array in fillers[len(results) :]:
        results.append(work(array))
    return list(zip(early, last)), results


def exchange_terms(value, axis):
    count = lax.axis_size(axis)
    other = jnp.zeros_like(value)
    stride = 1
    while stride < count:
        value = value + other if stride > 1 else value
        other = lax.ppermute(value, axis, [(i, i ^ stride) for i in range(count)])
        stride *= 2
    return value, other


def per_device(
    x_raw, bc_raw, z_gate, dt_raw, resets, conv_x_weight, conv_x_bias, conv_bc_weight,
    conv_bc_bias, a_log, dt_bias, skip_weight, norm_gain, grad_out,
):
    rows, inner = x_raw.shape[1:]
    groups = bc_raw.shape[3] // NSTATE
    heads = a_log.shape[0] // groups
    channels = inner // groups
    blocks = rows // STRETCH
    width = 2 * NSTATE

    def by_group(value):
        lead = value.shape[:-2]
        split = value.reshape(lead + (2, groups, NSTATE))
        return jnp.moveaxis(split, -3, -2).reshape(lead + (groups * width,))

    x_own, z_own, go_own, dt_own = x_raw[0], z_gate[0], grad_out[0], dt_raw[0]
    bc_own = by_group(bc_raw[0])
    flags = resets
    count = lax.axis_size("ctx")
    sent = call(
        tails,
        [
            (x_raw, {1: slice(rows - 16, rows)}, [0]),
            (bc_raw, {1: slice(rows - 16, rows)}, [0]),
            (flags, {1: slice(rows - STRETCH, rows)}, [0]),
        ],
        [((HALO, inner + groups * width), f32)],
        [],
        rows,
        "tails",
    )[0]
    halo = lax.ppermute(sent, "ctx", [(i, i + 1) for i in range(count - 1)])
    head_rows = jnp.stack([a_log, dt_bias, skip_weight])
    head_rows = jnp.pad(head_rows, ((0, PAD - 3), (0, -head_rows.shape[1] % STRETCH)))
    bx, gain = conv_x_bias[None], norm_gain[None]
    wb, bb = by_group(conv_bc_weight), by_group(conv_bc_bias)[None]

    def wide(array, group):
        return (array, {1: slice(group * channels, (group + 1) * channels)})

    def narrow(array, group, first=0):
        return (array, {1: slice(first + group * width, first + (group + 1) * width)})

    def per_head(array, group):
        return (array, {0: slice(group * heads, (group + 1) * heads)})

    def whole(array):
        return (array, None)

    keep_rows = -(-blocks // PAD) * PAD
    tall, thin, row_shape = (rows, channels), (rows, width), (heads, rows)
    state_shape = (NSTATE, channels)
    piece_shape = (NSTATE, channels // PIECES)
    local_shape = (blocks - 1, NSTATE, channels)
    clear_shape, live_shape = (rows + PAD, STRETCH), (HALO, rows + 2 * PAD, STRETCH)
    wide_scratch = (STRETCH, channels)
    run_scratch = [(STRETCH, heads * STRETCH), (heads * PAD, STRETCH)]
    work = rows * channels * STRETCH
    group_range = range(groups)
    here = lax.axis_index("ctx")
    picks = [(here ^ shift) == here + 1 for shift in range(1, count)]
    pick = jnp.broadcast_to(jnp.stack(picks).astype(f32)[:, None], (count - 1, STRETCH))
    flags, pick = together(flags, pick)
    held = []
    flags_now = flags
    for g in group_range:
        if held:
            flags_now = together(flags, held[-1][-1])[0]
        held.append(
            call(
                functools.partial(conv_and_state, group=g),
                [
                    wide(x_own, g), wide(halo, g), narrow(bc_own, g), narrow(halo, g, inner),
                    wide(conv_x_weight, g), wide(bx, g), narrow(wb, g), narrow(bb, g),
                    per_head(dt_own, g), whole(head_rows), whole(flags_now),
                ],
                [
                    (tall, bf16), (tall, bf16), (tall, f32), (thin, bf16), (thin, f32),
                    (row_shape, f32), ((keep_rows, channels), f32), (local_shape, bf16),
                ]
                + [(piece_shape, bf16)] * PIECES
                + [((1, channels // PIECES), f32)] * PIECES,
                [
                    (channels // STRETCH, rows + PAD, STRETCH), (width // STRETCH, rows + PAD, STRETCH),
                    clear_shape, live_shape,
                    wide_scratch, wide_scratch, state_shape,
                ],
                2 * work,
                "conv_and_state",
            )
        )
    xc, xp, ux, bcc, ubc, run, keep, s_loc, *pieces = zip(*held)
    s_dev, decay = pieces[:PIECES], pieces[PIECES:]

    def in_a_row(pieces):
        return [piece[g] for g in group_range for piece in pieces]

    def by_pieces(pairs):
        return [
            [pair[term] for term in range(2) for pair in pairs[g * PIECES : (g + 1) * PIECES]]
            for g in group_range
        ]


    def forward_work(g):
        return lambda bcc_now: call(
            within_blocks,
            [
                whole(xp[g]), whole(bcc_now), whole(run[g]), whole(flags), whole(ux[g]), whole(ubc[g]),
            ],
            [(tall, f32), (tall, f32), (thin, f32)],
            run_scratch,
            6 * work,
            "within_blocks",
        )

    prior, held = chain(
        in_a_row(s_dev), in_a_row(decay), "ctx", False, [(forward_work(g), bcc[g]) for g in group_range]
    )
    prior = by_pieces(prior)
    y_within, slope_x, slope_bc = zip(*held)
    held, sums = [], ()
    for g in group_range:
        bundle, total = call(
            functools.partial(gate_forward, group=g),
            [
                whole(y_within[g]), whole(s_loc[g]), whole(keep[g]), whole(bcc[g]), whole(run[g]),
                whole(flags), whole(xc[g]), whole(head_rows), wide(z_own, g), wide(go_own, g),
                wide(gain, g),
            ]
            + [whole(each) for each in prior[g]]
            + [whole(each) for each in sums],
            [((bundle_rows(rows)[-1], channels), f32), ((2, rows), f32)],
            [wide_scratch, (PAD, channels)],
            2 * work,
            "gate_forward",
        )
        sums = (total,)
        held.append(bundle)
    bundle = held
    own, other = exchange_terms(sums[0], "head")
    held = []
    for g in group_range:
        bundle_now = together(bundle[g], held[-1][-1])[0] if held else bundle[g]
        held.append(
            call(
                functools.partial(gate_backward, heads=heads),
                [whole(own), whole(other), whole(bundle_now), wide(z_own, g), wide(go_own, g)],
                [(tall, bf16), (local_shape, bf16), ((2, rows), f32), (tall, f32)]
                + [(piece_shape, bf16)] * PIECES,
                [wide_scratch, state_shape],
                2 * work,
                "gate_backward",
            )
        )
    dy, a_loc, totals, y_all, *a_dev = zip(*held)

    def backward_work(g):
        return lambda bcc_now: call(
            functools.partial(within_backward, group=g),
            [
                whole(totals[g]), whole(y_all[g]), wide(z_own, g), wide(go_own, g), wide(gain, g),
                whole(dy[g]), whole(xc[g]), whole(xp[g]), whole(bcc_now),
                whole(run[g]), whole(flags), whole(s_loc[g]), whole(keep[g]), whole(head_rows),
                whole(slope_x[g]), per_head(dt_own, g),
            ]
            + [whole(each) for each in prior[g]],
            [
                (tall, bf16), (tall, f32), (tall, f32), (tall, bf16), (thin, f32), (row_shape, f32),
                (row_shape, f32), ((PAD, channels), f32),
            ],
            run_scratch + [wide_scratch, (PAD, channels), wide_scratch, wide_scratch],
            10 * work,
            "within_backward",
            BLOCKED_LIMIT,
        )

    later, held = chain(
        in_a_row(a_dev), in_a_row(decay), "ctx", True, [(backward_work(g), bcc[g]) for g in group_range]
    )
    later = by_pieces(later)
    gz, dux, dts, ended, dbc, drun, per_step, chan = zip(*held)
    held = []
    for g in group_range:
        rows_now = together(head_rows, held[-1][-1])[0] if held else head_rows
        held.append(call(
            functools.partial(finish_backward, group=g),
            [
                whole(a_loc[g]), whole(s_loc[g]), whole(keep[g]), whole(dux[g]), whole(dts[g]),
                whole(ended[g]), whole(dbc[g]), whole(drun[g]), whole(per_step[g]), whole(xp[g]),
                whole(bcc[g]), whole(run[g]), whole(flags), whole(slope_bc[g]), wide(x_own, g),
                wide(halo, g), narrow(bc_own, g), narrow(halo, g, inner), wide(conv_x_weight, g),
                narrow(wb, g), whole(rows_now), per_head(dt_own, g), whole(chan[g]),
            ]
            + [whole(each) for each in later[g] + prior[g]],
            [
                (tall, bf16), ((HALO, channels), f32), ((PACKED, channels), f32), (thin, bf16),
                ((HALO, width), f32), ((PACKED, width), f32), (row_shape, f32),
            ],
            [
                clear_shape, live_shape, (HALO, rows + PAD, STRETCH),
                (channels // STRETCH, rows + 2 * PAD, STRETCH),
                (width // STRETCH, rows + 2 * PAD, STRETCH), wide_scratch, (PAD, channels),
            ],
            4 * work,
            "finish_backward",
        ))
    gx, x_tail, x_pack, gbc, bc_tail, bc_pack, gdt = zip(*held)

    def joined(pieces):
        return jnp.concatenate(pieces, axis=1)

    def ungroup(value):
        lead = value.shape[:-1]
        split = value.reshape(lead + (groups, 2, NSTATE))
        return jnp.moveaxis(split, -3, -2).reshape(lead + (2, groups * NSTATE))

    length = inner + groups * width
    packed = call(
        pack,
        [whole(each) for each in x_pack + bc_pack],
        [((PAD, length + 2 * length // PAD), f32)],
        [],
        rows,
        "pack",
    )[0]
    mine = packed
    own_rows = np.ones((PAD, packed.shape[1]), np.float32)
    own_rows[BACK:] = 0.0
    own_rows[:, length:] = 0.0
    for shift in range(1, lax.axis_size("dp")):
        size = lax.axis_size("dp")
        other = lax.ppermute(packed, "dp", [(i, (i + shift) % size) for i in range(size)])
        mine = mine + other * own_rows
    leaving = mine.astype(bf16)
    arrived = [
        lax.ppermute(leaving, "ctx", [(i, i ^ shift) for i in range(count)])
        for shift in range(1, count)
    ]
    out_wx, out_bx, out_wb, out_bb, out_alog, out_dtb, out_skip, out_gain, ending = call(
        functools.partial(
            final_sums,
            arrivals=count - 1,
            groups=groups,
            scale=float(lax.axis_size("dp") * count * rows) ** (-0.5),
        ),
        [whole(mine), whole(pick), whole(flags)]
        + [whole(each) for each in arrived]
        + [whole(each) for each in x_tail + bc_tail],
        [
            ((CONV, inner), f32), ((1, inner), f32), ((CONV, 2, groups * NSTATE), f32),
            ((2, groups * NSTATE), f32),
            ((1, groups * heads), f32), ((1, groups * heads), f32), ((1, groups * heads), f32),
            ((1, inner), f32), ((HALO, inner + groups * width), bf16),
        ],
        [],
        rows * inner,
        "final_sums",
    )
    grad_x = lax.dynamic_update_slice(joined(gx), ending[:, :inner], (rows - HALO, 0))
    grad_bc = lax.dynamic_update_slice(
        ungroup(joined(gbc)), ungroup(ending[:, inner:]), (rows - HALO, 0, 0)
    )
    return (
        grad_x[None],
        grad_bc[None],
        joined(gz)[None],
        jnp.concatenate(gdt, axis=0)[None],
        out_wx,
        out_bx[0],
        out_wb,
        out_bb,
        out_alog[0],
        out_dtb[0],
        out_skip[0],
        out_gain[0],
    )


def solution(mesh):
    return jax.shard_map(
        per_device,
        mesh=mesh,
        in_specs=(
            P("dp", "ctx", "head"),
            P("dp", "ctx", None, "head"),
            P("dp", "ctx", "head"),
            P("dp", "head", "ctx"),
            P("dp", "ctx"),
            P(None, "head"),
            P("head"),
            P(None, None, "head"),
            P(None, "head"),
            P("head"),
            P("head"),
            P("head"),
            P("head"),
            P("dp", "ctx", "head"),
        ),
        out_specs=(
            P("dp", "ctx", "head"),
            P("dp", "ctx", None, "head"),
            P("dp", "ctx", "head"),
            P("dp", "head", "ctx"),
            P(None, "head"),
            P("head"),
            P(None, None, "head"),
            P(None, "head"),
            P("head"),
            P("head"),
            P("head"),
            P("head"),
        ),
        check_vma=False,
    )
```
